32 devices in a mesh: table: 16 (over z, y, core), rep: 2 (over x).
Axes of the slice: x: 2, y: 2, z: 4, core: 2. Of those that a mesh axis runs over, the one named last changes fastest.
Arguments:
- bag_rows: int32 [32, 1024, 8], P(('table', 'rep')), may hold values from 0 to 2047
- bag_owner: int32 [32, 1024, 8], P(('table', 'rep')), may hold values from 0 to 15, all different within a row; in each aligned block of 1024 rows (0 to 1023, 1024 to 2047, ..., all dimensions but the last counted through in order) at most 768 rows name the same one
- bag_weight: float32 [32, 1024, 8], P(('table', 'rep')), may hold values from 0.25 to 2
- tables: bfloat16 [4, 32768, 128], P(None, 'table'), may hold values from -3 to 3
- returning: int32 [32], P(('table', 'rep')), may hold values 0 or 1
- home: int32 [32], P(('table', 'rep')), may hold values from 0 to 1
- entry: int32 [32], P(('table', 'rep')), may hold values from 0 to 7
- stores: bfloat16 [256, 30, 512], P(('table', 'rep')), may hold values from -6 to 6
- conv_weight: bfloat16 [4, 1536, 512], P(None, 'table'), may hold values from -0.15625 to 0.15625
- norm_gain: float32 [4, 512], replicated, may hold values from 0.1 to 1.9
Outputs:
- hidden: bfloat16 [32, 1024, 512], P(('table', 'rep'))
The draws below stay inside these ranges and needn't reach their ends.
Inputs may be any that keep to these rules, and one draw needn't show every extreme that they name: `bag_owner`: the 8 ids of one slot name different owners. Among the slots of one device no owner is named by more than 768 ids, and in some devices' slots one owner is named by exactly 768.
All inputs are finite; a program needn't handle non-finite values. No bound on the sum of `returning` on one device may be relied on, other than what follows from the above.
Results may differ from the reference program's by a relative error of at most 0.0057.
Values may be sent and summed in bfloat16 or wider, within the bound.
No kernel may reach another device: no remote copies, remote signals or barrier semaphores. Data moves between devices by JAX's collectives and lax.ppermute only.
A program may use at most 64 MiB of HBM per device.

```python
import math
import jax
import jax.numpy as jnp
import numpy as np
from jax import lax

E = 128
NTAB = 4
C = 512
BAGTOT = 8
SLOTS = 1024
SAMP_DEV = 1
LAYERS = 4
ROWS_DEV = 2048
STORE_DEV = 8
STATE_LEN = 30
TOK_DEV = 1024
SAMPLES = 32
ROWS = 32768
STORED = 256
CAP = 768
N_TABLE = 16
N_REP = 2


def set_ends(entries, stream_key, smallest, top_value):
    longest = entries.shape.index(max(entries.shape))
    spots = []
    for shift in (0, 1):
        where = [jax.random.randint(jax.random.fold_in(stream_key, axis), (), 0, length) for axis, length in enumerate(entries.shape)]
        where[longest] = (where[longest] + shift) % entries.shape[longest]
        spots.append(tuple(where))
    return entries.at[spots[0]].set(smallest).at[spots[1]].set(top_value)


def level_of(key, extent, shards, smallest, high):
    def one(position, shards_of):
        steps = jax.random.uniform(jax.random.fold_in(jax.random.fold_in(key, 6), position), (shards_of,), jnp.float32, smallest / len(shards), high / len(shards))
        return jnp.repeat(jnp.exp(steps), extent[position] // shards_of).reshape((-1,) + (1,) * (len(extent) - position - 1))

    level = one(*shards[0])
    for cut in shards[1:]:
        level = level * one(*cut)
    return level


def deal_out(key, own, number, rows, count, top, reach, skew):
    ranking = jax.random.permutation(key, count)
    crowded, common = shares(count, rows * top, reach, skew, True), shares(count, rows * top, reach, skew, False)
    places = jnp.arange(count)

    def named(tallies, rotation):
        used = int((tallies > 0).sum())
        fixed = max(1, used // 4)
        moved = fixed + (places - fixed + rotation * (used - fixed)) % max(1, count - fixed)
        return jnp.zeros((count,), jnp.int32).at[ranking[jnp.where(places < fixed, places, moved)]].set(jnp.asarray(tallies, jnp.int32))

    tallies = jnp.where(number % 4 == 0, named(crowded, number // 4), named(common, number - number // 4 - 1))
    mixed = jax.random.permutation(jax.random.fold_in(own, 3), count)
    giver, taker = mixed[0:count // 2 * 2:2], mixed[1:count // 2 * 2:2]
    room = jnp.minimum(tallies[giver] - 1, reach - tallies[taker]) // 2
    room = jnp.where((giver == ranking[0]) | (taker == ranking[0]) | (tallies[taker] == 0), 0, jnp.maximum(room, 0))
    moved = jax.random.randint(jax.random.fold_in(own, 4), (count // 2,), 0, 1 << 20) % (room + 1)
    tallies = tallies.at[giver].add(-moved).at[taker].add(moved)
    items = jnp.searchsorted(jnp.cumsum(tallies), jnp.arange(rows * top), side="right").astype(jnp.int32)
    table = items.reshape(top, rows).T
    table = table[jax.random.permutation(jax.random.fold_in(own, 1), rows)]
    rotation = jax.random.randint(jax.random.fold_in(own, 2), (rows, 1), 0, top)
    return jnp.take_along_axis(table, (jnp.arange(top)[None, :] + rotation) % top, axis=1)


def shares(amount, total, most, lean, full):
    loads = [(1 << 20) // math.isqrt(rank ** lean) + 1 for rank in range(1, amount + 1)]
    largest = most if full else min(most, max(-(-total // amount), total * loads[0] // sum(loads)))
    least = 1 if total - largest >= amount - 1 else 0
    given, spare = [largest] + [least] * (amount - 1), total - largest - least * (amount - 1)
    while spare > 0:
        movable = [i for i in range(1, amount) if given[i] < largest] or [i for i in range(1, amount) if given[i] < most]
        mass, left = sum([loads[i] for i in movable]), spare
        for i in movable:
            more = min(most - given[i], max(1, left * loads[i] // mass), spare)
            given[i] = given[i] + more
            spare = spare - more
    return np.array(given)


def normal_values(own_key, dims, scale, limit, shards=(), kind=jnp.bfloat16):
    drawn = scale * jax.random.normal(own_key, dims, jnp.float32)
    if shards:
        drawn = drawn * level_of(own_key, dims, shards, -0.22, 0.18)
    return jnp.clip(drawn, -limit, limit).astype(kind)


def setup_inputs(seed: int = 0) -> dict:
    key_of = jax.random.split(jax.random.key(seed), 11)
    bag_rows = set_ends(jax.random.randint(key_of[0], (SAMPLES, SLOTS, BAGTOT), 0, ROWS_DEV), jax.random.fold_in(key_of[0], 1), 0, ROWS_DEV - 1).astype(jnp.int32)
    bag_owner_keys = jax.random.split(jax.random.fold_in(key_of[1], 1), SAMPLES * SLOTS // TOK_DEV)
    bag_owner_turns = jax.random.permutation(jax.random.fold_in(key_of[1], 3), SAMPLES * SLOTS // TOK_DEV)
    bag_owner = jax.vmap(lambda own, number: deal_out(jax.random.fold_in(key_of[1], 2), own, number, TOK_DEV, N_TABLE, BAGTOT, CAP, 2))(bag_owner_keys, bag_owner_turns).reshape((SAMPLES, SLOTS, BAGTOT))
    bag_weight = jnp.clip(jnp.exp(math.log(2.0) - 2.0794415 * jax.random.uniform(key_of[2], (SAMPLES, SLOTS, BAGTOT), jnp.float32) ** level_of(key_of[2], (SAMPLES, SLOTS, BAGTOT), ((0, 32),), -0.2, 0.2)), 0.25, 2.0)
    tables = normal_values(key_of[3], (NTAB, ROWS, E), 0.5, 3.0, ((1, 16),))
    returning = set_ends((jax.random.randint(key_of[4], (SAMPLES,), 0, 4) < 3).astype(jnp.int32), jax.random.fold_in(key_of[4], 1), 0, 1)
    home = set_ends(jax.random.randint(key_of[5], (SAMPLES,), 0, N_REP), jax.random.fold_in(key_of[5], 1), 0, N_REP - 1).astype(jnp.int32)
    entry = set_ends(jax.random.randint(key_of[6], (SAMPLES,), 0, STORE_DEV), jax.random.fold_in(key_of[6], 1), 0, STORE_DEV - 1).astype(jnp.int32)
    stores = normal_values(key_of[7], (STORED, STATE_LEN, C), 1.0, 6.0, ((0, 32),))
    conv_weight = normal_values(key_of[8], (LAYERS, 3 * C, C), (3 * C) ** -0.5, 0.15625, ((1, 16),))
    norm_gain = jnp.clip(1.0 + 0.18 * jax.random.normal(key_of[9], (LAYERS, C), jnp.float32), 0.1, 1.9)
    return dict(bag_rows=bag_rows, bag_owner=bag_owner, bag_weight=bag_weight, tables=tables, returning=returning, home=home, entry=entry, stores=stores, conv_weight=conv_weight, norm_gain=norm_gain)


table_of_id = (0, 1, 2, 2, 3, 3, 3, 3)
bag_bounds = ((0, 1), (1, 2), (2, 4), (4, 8))
epsilon = 1e-05

def pool_bags(weighted):
    sums = [lax.optimization_barrier(jnp.sum(weighted[..., lower:upper, :], axis=-2)) for lower, upper in bag_bounds]
    return jnp.concatenate(sums, axis=-1)

def norm_relu(values, gain):
    mean = lax.optimization_barrier(jnp.mean(values, axis=-1, keepdims=True))
    centred = values - mean
    spread = lax.optimization_barrier(jnp.mean(centred * centred, axis=-1, keepdims=True))
    return jnp.maximum(centred * lax.rsqrt(spread + epsilon) * gain, 0.0)

def stack_taps(inputs, carried, offset, dilation):
    span = 2 * dilation
    extended = jnp.concatenate([carried[..., offset:offset + span, :], inputs], axis=-2)
    length = inputs.shape[-2]
    taps = [extended[..., span - tap * dilation:span - tap * dilation + length, :] for tap in range(3)]
    return jnp.concatenate(taps, axis=-1)

def reference(bag_rows, bag_owner, bag_weight, tables, returning, home, entry, stores, conv_weight, norm_gain):
    flat_table = tables.reshape(NTAB * ROWS, E)
    table_ids = jnp.array(table_of_id, jnp.int32)
    device_of = jnp.arange(SAMPLES, dtype=jnp.int32) // SAMP_DEV
    store_row = device_of // N_REP * (N_REP * STORE_DEV) + home * STORE_DEV + entry
    carried_all = stores[store_row]
    carried_all = jnp.where(returning[:, None, None] > 0, carried_all, jnp.zeros_like(carried_all))

    def one_sample(item):
        rows, owner, weight, carried = item
        index = table_ids[None, :] * ROWS + owner * ROWS_DEV + rows
        picked = flat_table[index].astype(jnp.float32) * weight[..., None]
        block_in = pool_bags(picked).astype(jnp.bfloat16)
        inputs = block_in
        offset = 0
        for layer in range(LAYERS):
            dilation = 2 ** layer
            stacked = stack_taps(inputs, carried, offset, dilation)
            output = jnp.dot(stacked, conv_weight[layer], preferred_element_type=jnp.float32)
            active = norm_relu(output, norm_gain[layer])
            offset = offset + 2 * dilation
            if layer % 2 == 0:
                inputs = active.astype(jnp.bfloat16)
            else:
                block_in = (active + block_in.astype(jnp.float32)).astype(jnp.bfloat16)
                inputs = block_in
        return block_in
    return lax.map(one_sample, (bag_rows, bag_owner, bag_weight, carried_all))
```

```python
import functools
import jax
import jax.numpy as jnp
from jax import lax
from jax.experimental import pallas as pl
from jax.experimental.pallas import tpu as pltpu
from jax.sharding import PartitionSpec as P

table_of_id = (0, 1, 2, 2, 3, 3, 3, 3)
bag_bounds = ((0, 1), (1, 2), (2, 4), (4, 8))
epsilon = 1e-05
parts = 3
unroll = 16
vmem_bytes = 48 * 1024 * 1024


def prep_kernel(piece, shard_rows, rows_ref, owner_ref, request_ref, place_ref):
    owner = owner_ref[...]
    rows = rows_ref[...]
    owners = request_ref.shape[0]
    width, slots = owner.shape
    value_bits = (len(bag_bounds) * shard_rows).bit_length()
    owner_ids = lax.broadcasted_iota(jnp.int32, (owners, slots), 0)
    lane = lax.broadcasted_iota(jnp.int32, (owners, slots), 1)
    value = jnp.zeros((owners, slots), jnp.int32)
    for k in range(width):
        named = owner[k : k + 1, :] == owner_ids
        value = jnp.where(named, rows[k : k + 1, :] + (table_of_id[k] * shard_rows + 1), value)
    present = jnp.where(value > 0, 1, 0)
    rank = present
    step = 1
    while step < slots:
        rank = rank + jnp.where(lane >= step, pltpu.roll(rank, step, 1), 0)
        step *= 2
    rank = rank - present
    place = jnp.zeros((width, slots), jnp.int32)
    for number in range(owners):
        place = jnp.where(owner == number, rank[number : number + 1, :], place)
    part = jnp.zeros((width, slots), jnp.int32)
    for number in range(1, parts):
        part = part + jnp.where(place >= number * piece, 1, 0)
    place_ref[...] = part * ((owners - 1) * piece) + owner * piece + place
    packed = jnp.where(value > 0, ((lane - rank) << value_bits) + value, 0)
    step = 1
    level = value_bits
    while step < slots:
        moving = jnp.where(((packed >> level) & 1) == 1, packed, 0)
        packed = (packed - moving) + pltpu.roll(moving, slots - step, 1)
        step *= 2
        level += 1
    value = jnp.maximum((packed & ((1 << value_bits) - 1)) - 1, 0)
    request_ref[...] = value[:, : request_ref.shape[1]]


def gather_kernel(first, piece, index_ref, table_ref, out_ref, scratch):
    owners = index_ref.shape[0]

    def one_owner(number, carry):
        def some_rows(block, inner):
            base = block * unroll
            for i in range(unroll):
                row = index_ref[number, first + base + i]
                scratch[pl.ds(base + i, 1), :] = table_ref[pl.ds(row, 1), :]
            return inner

        lax.fori_loop(0, piece // unroll, some_rows, 0)
        out_ref[number] = scratch[...].astype(jnp.bfloat16)
        return carry

    lax.fori_loop(0, owners, one_owner, 0)


def pool_kernel(place_ref, weight_ref, *refs):
    piece_refs = refs[:parts]
    out_ref, table, picked = refs[parts:]
    count = piece_refs[0].shape[0]
    for number in range(parts):
        table[number * count : (number + 1) * count, :] = piece_refs[number][...].astype(jnp.float32)
    width, slots, lanes = picked.shape
    block = 8

    def some_slots(step, carry):
        base = step * block
        for k in range(width):
            for i in range(block):
                row = place_ref[k, base + i]
                picked[k, pl.ds(base + i, 1), :] = table[pl.ds(row, 1), :]
        return carry

    lax.fori_loop(0, slots // block, some_slots, 0)
    for t, (lower, upper) in enumerate(bag_bounds):
        total = picked[lower] * weight_ref[:, lower : lower + 1]
        for k in range(lower + 1, upper):
            total = total + picked[k] * weight_ref[:, k : k + 1]
        out_ref[:, t * lanes : (t + 1) * lanes] = total.astype(jnp.bfloat16)


def conv_kernel(pooled_ref, carried_ref, weight_ref, gain_ref, out_ref, first_buf, second_buf):
    front = 16
    rows = 256
    slots = pooled_ref.shape[0]
    layers = weight_ref.shape[0]
    first_buf[front:, :] = pooled_ref[...].astype(jnp.float32)
    offset = 0
    for layer in range(layers):
        dilation = 2**layer
        span = 2 * dilation
        source, target = (first_buf, second_buf) if layer % 2 == 0 else (second_buf, first_buf)
        source[front - span : front, :] = carried_ref[offset : offset + span, :]
        offset += span
        for block in range(slots // rows):
            base = front + block * rows
            taps = [
                source[base - tap * dilation : base - tap * dilation + rows, :].astype(jnp.bfloat16)
                for tap in range(3)
            ]
            output = jnp.dot(
                jnp.concatenate(taps, axis=1), weight_ref[layer], preferred_element_type=jnp.float32
            )
            mean = jnp.mean(output, axis=-1, keepdims=True)
            centred = output - mean
            spread = jnp.mean(centred * centred, axis=-1, keepdims=True)
            active = jnp.maximum(
                centred * lax.rsqrt(spread + epsilon) * gain_ref[layer : layer + 1, :], 0.0
            )
            if layer % 2 == 1:
                active = active + target[base : base + rows, :]
            active = active.astype(jnp.bfloat16)
            if layer == layers - 1:
                out_ref[block * rows : (block + 1) * rows, :] = active
            else:
                target[base : base + rows, :] = active.astype(jnp.float32)


def local(
    bag_rows, bag_owner, bag_weight, tables, returning, home, entry, stores, conv_weight, norm_gain
):
    owners = lax.axis_size("table")
    copies = lax.axis_size("rep")
    samples_here, slot_count, bag_width = bag_rows.shape
    token_count = samples_here * slot_count
    shard_rows = tables.shape[1]
    row_width = tables.shape[2]
    channels = conv_weight.shape[-1]
    capacity = min(token_count, (3 * token_count * bag_width + 2 * owners - 1) // (2 * owners))
    piece = capacity // parts
    params = pltpu.CompilerParams(vmem_limit_bytes=vmem_bytes)
    smem = pl.BlockSpec(memory_space=pltpu.SMEM)
    vmem = pl.BlockSpec(memory_space=pltpu.VMEM)

    weights = lax.all_gather(conv_weight, "table", axis=1, tiled=True)

    rows_by_slot = bag_rows.reshape(token_count, bag_width).T
    owner_by_slot = bag_owner.reshape(token_count, bag_width).T
    requests, place = pl.pallas_call(
        functools.partial(prep_kernel, piece, shard_rows),
        out_shape=(
            jax.ShapeDtypeStruct((owners, capacity), jnp.int32),
            jax.ShapeDtypeStruct((bag_width, token_count), jnp.int32),
        ),
        in_specs=[vmem, vmem],
        out_specs=(vmem, vmem),
        compiler_params=params,
        name="prep",
    )(rows_by_slot, owner_by_slot)
    received = lax.all_to_all(requests, "table", split_axis=0, concat_axis=0, tiled=True)
    flat_table = tables.reshape(-1, row_width).astype(jnp.float32)
    returned = []
    for number in range(parts):
        sent = pl.pallas_call(
            functools.partial(gather_kernel, number * piece, piece),
            out_shape=jax.ShapeDtypeStruct((owners, piece, row_width), jnp.bfloat16),
            in_specs=[smem, vmem],
            out_specs=vmem,
            scratch_shapes=[pltpu.VMEM((piece, row_width), jnp.float32)],
            compiler_params=params,
            cost_estimate=pl.CostEstimate(
                flops=0, bytes_accessed=24 * 1024 * 1024, transcendentals=0
            ),
            name="owner_gather",
        )(received, flat_table)
        arrived = lax.all_to_all(sent, "table", split_axis=0, concat_axis=0, tiled=True)
        returned.append(arrived.reshape(owners * piece, row_width))
    pooled = pl.pallas_call(
        pool_kernel,
        out_shape=jax.ShapeDtypeStruct((token_count, channels), jnp.bfloat16),
        in_specs=[smem, vmem] + [vmem] * parts,
        out_specs=vmem,
        scratch_shapes=[
            pltpu.VMEM((parts * owners * piece, row_width), jnp.float32),
            pltpu.VMEM((bag_width, token_count, row_width), jnp.float32),
        ],
        compiler_params=params,
        name="pool",
    )(place, bag_weight.reshape(token_count, bag_width), *returned)

    me = lax.axis_index("rep")
    carried = jnp.zeros(stores.shape[1:], stores.dtype)
    for shift in range(copies):
        arrived = stores
        if shift:
            pairs = [(source, (source + shift) % copies) for source in range(copies)]
            arrived = lax.ppermute(stores, "rep", pairs)
        wanted = (returning[0] > 0) & (home[0] == (me + copies - shift) % copies)
        chosen = lax.dynamic_index_in_dim(arrived, entry[0], 0, keepdims=False)
        carried = jnp.where(wanted, chosen, carried)

    hidden = pl.pallas_call(
        conv_kernel,
        out_shape=jax.ShapeDtypeStruct((token_count, channels), jnp.bfloat16),
        in_specs=[vmem] * 4,
        out_specs=vmem,
        scratch_shapes=[
            pltpu.VMEM((token_count + 16, channels), jnp.float32),
            pltpu.VMEM((token_count + 16, channels), jnp.float32),
        ],
        compiler_params=params,
        name="convs",
    )(pooled, carried.astype(jnp.float32), weights, norm_gain)
    return hidden.reshape(samples_here, slot_count, channels)


def solution(mesh):
    in_specs = (
        P(("table", "rep"), None, None),
        P(("table", "rep"), None, None),
        P(("table", "rep"), None, None),
        P(None, "table", None),
        P(("table", "rep")),
        P(("table", "rep")),
        P(("table", "rep")),
        P(("table", "rep"), None, None),
        P(None, "table", None),
        P(),
    )
    out_specs = P(("table", "rep"), None, None)
    return jax.shard_map(local, mesh=mesh, in_specs=in_specs, out_specs=out_specs, check_vma=False)
```

```python
import functools
import jax
import jax.numpy as jnp
from jax import lax
from jax.experimental import pallas as pl
from jax.experimental.pallas import tpu as pltpu
from jax.sharding import PartitionSpec as P

table_of_id = (0, 1, 2, 2, 3, 3, 3, 3)
bag_bounds = ((0, 1), (1, 2), (2, 4), (4, 8))
epsilon = 1e-05
parts = 3
unroll = 16
megabyte = 1024 * 1024


def prep_kernel(cuts, shard_rows, rows_ref, owner_ref, request_ref, place_ref):
    owner = owner_ref[...]
    rows = rows_ref[...]
    owners = request_ref.shape[0]
    width, slots = owner.shape
    value_bits = (len(bag_bounds) * shard_rows).bit_length()
    owner_ids = lax.broadcasted_iota(jnp.int32, (owners, slots), 0)
    lane = lax.broadcasted_iota(jnp.int32, (owners, slots), 1)
    value = jnp.zeros((owners, slots), jnp.int32)
    for k in range(width):
        named = owner[k : k + 1, :] == owner_ids
        value = jnp.where(named, rows[k : k + 1, :] + (table_of_id[k] * shard_rows + 1), value)
    present = jnp.where(value > 0, 1, 0)
    rank = present
    step = 1
    while step < slots:
        rank = rank + jnp.where(lane >= step, pltpu.roll(rank, step, 1), 0)
        step *= 2
    rank = rank - present
    place = jnp.zeros((width, slots), jnp.int32)
    for number in range(owners):
        place = jnp.where(owner == number, rank[number : number + 1, :], place)
    landing = jnp.zeros((width, slots), jnp.int32)
    for start, stop in zip(cuts[:-1], cuts[1:]):
        where = owners * start + owner * (stop - start) + place - start
        landing = jnp.where(place >= start, where, landing)
    place_ref[...] = landing
    packed = jnp.where(value > 0, ((lane - rank) << value_bits) + value, 0)
    step = 1
    level = value_bits
    while step < slots:
        moving = jnp.where(((packed >> level) & 1) == 1, packed, 0)
        packed = (packed - moving) + pltpu.roll(moving, slots - step, 1)
        step *= 2
        level += 1
    value = jnp.maximum((packed & ((1 << value_bits) - 1)) - 1, 0)
    request_ref[...] = value[:, : request_ref.shape[1]]


def gather_kernel(capacity, first, index_ref, table_ref, out_ref, scratch):
    owners, piece, _ = out_ref.shape

    def one_owner(number, carry):
        origin = number * capacity + first

        def some_rows(block, inner):
            base = pl.multiple_of(block * unroll, unroll)
            picks = [index_ref[origin + base + i] for i in range(unroll)]
            rows = [table_ref[pick] for pick in picks]
            for i in range(unroll):
                scratch[pl.ds(base + i, 1), :] = rows[i]
            return inner

        lax.fori_loop(0, piece // unroll, some_rows, 0)
        out_ref[number] = scratch[...].astype(jnp.bfloat16)
        return carry

    lax.fori_loop(0, owners, one_owner, 0)


def stage_kernel(number, first, place_ref, weight_ref, carried_ref, filter_ref, gain_ref, *refs):
    piece_refs = refs[: number + 1]
    refs = refs[number + 1 + (number > 0) :]
    out_ref, state_ref, table, picked, first_buf, second_buf, result, semaphore = refs
    width, slots, lanes = picked.shape
    start = 0
    for piece_ref in piece_refs:
        count = piece_ref.shape[0]
        rows = 256

        def widen(step, carry, piece_ref=piece_ref, start=start):
            base = pl.multiple_of(step * rows, rows)
            table[pl.ds(start + base, rows), :] = piece_ref[pl.ds(base, rows), :].astype(jnp.float32)
            return carry

        lax.fori_loop(0, count // rows, widen, 0)
        start += count

    def some_slots(step, carry):
        base = pl.multiple_of(step * 8, 8)
        for k in range(width):
            picks = [place_ref[k, first + base + i] for i in range(8)]
            rows = [table[pl.ds(pick, 1), :] for pick in picks]
            for i in range(8):
                picked[k, pl.ds(base + i, 1), :] = rows[i]
        return carry

    lax.fori_loop(0, slots // 8, some_slots, 0)
    front = 16
    for t, (lower, upper) in enumerate(bag_bounds):
        total = picked[lower] * weight_ref[first : first + slots, lower : lower + 1]
        for k in range(lower + 1, upper):
            total = total + picked[k] * weight_ref[first : first + slots, k : k + 1]
        total = total.astype(jnp.bfloat16).astype(jnp.float32)
        first_buf[front:, t * lanes : (t + 1) * lanes] = total

    layers = filter_ref.shape[0]
    offset = 0
    for layer in range(layers):
        dilation = 2**layer
        span = 2 * dilation
        source, target = (first_buf, second_buf) if layer % 2 == 0 else (second_buf, first_buf)
        source[front - span : front, :] = carried_ref[offset : offset + span, :]
        state_ref[offset : offset + span, :] = source[front + slots - span : front + slots, :]
        offset += span
        for begin in range(0, slots, 256):
            rows = min(256, slots - begin)
            base = front + begin
            taps = [
                source[base - tap * dilation : base - tap * dilation + rows, :].astype(jnp.bfloat16)
                for tap in range(3)
            ]
            output = jnp.dot(
                jnp.concatenate(taps, axis=1), filter_ref[layer], preferred_element_type=jnp.float32
            )
            mean = jnp.mean(output, axis=-1, keepdims=True)
            centred = output - mean
            spread = jnp.mean(centred * centred, axis=-1, keepdims=True)
            active = jnp.maximum(
                centred * lax.rsqrt(spread + epsilon) * gain_ref[layer : layer + 1, :], 0.0
            )
            if layer % 2 == 1:
                active = active + target[base : base + rows, :]
            active = active.astype(jnp.bfloat16)
            if layer == layers - 1:
                result[begin : begin + rows, :] = active
            else:
                target[base : base + rows, :] = active.astype(jnp.float32)
    copy = pltpu.make_async_copy(result, out_ref.at[pl.ds(first, slots), :], semaphore)
    copy.start()
    copy.wait()


def gather_filters(conv_weight):
    owners = lax.axis_size("table")
    copies = lax.axis_size("rep")
    layers, depth, channels = conv_weight.shape
    if owners % 2 or copies % 2 or layers % 2:
        return lax.all_gather(conv_weight, "table", axis=1, tiled=True)
    half = layers // 2
    parity = lax.axis_index("table") % 2
    side = lax.axis_index("rep") % 2
    groups = [list(range(start, owners, 2)) for start in range(2)]
    mine = lax.dynamic_slice_in_dim(conv_weight, side * half, half, 0)
    mine = lax.all_gather(mine, "table", axis_index_groups=groups, axis=0, tiled=False)
    other = lax.ppermute(mine, "rep", [(r, r ^ 1) for r in range(copies)])
    low = jnp.where(side == 0, mine, other)
    high = jnp.where(side == 0, other, mine)
    own = jnp.concatenate([low, high], axis=1)
    partner = lax.ppermute(own, "table", [(i, i ^ 1) for i in range(owners)])
    even = jnp.where(parity == 0, own, partner)
    odd = jnp.where(parity == 0, partner, own)
    both = jnp.stack([even, odd], axis=1)
    return jnp.transpose(both, (2, 0, 1, 3, 4)).reshape(layers, owners * depth, channels)


def local(
    bag_rows, bag_owner, bag_weight, tables, returning, home, entry, stores, conv_weight, norm_gain
):
    owners = lax.axis_size("table")
    copies = lax.axis_size("rep")
    samples_here, slot_count, bag_width = bag_rows.shape
    token_count = samples_here * slot_count
    shard_rows = tables.shape[1]
    row_width = tables.shape[2]
    channels = conv_weight.shape[-1]
    capacity = min(token_count, (3 * token_count * bag_width + 2 * owners - 1) // (2 * owners))
    cuts = [capacity * cut // parts for cut in range(parts + 1)]
    slot_cuts = cuts[:-1] + [token_count]
    smem = pl.BlockSpec(memory_space=pltpu.SMEM)
    vmem = pl.BlockSpec(memory_space=pltpu.VMEM)
    anywhere = pl.BlockSpec(memory_space=pl.ANY)

    filters = gather_filters(conv_weight)

    rows_by_slot = bag_rows.reshape(token_count, bag_width).T
    owner_by_slot = bag_owner.reshape(token_count, bag_width).T
    requests, place = pl.pallas_call(
        functools.partial(prep_kernel, cuts, shard_rows),
        out_shape=(
            jax.ShapeDtypeStruct((owners, capacity), jnp.int32),
            jax.ShapeDtypeStruct((bag_width, token_count), jnp.int32),
        ),
        in_specs=[vmem, vmem],
        out_specs=(vmem, vmem),
        compiler_params=pltpu.CompilerParams(vmem_limit_bytes=8 * megabyte),
        name="prep",
    )(rows_by_slot, owner_by_slot)
    received = lax.all_to_all(requests, "table", split_axis=0, concat_axis=0, tiled=True)
    received = received.reshape(owners * capacity)
    wide_table = tables.astype(jnp.float32).reshape(-1, 1, row_width)
    returned = []
    for number in range(parts):
        piece = cuts[number + 1] - cuts[number]
        sent = pl.pallas_call(
            functools.partial(gather_kernel, capacity, cuts[number]),
            out_shape=jax.ShapeDtypeStruct((owners, piece, row_width), jnp.bfloat16),
            in_specs=[smem, vmem],
            out_specs=vmem,
            scratch_shapes=[pltpu.VMEM((piece, row_width), jnp.float32)],
            compiler_params=pltpu.CompilerParams(vmem_limit_bytes=12 * megabyte),
            cost_estimate=pl.CostEstimate(
                flops=0, bytes_accessed=20 * megabyte, transcendentals=0
            ),
            name="owner_gather",
        )(received, wide_table)
        arrived = lax.all_to_all(sent, "table", split_axis=0, concat_axis=0, tiled=True)
        returned.append(arrived.reshape(owners * piece, row_width))

    me = lax.axis_index("rep")
    carried = jnp.zeros(stores.shape[1:], stores.dtype)
    for shift in range(copies):
        arrived = stores
        if shift:
            pairs = [(source, (source + shift) % copies) for source in range(copies)]
            arrived = lax.ppermute(stores, "rep", pairs)
        wanted = (returning[0] > 0) & (home[0] == (me + copies - shift) % copies)
        chosen = lax.dynamic_index_in_dim(arrived, entry[0], 0, keepdims=False)
        carried = jnp.where(wanted, chosen, carried)

    state = carried.astype(jnp.float32)
    weight_by_slot = bag_weight.reshape(token_count, bag_width)
    hidden = None
    for number in range(parts):
        first, last = slot_cuts[number], slot_cuts[number + 1]
        slots = last - first
        known = [] if hidden is None else [hidden]
        hidden, state = pl.pallas_call(
            functools.partial(stage_kernel, number, first),
            out_shape=(
                jax.ShapeDtypeStruct((token_count, channels), jnp.bfloat16),
                jax.ShapeDtypeStruct(state.shape, jnp.float32),
            ),
            in_specs=[smem] + [vmem] * (5 + number) + [anywhere] * len(known),
            out_specs=(anywhere, vmem),
            scratch_shapes=[
                pltpu.VMEM((owners * cuts[number + 1], row_width), jnp.float32),
                pltpu.VMEM((bag_width, slots, row_width), jnp.float32),
                pltpu.VMEM((slots + 16, channels), jnp.float32),
                pltpu.VMEM((slots + 16, channels), jnp.float32),
                pltpu.VMEM((slots, channels), jnp.bfloat16),
                pltpu.SemaphoreType.DMA,
            ],
            input_output_aliases={6 + number: 0} if known else {},
            compiler_params=pltpu.CompilerParams(vmem_limit_bytes=32 * megabyte),
            cost_estimate=pl.CostEstimate(
                flops=2 * slots * 3 * channels * channels * conv_weight.shape[0],
                bytes_accessed=24 * megabyte,
                transcendentals=0,
            ),
            name="stage",
        )(place, weight_by_slot, state, filters, norm_gain, *returned[: number + 1], *known)
    return hidden.reshape(samples_here, slot_count, channels)


def solution(mesh):
    in_specs = (
        P(("table", "rep"), None, None),
        P(("table", "rep"), None, None),
        P(("table", "rep"), None, None),
        P(None, "table", None),
        P(("table", "rep")),
        P(("table", "rep")),
        P(("table", "rep")),
        P(("table", "rep"), None, None),
        P(None, "table", None),
        P(),
    )
    out_specs = P(("table", "rep"), None, None)
    return jax.shard_map(local, mesh=mesh, in_specs=in_specs, out_specs=out_specs, check_vma=False)
```

```python
import functools
import jax
import jax.numpy as jnp
from jax import lax
from jax.experimental import pallas as pl
from jax.experimental.pallas import tpu as pltpu
from jax.sharding import PartitionSpec as P

table_of_id = (0, 1, 2, 2, 3, 3, 3, 3)
bag_bounds = ((0, 1), (1, 2), (2, 4), (4, 8))
epsilon = 1e-05
parts = 2
unroll = 32
megabyte = 1024 * 1024


def prep_kernel(cuts, shard_rows, me_ref, rows_ref, owner_ref, request_ref, place_ref):
    owner = owner_ref[...]
    rows = rows_ref[...]
    owners = request_ref.shape[0]
    width, slots = owner.shape
    value_bits = (len(bag_bounds) * shard_rows).bit_length()
    owner_ids = lax.broadcasted_iota(jnp.int32, (owners, slots), 0)
    lane = lax.broadcasted_iota(jnp.int32, (owners, slots), 1)
    value = jnp.zeros((owners, slots), jnp.int32)
    for k in range(width):
        named = owner[k : k + 1, :] == owner_ids
        value = jnp.where(named, rows[k : k + 1, :] + (table_of_id[k] * shard_rows + 1), value)
    present = jnp.where(value > 0, 1, 0)
    rank = present
    step = 1
    while step < slots:
        rank = rank + jnp.where(lane >= step, pltpu.roll(rank, step, 1), 0)
        step *= 2
    rank = rank - present
    place = jnp.zeros((width, slots), jnp.int32)
    for number in range(owners):
        place = jnp.where(owner == number, rank[number : number + 1, :], place)
    landing = jnp.zeros((width, slots), jnp.int32)
    for start, stop in zip(cuts[:-1], cuts[1:]):
        where = owners * start + (owner ^ me_ref[0]) * (stop - start) + place - start
        landing = jnp.where(place >= start, where, landing)
    place_ref[...] = landing
    packed = jnp.where(value > 0, ((lane - rank) << value_bits) + value, 0)
    step = 1
    level = value_bits
    while step < slots:
        moving = jnp.where(((packed >> level) & 1) == 1, packed, 0)
        packed = (packed - moving) + pltpu.roll(moving, slots - step, 1)
        step *= 2
        level += 1
    value = jnp.maximum((packed & ((1 << value_bits) - 1)) - 1, 0)
    request_ref[...] = value[:, : request_ref.shape[1]]


def gather_kernel(first, me_ref, index_ref, table_ref, *refs):
    owners = index_ref.shape[0]
    out_refs = refs[:owners]
    wide, picked, packed, index, index_sem, out_sems = refs[owners:]
    index_copy = pltpu.make_async_copy(index_ref, index, index_sem)
    index_copy.start()
    rows = 256

    def widen(step, carry):
        base = pl.multiple_of(step * rows, rows)
        wide[pl.ds(base, rows), :] = table_ref[pl.ds(base, rows), :].astype(jnp.float32)
        return carry

    lax.fori_loop(0, table_ref.shape[0] // rows, widen, 0)
    index_copy.wait()
    piece = picked.shape[0]
    copies = []
    for number in range(owners):
        requester = me_ref[0] ^ number

        def some_rows(block, carry, requester=requester):
            base = pl.multiple_of(block * unroll, unroll)
            picks = [index[requester, first + base + i] for i in range(unroll)]
            found = [wide[pl.ds(pick, 1), :] for pick in picks]
            for i in range(unroll):
                picked[pl.ds(base + i, 1), :] = found[i]
            return carry

        lax.fori_loop(0, piece // unroll, some_rows, 0)
        packed[number] = picked[...].astype(jnp.bfloat16)
        copy = pltpu.make_async_copy(packed.at[number], out_refs[number], out_sems.at[number])
        copy.start()
        copies.append(copy)
    for copy in copies:
        copy.wait()


def stage_kernel(
    pieces, first, aliased, place_ref, weight_ref, carried_ref, gain_ref, filter_ref, *refs
):
    piece_refs = refs[:pieces]
    refs = refs[pieces + aliased :]
    out_ref, state_ref, packed, table, picked, filters, first_buf, second_buf, result = refs[:9]
    piece_sems, filter_sems, out_sem = refs[9:]
    width, slots, lanes = picked.shape
    copies = []
    start = 0
    for number, piece_ref in enumerate(piece_refs):
        count = piece_ref.shape[0]
        copy = pltpu.make_async_copy(
            piece_ref, packed.at[pl.ds(start, count), :], piece_sems.at[number]
        )
        copy.start()
        copies.append((copy, start, count))
        start += count
    layers = filter_ref.shape[0]
    filter_copies = []
    for layer in range(layers):
        copy = pltpu.make_async_copy(filter_ref.at[layer], filters.at[layer], filter_sems.at[layer])
        copy.start()
        filter_copies.append(copy)
    for copy, start, count in copies:
        copy.wait()
        table[start : start + count, :] = packed[start : start + count, :].astype(jnp.float32)

    def some_slots(step, carry):
        base = pl.multiple_of(step * 8, 8)
        for k in range(width):
            picks = [place_ref[k, first + base + i] for i in range(8)]
            rows = [table[pl.ds(pick, 1), :] for pick in picks]
            for i in range(8):
                picked[k, pl.ds(base + i, 1), :] = rows[i]
        return carry

    lax.fori_loop(0, slots // 8, some_slots, 0)
    front = 16
    for t, (lower, upper) in enumerate(bag_bounds):
        total = picked[lower] * weight_ref[first : first + slots, lower : lower + 1]
        for k in range(lower + 1, upper):
            total = total + picked[k] * weight_ref[first : first + slots, k : k + 1]
        total = total.astype(jnp.bfloat16).astype(jnp.float32)
        first_buf[front:, t * lanes : (t + 1) * lanes] = total

    offset = 0
    for layer in range(layers):
        dilation = 2**layer
        span = 2 * dilation
        source, target = (first_buf, second_buf) if layer % 2 == 0 else (second_buf, first_buf)
        source[front - span : front, :] = carried_ref[offset : offset + span, :]
        state_ref[offset : offset + span, :] = source[front + slots - span : front + slots, :]
        offset += span
        filter_copies[layer].wait()
        for begin in range(0, slots, 256):
            rows = min(256, slots - begin)
            base = front + begin
            taps = [
                source[base - tap * dilation : base - tap * dilation + rows, :].astype(jnp.bfloat16)
                for tap in range(3)
            ]
            output = jnp.dot(
                jnp.concatenate(taps, axis=1), filters[layer], preferred_element_type=jnp.float32
            )
            mean = jnp.mean(output, axis=-1, keepdims=True)
            centred = output - mean
            spread = jnp.mean(centred * centred, axis=-1, keepdims=True)
            active = jnp.maximum(
                centred * lax.rsqrt(spread + epsilon) * gain_ref[layer : layer + 1, :], 0.0
            )
            if layer % 2 == 1:
                active = active + target[base : base + rows, :]
            active = active.astype(jnp.bfloat16)
            if layer == layers - 1:
                result[begin : begin + rows, :] = active
            else:
                target[base : base + rows, :] = active.astype(jnp.float32)
    copy = pltpu.make_async_copy(result, out_ref.at[pl.ds(first, slots), :], out_sem)
    copy.start()
    copy.wait()


def gather_filters(conv_weight, after):
    owners = lax.axis_size("table")
    copies = lax.axis_size("rep")
    layers, depth, channels = conv_weight.shape
    if owners % 2 or copies % 2 or layers % 2:
        return lax.all_gather(conv_weight, "table", axis=1, tiled=True)
    half = layers // 2
    parity = lax.axis_index("table") % 2
    side = lax.axis_index("rep") % 2
    groups = [list(range(start, owners, 2)) for start in range(2)]
    mine = lax.dynamic_slice_in_dim(conv_weight, side * half, half, 0)
    mine = lax.all_gather(mine, "table", axis_index_groups=groups, axis=0, tiled=False)
    mine, _ = lax.optimization_barrier((mine, after))
    other = lax.ppermute(mine, "rep", [(r, r ^ 1) for r in range(copies)])
    low = jnp.where(side == 0, mine, other)
    high = jnp.where(side == 0, other, mine)
    own = jnp.concatenate([low, high], axis=1)
    partner = lax.ppermute(own, "table", [(i, i ^ 1) for i in range(owners)])
    even = jnp.where(parity == 0, own, partner)
    odd = jnp.where(parity == 0, partner, own)
    both = jnp.stack([even, odd], axis=1)
    return jnp.transpose(both, (2, 0, 1, 3, 4)).reshape(layers, owners * depth, channels)


def local(
    bag_rows, bag_owner, bag_weight, tables, returning, home, entry, stores, conv_weight, norm_gain
):
    owners = lax.axis_size("table")
    copies = lax.axis_size("rep")
    samples_here, slot_count, bag_width = bag_rows.shape
    token_count = samples_here * slot_count
    shard_rows = tables.shape[1]
    row_width = tables.shape[2]
    channels = conv_weight.shape[-1]
    capacity = min(token_count, (3 * token_count * bag_width + 2 * owners - 1) // (2 * owners))
    cuts = [capacity * cut // parts for cut in range(parts + 1)]
    slot_cuts = cuts[:-1] + [token_count]
    smem = pl.BlockSpec(memory_space=pltpu.SMEM)
    vmem = pl.BlockSpec(memory_space=pltpu.VMEM)
    anywhere = pl.BlockSpec(memory_space=pl.ANY)

    me = lax.axis_index("table").astype(jnp.int32).reshape(1)
    rows_by_slot = bag_rows.reshape(token_count, bag_width).T
    owner_by_slot = bag_owner.reshape(token_count, bag_width).T
    requests, place = pl.pallas_call(
        functools.partial(prep_kernel, cuts, shard_rows),
        out_shape=(
            jax.ShapeDtypeStruct((owners, capacity), jnp.int32),
            jax.ShapeDtypeStruct((bag_width, token_count), jnp.int32),
        ),
        in_specs=[smem, vmem, vmem],
        out_specs=(vmem, vmem),
        compiler_params=pltpu.CompilerParams(vmem_limit_bytes=8 * megabyte),
        name="prep",
    )(me, rows_by_slot, owner_by_slot)
    received = lax.all_to_all(requests, "table", split_axis=0, concat_axis=0, tiled=True)
    flat_table = tables.reshape(-1, row_width)
    far = owners // 2
    order = [shift for near in range(far) for shift in (far + near, near) if shift]
    returned = []
    for number in range(parts):
        piece = cuts[number + 1] - cuts[number]
        sent = pl.pallas_call(
            functools.partial(gather_kernel, cuts[number]),
            out_shape=[jax.ShapeDtypeStruct((piece, row_width), jnp.bfloat16)] * owners,
            in_specs=[smem, anywhere, vmem],
            out_specs=[anywhere] * owners,
            scratch_shapes=[
                pltpu.VMEM(flat_table.shape, jnp.float32),
                pltpu.VMEM((piece, row_width), jnp.float32),
                pltpu.VMEM((owners, piece, row_width), jnp.bfloat16),
                pltpu.SMEM((owners, capacity), jnp.int32),
                pltpu.SemaphoreType.DMA,
                pltpu.SemaphoreType.DMA((owners,)),
            ],
            compiler_params=pltpu.CompilerParams(vmem_limit_bytes=24 * megabyte),
            cost_estimate=pl.CostEstimate(
                flops=0, bytes_accessed=30 * megabyte, transcendentals=0
            ),
            name="owner_gather",
        )(me, received, flat_table)
        arrived = list(sent)
        for shift in order:
            pairs = [(source, source ^ shift) for source in range(owners)]
            arrived[shift] = lax.ppermute(sent[shift], "table", pairs)
        returned.append(arrived)
    filters = gather_filters(conv_weight, sent[0])

    side = lax.axis_index("rep")
    carried = jnp.zeros(stores.shape[1:], stores.dtype)
    for shift in range(copies):
        arrived = stores
        if shift:
            pairs = [(source, (source + shift) % copies) for source in range(copies)]
            arrived = lax.ppermute(stores, "rep", pairs)
        wanted = (returning[0] > 0) & (home[0] == (side + copies - shift) % copies)
        chosen = lax.dynamic_index_in_dim(arrived, entry[0], 0, keepdims=False)
        carried = jnp.where(wanted, chosen, carried)

    state = carried.astype(jnp.float32)
    weight_by_slot = bag_weight.reshape(token_count, bag_width)
    hidden = None
    for number in range(parts):
        first, last = slot_cuts[number], slot_cuts[number + 1]
        slots = last - first
        known = [] if hidden is None else [hidden]
        pieces = [block for arrived in returned[: number + 1] for block in arrived]
        hidden, state = pl.pallas_call(
            functools.partial(stage_kernel, len(pieces), first, len(known)),
            out_shape=(
                jax.ShapeDtypeStruct((token_count, channels), jnp.bfloat16),
                jax.ShapeDtypeStruct(state.shape, jnp.float32),
            ),
            in_specs=[smem, vmem, vmem, vmem] + [anywhere] * (1 + len(pieces) + len(known)),
            out_specs=(anywhere, vmem),
            scratch_shapes=[
                pltpu.VMEM((owners * cuts[number + 1], row_width), jnp.bfloat16),
                pltpu.VMEM((owners * cuts[number + 1], row_width), jnp.float32),
                pltpu.VMEM((bag_width, slots, row_width), jnp.float32),
                pltpu.VMEM(filters.shape, filters.dtype),
                pltpu.VMEM((slots + 16, channels), jnp.float32),
                pltpu.VMEM((slots + 16, channels), jnp.float32),
                pltpu.VMEM((slots, channels), jnp.bfloat16),
                pltpu.SemaphoreType.DMA((len(pieces),)),
                pltpu.SemaphoreType.DMA((filters.shape[0],)),
                pltpu.SemaphoreType.DMA,
            ],
            input_output_aliases={5 + len(pieces): 0} if known else {},
            compiler_params=pltpu.CompilerParams(vmem_limit_bytes=60 * megabyte),
            cost_estimate=pl.CostEstimate(
                flops=2 * slots * 3 * channels * channels * conv_weight.shape[0],
                bytes_accessed=24 * megabyte,
                transcendentals=0,
            ),
            name="stage",
        )(place, weight_by_slot, state, norm_gain, filters, *pieces, *known)
    return hidden.reshape(samples_here, slot_count, channels)


def solution(mesh):
    in_specs = (
        P(("table", "rep"), None, None),
        P(("table", "rep"), None, None),
        P(("table", "rep"), None, None),
        P(None, "table", None),
        P(("table", "rep")),
        P(("table", "rep")),
        P(("table", "rep")),
        P(("table", "rep"), None, None),
        P(None, "table", None),
        P(),
    )
    out_specs = P(("table", "rep"), None, None)
    return jax.shard_map(local, mesh=mesh, in_specs=in_specs, out_specs=out_specs, check_vma=False)
```

```python
import functools
import jax
import jax.numpy as jnp
from jax import lax
from jax.experimental import pallas as pl
from jax.experimental.pallas import tpu as pltpu
from jax.sharding import PartitionSpec as P

table_of_id = (0, 1, 2, 2, 3, 3, 3, 3)
bag_bounds = ((0, 1), (1, 2), (2, 4), (4, 8))
epsilon = 1e-05
parts = 3
unroll = 32
megabyte = 1024 * 1024


def prep_kernel(cuts, shard_rows, rows_ref, owner_ref, request_ref, place_ref):
    owner = owner_ref[...]
    rows = rows_ref[...]
    owners = request_ref.shape[0]
    width, slots = owner.shape
    value_bits = (len(bag_bounds) * shard_rows).bit_length()
    owner_ids = lax.broadcasted_iota(jnp.int32, (owners, slots), 0)
    lane = lax.broadcasted_iota(jnp.int32, (owners, slots), 1)
    value = jnp.zeros((owners, slots), jnp.int32)
    for k in range(width):
        named = owner[k : k + 1, :] == owner_ids
        value = jnp.where(named, rows[k : k + 1, :] + (table_of_id[k] * shard_rows + 1), value)
    present = jnp.where(value > 0, 1, 0)
    rank = present
    step = 1
    while step < slots:
        rank = rank + jnp.where(lane >= step, pltpu.roll(rank, step, 1), 0)
        step *= 2
    rank = rank - present
    place = jnp.zeros((width, slots), jnp.int32)
    for number in range(owners):
        place = jnp.where(owner == number, rank[number : number + 1, :], place)
    landing = jnp.zeros((width, slots), jnp.int32)
    for start, stop in zip(cuts[:-1], cuts[1:]):
        where = owners * start + owner * (stop - start) + place - start
        landing = jnp.where(place >= start, where, landing)
    place_ref[...] = landing
    packed = jnp.where(value > 0, ((lane - rank) << value_bits) + value, 0)
    step = 1
    level = value_bits
    while step < slots:
        moving = jnp.where(((packed >> level) & 1) == 1, packed, 0)
        packed = (packed - moving) + pltpu.roll(moving, slots - step, 1)
        step *= 2
        level += 1
    value = jnp.maximum((packed & ((1 << value_bits) - 1)) - 1, 0)
    for number in range(owners):
        request_ref[number] = value[number : number + 1, : request_ref.shape[2]]


def pass_kernel(*refs):
    pass


def tie(array, *others):
    anywhere = pl.BlockSpec(memory_space=pl.ANY)
    return pl.pallas_call(
        pass_kernel,
        out_shape=jax.ShapeDtypeStruct(array.shape, array.dtype),
        in_specs=[anywhere] * (1 + len(others)),
        out_specs=anywhere,
        input_output_aliases={0: 0},
        name="tie",
    )(array, *others)


def gather_kernel(capacity, first, index_ref, table_ref, out_ref, *scratch):
    wide, picked, packed, index, index_sem, out_sems = scratch
    owners, piece, _ = out_ref.shape
    index_copy = pltpu.make_async_copy(index_ref, index, index_sem)
    index_copy.start()
    rows = 256

    def widen(step, carry):
        base = pl.multiple_of(step * rows, rows)
        wide[pl.ds(base, rows), :] = table_ref[pl.ds(base, rows), :].astype(jnp.float32)
        return carry

    lax.fori_loop(0, table_ref.shape[0] // rows, widen, 0)
    index_copy.wait()
    copies = []
    for number in range(owners):
        origin = number * capacity + first

        def some_rows(block, carry, origin=origin):
            base = pl.multiple_of(block * unroll, unroll)
            picks = [index[origin + base + i] for i in range(unroll)]
            found = [wide[pl.ds(pick, 1), :] for pick in picks]
            for i in range(unroll):
                picked[pl.ds(base + i, 1), :] = found[i]
            return carry

        lax.fori_loop(0, piece // unroll, some_rows, 0)
        packed[number] = picked[...].astype(jnp.bfloat16)
        copy = pltpu.make_async_copy(packed.at[number], out_ref.at[number], out_sems.at[number])
        copy.start()
        copies.append(copy)
    for copy in copies:
        copy.wait()


def stage_kernel(number, first, place_ref, weight_ref, carried_ref, filter_ref, gain_ref, *refs):
    piece_refs = refs[: number + 1]
    refs = refs[number + 1 + (number > 0) :]
    out_ref, state_ref, table, picked, first_buf, second_buf, result, semaphore = refs
    width, slots, lanes = picked.shape
    start = 0
    for piece_ref in piece_refs:
        count = piece_ref.shape[0]
        rows = 256

        def widen(step, carry, piece_ref=piece_ref, start=start):
            base = pl.multiple_of(step * rows, rows)
            table[pl.ds(start + base, rows), :] = piece_ref[pl.ds(base, rows), :].astype(jnp.float32)
            return carry

        lax.fori_loop(0, count // rows, widen, 0)
        start += count

    def some_slots(step, carry):
        base = pl.multiple_of(step * 8, 8)
        for k in range(width):
            picks = [place_ref[k, first + base + i] for i in range(8)]
            rows = [table[pl.ds(pick, 1), :] for pick in picks]
            for i in range(8):
                picked[k, pl.ds(base + i, 1), :] = rows[i]
        return carry

    lax.fori_loop(0, slots // 8, some_slots, 0)
    front = 16
    for t, (lower, upper) in enumerate(bag_bounds):
        total = picked[lower] * weight_ref[first : first + slots, lower : lower + 1]
        for k in range(lower + 1, upper):
            total = total + picked[k] * weight_ref[first : first + slots, k : k + 1]
        total = total.astype(jnp.bfloat16).astype(jnp.float32)
        first_buf[front:, t * lanes : (t + 1) * lanes] = total

    layers = filter_ref.shape[0]
    offset = 0
    for layer in range(layers):
        dilation = 2**layer
        span = 2 * dilation
        source, target = (first_buf, second_buf) if layer % 2 == 0 else (second_buf, first_buf)
        source[front - span : front, :] = carried_ref[offset : offset + span, :]
        state_ref[offset : offset + span, :] = source[front + slots - span : front + slots, :]
        offset += span
        for begin in range(0, slots, 256):
            rows = min(256, slots - begin)
            base = front + begin
            taps = [
                source[base - tap * dilation : base - tap * dilation + rows, :].astype(jnp.bfloat16)
                for tap in range(3)
            ]
            output = jnp.dot(
                jnp.concatenate(taps, axis=1), filter_ref[layer], preferred_element_type=jnp.float32
            )
            mean = jnp.mean(output, axis=-1, keepdims=True)
            centred = output - mean
            spread = jnp.mean(centred * centred, axis=-1, keepdims=True)
            active = jnp.maximum(
                centred * lax.rsqrt(spread + epsilon) * gain_ref[layer : layer + 1, :], 0.0
            )
            if layer % 2 == 1:
                active = active + target[base : base + rows, :]
            active = active.astype(jnp.bfloat16)
            if layer == layers - 1:
                result[begin : begin + rows, :] = active
            else:
                target[base : base + rows, :] = active.astype(jnp.float32)
    copy = pltpu.make_async_copy(result, out_ref.at[pl.ds(first, slots), :], semaphore)
    copy.start()
    copy.wait()


def gather_filters(conv_weight, after):
    owners = lax.axis_size("table")
    copies = lax.axis_size("rep")
    layers, depth, channels = conv_weight.shape
    if owners % 2 or copies % 2 or layers % 2:
        return lax.all_gather(conv_weight, "table", axis=1, tiled=True)
    half = layers // 2
    parity = lax.axis_index("table") % 2
    side = lax.axis_index("rep") % 2
    groups = [list(range(start, owners, 2)) for start in range(2)]
    mine = lax.dynamic_slice_in_dim(conv_weight, side * half, half, 0)
    mine = lax.all_gather(mine, "table", axis_index_groups=groups, axis=0, tiled=False)
    mine = tie(mine, after)
    other = lax.ppermute(mine, "rep", [(r, r ^ 1) for r in range(copies)])
    low = jnp.where(side == 0, mine, other)
    high = jnp.where(side == 0, other, mine)
    own = jnp.concatenate([low, high], axis=1)
    partner = lax.ppermute(own, "table", [(i, i ^ 1) for i in range(owners)])
    even = jnp.where(parity == 0, own, partner)
    odd = jnp.where(parity == 0, partner, own)
    both = jnp.stack([even, odd], axis=1)
    return jnp.transpose(both, (2, 0, 1, 3, 4)).reshape(layers, owners * depth, channels)


def local(
    bag_rows, bag_owner, bag_weight, tables, returning, home, entry, stores, conv_weight, norm_gain
):
    owners = lax.axis_size("table")
    copies = lax.axis_size("rep")
    samples_here, slot_count, bag_width = bag_rows.shape
    token_count = samples_here * slot_count
    shard_rows = tables.shape[1]
    row_width = tables.shape[2]
    channels = conv_weight.shape[-1]
    capacity = min(token_count, (3 * token_count * bag_width + 2 * owners - 1) // (2 * owners))
    cuts = [capacity * cut // parts for cut in range(parts + 1)]
    slot_cuts = cuts[:-1] + [token_count]
    smem = pl.BlockSpec(memory_space=pltpu.SMEM)
    vmem = pl.BlockSpec(memory_space=pltpu.VMEM)
    anywhere = pl.BlockSpec(memory_space=pl.ANY)

    rows_by_slot = bag_rows.reshape(token_count, bag_width).T
    owner_by_slot = bag_owner.reshape(token_count, bag_width).T
    requests, place = pl.pallas_call(
        functools.partial(prep_kernel, cuts, shard_rows),
        out_shape=(
            jax.ShapeDtypeStruct((owners, 1, capacity), jnp.int32),
            jax.ShapeDtypeStruct((bag_width, token_count), jnp.int32),
        ),
        in_specs=[vmem, vmem],
        out_specs=(vmem, vmem),
        compiler_params=pltpu.CompilerParams(vmem_limit_bytes=8 * megabyte),
        name="prep",
    )(rows_by_slot, owner_by_slot)
    received = lax.all_to_all(requests, "table", split_axis=0, concat_axis=0, tiled=True)
    received = received.reshape(owners * capacity)
    flat_table = tables.reshape(-1, row_width)
    returned = []
    for number in range(parts):
        piece = cuts[number + 1] - cuts[number]
        sent = pl.pallas_call(
            functools.partial(gather_kernel, capacity, cuts[number]),
            out_shape=jax.ShapeDtypeStruct((owners, piece, row_width), jnp.bfloat16),
            in_specs=[anywhere, vmem],
            out_specs=anywhere,
            scratch_shapes=[
                pltpu.VMEM(flat_table.shape, jnp.float32),
                pltpu.VMEM((piece, row_width), jnp.float32),
                pltpu.VMEM((owners, piece, row_width), jnp.bfloat16),
                pltpu.SMEM((owners * capacity,), jnp.int32),
                pltpu.SemaphoreType.DMA,
                pltpu.SemaphoreType.DMA((owners,)),
            ],
            compiler_params=pltpu.CompilerParams(vmem_limit_bytes=16 * megabyte),
            cost_estimate=pl.CostEstimate(
                flops=0, bytes_accessed=20 * megabyte, transcendentals=0
            ),
            name="owner_gather",
        )(received, flat_table)
        arrived = lax.all_to_all(sent, "table", split_axis=0, concat_axis=0, tiled=True)
        returned.append(arrived.reshape(owners * piece, row_width))
        if number == 1:
            filters = gather_filters(conv_weight, sent)

    me = lax.axis_index("rep")
    carried = jnp.zeros(stores.shape[1:], stores.dtype)
    for shift in range(copies):
        arrived = stores
        if shift:
            pairs = [(source, (source + shift) % copies) for source in range(copies)]
            arrived = lax.ppermute(stores, "rep", pairs)
        wanted = (returning[0] > 0) & (home[0] == (me + copies - shift) % copies)
        chosen = lax.dynamic_index_in_dim(arrived, entry[0], 0, keepdims=False)
        carried = jnp.where(wanted, chosen, carried)

    state = carried.astype(jnp.float32)
    weight_by_slot = bag_weight.reshape(token_count, bag_width)
    hidden = None
    for number in range(parts):
        first, last = slot_cuts[number], slot_cuts[number + 1]
        slots = last - first
        known = [] if hidden is None else [hidden]
        hidden, state = pl.pallas_call(
            functools.partial(stage_kernel, number, first),
            out_shape=(
                jax.ShapeDtypeStruct((token_count, channels), jnp.bfloat16),
                jax.ShapeDtypeStruct(state.shape, jnp.float32),
            ),
            in_specs=[smem] + [vmem] * (5 + number) + [anywhere] * len(known),
            out_specs=(anywhere, vmem),
            scratch_shapes=[
                pltpu.VMEM((owners * cuts[number + 1], row_width), jnp.float32),
                pltpu.VMEM((bag_width, slots, row_width), jnp.float32),
                pltpu.VMEM((slots + 16, channels), jnp.float32),
                pltpu.VMEM((slots + 16, channels), jnp.float32),
                pltpu.VMEM((slots, channels), jnp.bfloat16),
                pltpu.SemaphoreType.DMA,
            ],
            input_output_aliases={6 + number: 0} if known else {},
            compiler_params=pltpu.CompilerParams(vmem_limit_bytes=32 * megabyte),
            cost_estimate=pl.CostEstimate(
                flops=2 * slots * 3 * channels * channels * conv_weight.shape[0],
                bytes_accessed=24 * megabyte,
                transcendentals=0,
            ),
            name="stage",
        )(place, weight_by_slot, state, filters, norm_gain, *returned[: number + 1], *known)
    return hidden.reshape(samples_here, slot_count, channels)


def solution(mesh):
    in_specs = (
        P(("table", "rep"), None, None),
        P(("table", "rep"), None, None),
        P(("table", "rep"), None, None),
        P(None, "table", None),
        P(("table", "rep")),
        P(("table", "rep")),
        P(("table", "rep")),
        P(("table", "rep"), None, None),
        P(None, "table", None),
        P(),
    )
    out_specs = P(("table", "rep"), None, None)
    return jax.shard_map(local, mesh=mesh, in_specs=in_specs, out_specs=out_specs, check_vma=False)
```

```python
import functools
import jax
import jax.numpy as jnp
from jax import lax
from jax.experimental import pallas as pl
from jax.experimental.pallas import tpu as pltpu
from jax.sharding import PartitionSpec as P

table_of_id = (0, 1, 2, 2, 3, 3, 3, 3)
bag_bounds = ((0, 1), (1, 2), (2, 4), (4, 8))
epsilon = 1e-05
part_ends = (0.25, 2 / 3, 1.0)
stage_parts = (2, 3)
megabyte = 1024 * 1024


def prep_kernel(cuts, shard_rows, rows_ref, owner_ref, request_ref, place_ref):
    owner = owner_ref[...]
    rows = rows_ref[...]
    owners = request_ref.shape[0]
    width, slots = owner.shape
    value_bits = (len(bag_bounds) * shard_rows).bit_length()
    owner_ids = lax.broadcasted_iota(jnp.int32, (owners, slots), 0)
    lane = lax.broadcasted_iota(jnp.int32, (owners, slots), 1)
    value = jnp.zeros((owners, slots), jnp.int32)
    for k in range(width):
        named = owner[k : k + 1, :] == owner_ids
        value = jnp.where(named, rows[k : k + 1, :] + (table_of_id[k] * shard_rows + 1), value)
    present = jnp.where(value > 0, 1, 0)
    rank = present
    step = 1
    while step < slots:
        rank = rank + jnp.where(lane >= step, pltpu.roll(rank, step, 1), 0)
        step *= 2
    rank = rank - present
    place = jnp.zeros((width, slots), jnp.int32)
    for number in range(owners):
        place = jnp.where(owner == number, rank[number : number + 1, :], place)
    landing = jnp.zeros((width, slots), jnp.int32)
    for start, stop in zip(cuts[:-1], cuts[1:]):
        where = owners * start + owner * (stop - start) + place - start
        landing = jnp.where(place >= start, where, landing)
    place_ref[...] = landing
    packed = jnp.where(value > 0, ((lane - rank) << value_bits) + value, 0)
    step = 1
    level = value_bits
    while step < slots:
        moving = jnp.where(((packed >> level) & 1) == 1, packed, 0)
        packed = (packed - moving) + pltpu.roll(moving, slots - step, 1)
        step *= 2
        level += 1
    value = jnp.maximum((packed & ((1 << value_bits) - 1)) - 1, 0)
    for number in range(owners):
        request_ref[number] = value[number : number + 1, : request_ref.shape[2]]


def pass_kernel(*refs):
    pass


def tie(array, *others):
    anywhere = pl.BlockSpec(memory_space=pl.ANY)
    return pl.pallas_call(
        pass_kernel,
        out_shape=jax.ShapeDtypeStruct(array.shape, array.dtype),
        in_specs=[anywhere] * (1 + len(others)),
        out_specs=anywhere,
        input_output_aliases={0: 0},
        name="tie",
    )(array, *others)


def gather_kernel(capacity, first, index_ref, table_ref, *refs):
    out_ref, narrow, wide, picked, packed, index, index_sem, table_sems, out_sems = refs[-9:]
    owners, piece, _ = out_ref.shape
    unroll = 32 if piece % 32 == 0 else 16
    blocks = table_sems.shape[0]
    block_rows = table_ref.shape[0] // blocks
    table_copies = []
    for block in range(blocks):
        part = pl.ds(block * block_rows, block_rows)
        copy = pltpu.make_async_copy(table_ref.at[part, :], narrow.at[part, :], table_sems.at[block])
        copy.start()
        table_copies.append(copy)
    index_copy = pltpu.make_async_copy(index_ref, index, index_sem)
    index_copy.start()
    rows = 256

    for block in range(blocks):
        table_copies[block].wait()

        def widen(step, carry, block=block):
            base = pl.multiple_of(block * block_rows + step * rows, rows)
            wide[pl.ds(base, rows), :] = narrow[pl.ds(base, rows), :].astype(jnp.float32)
            return carry

        lax.fori_loop(0, block_rows // rows, widen, 0)
    index_copy.wait()
    copies = []
    for number in range(owners):
        origin = number * capacity + first

        def some_rows(block, carry, origin=origin):
            base = pl.multiple_of(block * unroll, unroll)
            picks = [index[origin + base + i] for i in range(unroll)]
            found = [wide[pl.ds(pick, 1), :] for pick in picks]
            for i in range(unroll):
                picked[pl.ds(base + i, 1), :] = found[i]
            return carry

        lax.fori_loop(0, piece // unroll, some_rows, 0)
        packed[number] = picked[...].astype(jnp.bfloat16)
        copy = pltpu.make_async_copy(packed.at[number], out_ref.at[number], out_sems.at[number])
        copy.start()
        copies.append(copy)
    for copy in copies:
        copy.wait()


def stage_kernel(
    pieces, first, aliased, place_ref, weight_ref, carried_ref, gain_ref, filter_ref, *refs
):
    piece_refs = refs[:pieces]
    refs = refs[pieces + aliased :]
    out_ref, state_ref, table, picked, filters, first_buf, second_buf, result = refs[:8]
    filter_sems, out_sems = refs[8:]
    width, slots, lanes = picked.shape
    layers = filter_ref.shape[0]
    filter_copies = []
    for layer in range(layers):
        copy = pltpu.make_async_copy(filter_ref.at[layer], filters.at[layer], filter_sems.at[layer])
        copy.start()
        filter_copies.append(copy)
    start = 0
    for piece_ref in piece_refs:
        count = piece_ref.shape[0]
        rows = 256

        def widen(step, carry, piece_ref=piece_ref, start=start):
            base = pl.multiple_of(step * rows, rows)
            table[pl.ds(start + base, rows), :] = piece_ref[pl.ds(base, rows), :].astype(jnp.float32)
            return carry

        lax.fori_loop(0, count // rows, widen, 0)
        start += count

    def some_slots(step, carry):
        base = pl.multiple_of(step * 8, 8)
        for k in range(width):
            picks = [place_ref[k, first + base + i] for i in range(8)]
            rows = [table[pl.ds(pick, 1), :] for pick in picks]
            for i in range(8):
                picked[k, pl.ds(base + i, 1), :] = rows[i]
        return carry

    lax.fori_loop(0, slots // 8, some_slots, 0)
    front = 16
    weights = jnp.transpose(weight_ref[:, first : first + slots])
    for t, (lower, upper) in enumerate(bag_bounds):
        total = picked[lower] * weights[:, lower : lower + 1]
        for k in range(lower + 1, upper):
            total = total + picked[k] * weights[:, k : k + 1]
        total = total.astype(jnp.bfloat16).astype(jnp.float32)
        first_buf[front:, t * lanes : (t + 1) * lanes] = total

    offset = 0
    out_copies = []
    for layer in range(layers):
        dilation = 2**layer
        span = 2 * dilation
        source, target = (first_buf, second_buf) if layer % 2 == 0 else (second_buf, first_buf)
        source[front - span : front, :] = carried_ref[offset : offset + span, :]
        state_ref[offset : offset + span, :] = source[front + slots - span : front + slots, :]
        offset += span
        filter_copies[layer].wait()
        for begin in range(0, slots, 256):
            rows = min(256, slots - begin)
            base = front + begin
            taps = [
                source[base - tap * dilation : base - tap * dilation + rows, :].astype(jnp.bfloat16)
                for tap in range(3)
            ]
            output = jnp.dot(
                jnp.concatenate(taps, axis=1), filters[layer], preferred_element_type=jnp.float32
            )
            mean = jnp.mean(output, axis=-1, keepdims=True)
            centred = output - mean
            spread = jnp.mean(centred * centred, axis=-1, keepdims=True)
            active = jnp.maximum(
                centred * lax.rsqrt(spread + epsilon) * gain_ref[layer : layer + 1, :], 0.0
            )
            if layer % 2 == 1:
                active = active + target[base : base + rows, :]
            active = active.astype(jnp.bfloat16)
            if layer == layers - 1:
                result[begin : begin + rows, :] = active
                copy = pltpu.make_async_copy(
                    result.at[pl.ds(begin, rows), :],
                    out_ref.at[pl.ds(first + begin, rows), :],
                    out_sems.at[len(out_copies)],
                )
                copy.start()
                out_copies.append(copy)
            else:
                target[base : base + rows, :] = active.astype(jnp.float32)
    for copy in out_copies:
        copy.wait()


def gather_filters(conv_weight, after_first, after_second):
    owners = lax.axis_size("table")
    copies = lax.axis_size("rep")
    layers, depth, channels = conv_weight.shape
    if owners % 2 or copies % 2 or layers % 2:
        return lax.all_gather(conv_weight, "table", axis=1, tiled=True)
    half = layers // 2
    parity = lax.axis_index("table") % 2
    side = lax.axis_index("rep") % 2
    groups = [list(range(start, owners, 2)) for start in range(2)]
    mine = lax.dynamic_slice_in_dim(conv_weight, side * half, half, 0)
    mine = lax.all_gather(mine, "table", axis_index_groups=groups, axis=0, tiled=False)
    mine = tie(mine, after_first)
    other = lax.ppermute(mine, "rep", [(r, r ^ 1) for r in range(copies)])
    low = jnp.where(side == 0, mine, other)
    high = jnp.where(side == 0, other, mine)
    own = jnp.concatenate([low, high], axis=1)
    own = tie(own, after_second)
    partner = lax.ppermute(own, "table", [(i, i ^ 1) for i in range(owners)])
    even = jnp.where(parity == 0, own, partner)
    odd = jnp.where(parity == 0, partner, own)
    both = jnp.stack([even, odd], axis=1)
    return jnp.transpose(both, (2, 0, 1, 3, 4)).reshape(layers, owners * depth, channels)


def local(
    bag_rows, bag_owner, bag_weight, tables, returning, home, entry, stores, conv_weight, norm_gain
):
    owners = lax.axis_size("table")
    copies = lax.axis_size("rep")
    samples_here, slot_count, bag_width = bag_rows.shape
    token_count = samples_here * slot_count
    shard_rows = tables.shape[1]
    row_width = tables.shape[2]
    channels = conv_weight.shape[-1]
    capacity = min(token_count, (3 * token_count * bag_width + 2 * owners - 1) // (2 * owners))
    cuts = [0] + [round(capacity * end) // 16 * 16 for end in part_ends]
    slot_cuts = [0] + [cuts[part] for part in stage_parts[:-1]] + [token_count]
    smem = pl.BlockSpec(memory_space=pltpu.SMEM)
    vmem = pl.BlockSpec(memory_space=pltpu.VMEM)
    anywhere = pl.BlockSpec(memory_space=pl.ANY)

    rows_by_slot = bag_rows.reshape(token_count, bag_width).T
    owner_by_slot = bag_owner.reshape(token_count, bag_width).T
    requests, place = pl.pallas_call(
        functools.partial(prep_kernel, cuts, shard_rows),
        out_shape=(
            jax.ShapeDtypeStruct((owners, 1, capacity), jnp.int32),
            jax.ShapeDtypeStruct((bag_width, token_count), jnp.int32),
        ),
        in_specs=[vmem, vmem],
        out_specs=(vmem, vmem),
        compiler_params=pltpu.CompilerParams(vmem_limit_bytes=8 * megabyte),
        name="prep",
    )(rows_by_slot, owner_by_slot)
    received = lax.all_to_all(requests, "table", split_axis=0, concat_axis=0, tiled=True)
    received = received.reshape(owners * capacity)
    flat_table = tables.reshape(-1, row_width)
    returned = []
    sent = []
    for number in range(len(part_ends)):
        piece = cuts[number + 1] - cuts[number]
        sent.append(
            pl.pallas_call(
                functools.partial(gather_kernel, capacity, cuts[number]),
                out_shape=jax.ShapeDtypeStruct((owners, piece, row_width), jnp.bfloat16),
                in_specs=[anywhere] * (2 + len(sent[-1:])),
                out_specs=anywhere,
                scratch_shapes=[
                    pltpu.VMEM(flat_table.shape, jnp.bfloat16),
                    pltpu.VMEM(flat_table.shape, jnp.float32),
                    pltpu.VMEM((piece, row_width), jnp.float32),
                    pltpu.VMEM((owners, piece, row_width), jnp.bfloat16),
                    pltpu.SMEM((owners * capacity,), jnp.int32),
                    pltpu.SemaphoreType.DMA,
                    pltpu.SemaphoreType.DMA((8,)),
                    pltpu.SemaphoreType.DMA((owners,)),
                ],
                compiler_params=pltpu.CompilerParams(vmem_limit_bytes=58 * megabyte),
                cost_estimate=pl.CostEstimate(
                    flops=0, bytes_accessed=20 * megabyte, transcendentals=0
                ),
                name="owner_gather",
            )(received, flat_table, *sent[-1:])
        )
        arrived = lax.all_to_all(sent[-1], "table", split_axis=0, concat_axis=0, tiled=True)
        returned.append(arrived.reshape(owners * piece, row_width))
    filters = gather_filters(conv_weight, returned[0], returned[1])

    me = lax.axis_index("rep")
    carried = jnp.zeros(stores.shape[1:], stores.dtype)
    for shift in range(copies):
        arrived = stores
        if shift:
            pairs = [(source, (source + shift) % copies) for source in range(copies)]
            arrived = lax.ppermute(tie(stores, sent[0]), "rep", pairs)
        wanted = (returning[0] > 0) & (home[0] == (me + copies - shift) % copies)
        chosen = lax.dynamic_index_in_dim(arrived, entry[0], 0, keepdims=False)
        carried = jnp.where(wanted, chosen, carried)

    state = carried.astype(jnp.float32)
    weight_by_slot = bag_weight.reshape(token_count, bag_width).T
    hidden = None
    for number, part in enumerate(stage_parts):
        first, last = slot_cuts[number], slot_cuts[number + 1]
        slots = last - first
        known = [] if hidden is None else [hidden]
        pieces = returned[:part]
        hidden, state = pl.pallas_call(
            functools.partial(stage_kernel, part, first, len(known)),
            out_shape=(
                jax.ShapeDtypeStruct((token_count, channels), jnp.bfloat16),
                jax.ShapeDtypeStruct(state.shape, jnp.float32),
            ),
            in_specs=[smem] + [vmem] * 3 + [anywhere] + [vmem] * part + [anywhere] * len(known),
            out_specs=(anywhere, vmem),
            scratch_shapes=[
                pltpu.VMEM((owners * cuts[part], row_width), jnp.float32),
                pltpu.VMEM((bag_width, slots, row_width), jnp.float32),
                pltpu.VMEM(filters.shape, filters.dtype),
                pltpu.VMEM((slots + 16, channels), jnp.float32),
                pltpu.VMEM((slots + 16, channels), jnp.float32),
                pltpu.VMEM((slots, channels), jnp.bfloat16),
                pltpu.SemaphoreType.DMA((filters.shape[0],)),
                pltpu.SemaphoreType.DMA(((slots + 255) // 256,)),
            ],
            input_output_aliases={5 + part: 0} if known else {},
            compiler_params=pltpu.CompilerParams(vmem_limit_bytes=56 * megabyte),
            cost_estimate=pl.CostEstimate(
                flops=2 * slots * 3 * channels * channels * conv_weight.shape[0],
                bytes_accessed=24 * megabyte,
                transcendentals=0,
            ),
            name="stage",
        )(place, weight_by_slot, state, norm_gain, filters, *pieces, *known)
    return hidden.reshape(samples_here, slot_count, channels)


def solution(mesh):
    in_specs = (
        P(("table", "rep"), None, None),
        P(("table", "rep"), None, None),
        P(("table", "rep"), None, None),
        P(None, "table", None),
        P(("table", "rep")),
        P(("table", "rep")),
        P(("table", "rep")),
        P(("table", "rep"), None, None),
        P(None, "table", None),
        P(),
    )
    out_specs = P(("table", "rep"), None, None)
    return jax.shard_map(local, mesh=mesh, in_specs=in_specs, out_specs=out_specs, check_vma=False)
```

```python
import functools
import jax
import jax.numpy as jnp
from jax import lax
from jax.experimental import pallas as pl
from jax.experimental.pallas import tpu as pltpu
from jax.sharding import PartitionSpec as P

table_of_id = (0, 1, 2, 2, 3, 3, 3, 3)
bag_bounds = ((0, 1), (1, 2), (2, 4), (4, 8))
epsilon = 1e-05
part_ends = (0.25, 2 / 3, 1.0)
stage_parts = (2, 3)
megabyte = 1024 * 1024


def prep_kernel(cuts, shard_rows, rows_ref, owner_ref, request_ref, place_ref):
    owner = owner_ref[...]
    rows = rows_ref[...]
    owners = request_ref.shape[0]
    width, slots = owner.shape
    value_bits = (len(bag_bounds) * shard_rows).bit_length()
    owner_ids = lax.broadcasted_iota(jnp.int32, (owners, slots), 0)
    lane = lax.broadcasted_iota(jnp.int32, (owners, slots), 1)
    value = jnp.zeros((owners, slots), jnp.int32)
    for k in range(width):
        named = owner[k : k + 1, :] == owner_ids
        value = jnp.where(named, rows[k : k + 1, :] + (table_of_id[k] * shard_rows + 1), value)
    present = jnp.where(value > 0, 1, 0)
    rank = present
    step = 1
    while step < slots:
        rank = rank + jnp.where(lane >= step, pltpu.roll(rank, step, 1), 0)
        step *= 2
    rank = rank - present
    place = jnp.zeros((width, slots), jnp.int32)
    for number in range(owners):
        place = jnp.where(owner == number, rank[number : number + 1, :], place)
    landing = jnp.zeros((width, slots), jnp.int32)
    for start, stop in zip(cuts[:-1], cuts[1:]):
        where = owners * start + owner * (stop - start) + place - start
        landing = jnp.where(place >= start, where, landing)
    place_ref[...] = landing
    packed = jnp.where(value > 0, ((lane - rank) << value_bits) + value, 0)
    step = 1
    level = value_bits
    while step < slots:
        moving = jnp.where(((packed >> level) & 1) == 1, packed, 0)
        packed = (packed - moving) + pltpu.roll(moving, slots - step, 1)
        step *= 2
        level += 1
    value = jnp.maximum((packed & ((1 << value_bits) - 1)) - 1, 0)
    for number in range(owners):
        request_ref[number] = value[number : number + 1, : request_ref.shape[2]]


def pass_kernel(*refs):
    pass


def tie(array, *others):
    anywhere = pl.BlockSpec(memory_space=pl.ANY)
    return pl.pallas_call(
        pass_kernel,
        out_shape=jax.ShapeDtypeStruct(array.shape, array.dtype),
        in_specs=[anywhere] * (1 + len(others)),
        out_specs=anywhere,
        input_output_aliases={0: 0},
        name="tie",
    )(array, *others)


def gather_kernel(capacity, first, index_ref, table_ref, *refs):
    out_ref, narrow, wide, picked, packed, index, index_sem, table_sems, out_sems = refs[-9:]
    owners, piece, _ = out_ref.shape
    unroll = 32 if piece % 32 == 0 else 16
    blocks = table_sems.shape[0]
    block_rows = table_ref.shape[0] // blocks
    table_copies = []
    for block in range(blocks):
        part = pl.ds(block * block_rows, block_rows)
        copy = pltpu.make_async_copy(table_ref.at[part, :], narrow.at[part, :], table_sems.at[block])
        copy.start()
        table_copies.append(copy)
    index_copy = pltpu.make_async_copy(index_ref, index, index_sem)
    index_copy.start()
    rows = 256

    for block in range(blocks):
        table_copies[block].wait()

        def widen(step, carry, block=block):
            base = pl.multiple_of(block * block_rows + step * rows, rows)
            wide[pl.ds(base, rows), :] = narrow[pl.ds(base, rows), :].astype(jnp.float32)
            return carry

        lax.fori_loop(0, block_rows // rows, widen, 0)
    index_copy.wait()
    copies = []
    for number in range(owners):
        origin = number * capacity + first

        def some_rows(block, carry, origin=origin):
            base = pl.multiple_of(block * unroll, unroll)
            picks = [index[origin + base + i] for i in range(unroll)]
            found = [wide[pl.ds(pick, 1), :] for pick in picks]
            for i in range(unroll):
                picked[pl.ds(base + i, 1), :] = found[i]
            return carry

        lax.fori_loop(0, piece // unroll, some_rows, 0)
        packed[number] = picked[...].astype(jnp.bfloat16)
        copy = pltpu.make_async_copy(packed.at[number], out_ref.at[number], out_sems.at[number])
        copy.start()
        copies.append(copy)
    for copy in copies:
        copy.wait()


def stage_kernel(
    pieces, first, aliased, place_ref, weight_ref, carried_ref, gain_ref, filter_ref, *refs
):
    piece_refs = refs[:pieces]
    refs = refs[pieces + aliased :]
    out_ref, state_ref, table, picked, filters, first_buf, second_buf, result = refs[:8]
    filter_sems, out_sems = refs[8:]
    width, slots, lanes = picked.shape
    halves, layers, depth, _ = filter_ref.shape
    filter_copies = []
    for layer in range(layers):
        for half in range(halves):
            copy = pltpu.make_async_copy(
                filter_ref.at[half, layer],
                filters.at[layer, pl.ds(half * depth, depth), :],
                filter_sems.at[layer, half],
            )
            copy.start()
            filter_copies.append(copy)
    start = 0
    for piece_ref in piece_refs:
        count = piece_ref.shape[0]
        rows = 256

        def widen(step, carry, piece_ref=piece_ref, start=start):
            base = pl.multiple_of(step * rows, rows)
            table[pl.ds(start + base, rows), :] = piece_ref[pl.ds(base, rows), :].astype(jnp.float32)
            return carry

        lax.fori_loop(0, count // rows, widen, 0)
        start += count

    def some_slots(step, carry):
        base = pl.multiple_of(step * 8, 8)
        for k in range(width):
            picks = [place_ref[k, first + base + i] for i in range(8)]
            rows = [table[pl.ds(pick, 1), :] for pick in picks]
            for i in range(8):
                picked[k, pl.ds(base + i, 1), :] = rows[i]
        return carry

    lax.fori_loop(0, slots // 8, some_slots, 0)
    front = 16
    weights = jnp.transpose(weight_ref[:, first : first + slots])
    for t, (lower, upper) in enumerate(bag_bounds):
        total = picked[lower] * weights[:, lower : lower + 1]
        for k in range(lower + 1, upper):
            total = total + picked[k] * weights[:, k : k + 1]
        total = total.astype(jnp.bfloat16).astype(jnp.float32)
        first_buf[front:, t * lanes : (t + 1) * lanes] = total

    offset = 0
    out_copies = []
    for layer in range(layers):
        dilation = 2**layer
        span = 2 * dilation
        source, target = (first_buf, second_buf) if layer % 2 == 0 else (second_buf, first_buf)
        source[front - span : front, :] = carried_ref[offset : offset + span, :]
        state_ref[offset : offset + span, :] = source[front + slots - span : front + slots, :]
        offset += span
        for half in range(halves):
            filter_copies[layer * halves + half].wait()
        for begin in range(0, slots, 256):
            rows = min(256, slots - begin)
            base = front + begin
            taps = [
                source[base - tap * dilation : base - tap * dilation + rows, :].astype(jnp.bfloat16)
                for tap in range(3)
            ]
            output = jnp.dot(
                jnp.concatenate(taps, axis=1), filters[layer], preferred_element_type=jnp.float32
            )
            mean = jnp.mean(output, axis=-1, keepdims=True)
            centred = output - mean
            spread = jnp.mean(centred * centred, axis=-1, keepdims=True)
            active = jnp.maximum(
                centred * lax.rsqrt(spread + epsilon) * gain_ref[layer : layer + 1, :], 0.0
            )
            if layer % 2 == 1:
                active = active + target[base : base + rows, :]
            active = active.astype(jnp.bfloat16)
            if layer == layers - 1:
                result[begin : begin + rows, :] = active
                copy = pltpu.make_async_copy(
                    result.at[pl.ds(begin, rows), :],
                    out_ref.at[pl.ds(first + begin, rows), :],
                    out_sems.at[len(out_copies)],
                )
                copy.start()
                out_copies.append(copy)
            else:
                target[base : base + rows, :] = active.astype(jnp.float32)
    for copy in out_copies:
        copy.wait()


def near_half(conv_weight, far, after):
    owners = lax.axis_size("table")
    half = owners // 2
    far = tie(far, after)
    in_low = lax.axis_index("table") < half
    low = jnp.where(in_low, conv_weight, far)
    high = jnp.where(in_low, far, conv_weight)
    groups = [
        [start + parity + step for step in range(0, half, 2)]
        for start in (0, half)
        for parity in (0, 1)
    ]
    both = jnp.stack([low, high], axis=0)
    return both, lax.all_gather(both, "table", axis_index_groups=groups, axis=2, tiled=False)


def all_filters(own, after):
    owners = lax.axis_size("table")
    own = tie(own, after)
    partner = lax.ppermute(own, "table", [(i, i ^ 1) for i in range(owners)])
    is_even = lax.axis_index("table") % 2 == 0
    even = jnp.where(is_even, own, partner)
    odd = jnp.where(is_even, partner, own)
    halves, layers, _, _, channels = own.shape
    return jnp.stack([even, odd], axis=3).reshape(halves, layers, -1, channels)


def carried_rows(returning, home, entry, stores, after):
    copies = lax.axis_size("rep")
    me = lax.axis_index("rep")
    carried = jnp.zeros(stores.shape[1:], stores.dtype)
    for shift in range(copies):
        arrived = stores
        if shift:
            pairs = [(source, (source + shift) % copies) for source in range(copies)]
            arrived = lax.ppermute(tie(stores, after), "rep", pairs)
        wanted = (returning[0] > 0) & (home[0] == (me + copies - shift) % copies)
        chosen = lax.dynamic_index_in_dim(arrived, entry[0], 0, keepdims=False)
        carried = jnp.where(wanted, chosen, carried)

    return carried.astype(jnp.float32)


def local(
    bag_rows, bag_owner, bag_weight, tables, returning, home, entry, stores, conv_weight, norm_gain
):
    owners = lax.axis_size("table")
    samples_here, slot_count, bag_width = bag_rows.shape
    token_count = samples_here * slot_count
    shard_rows = tables.shape[1]
    row_width = tables.shape[2]
    channels = conv_weight.shape[-1]
    capacity = min(token_count, (3 * token_count * bag_width + 2 * owners - 1) // (2 * owners))
    cuts = [0] + [round(capacity * end) // 16 * 16 for end in part_ends]
    slot_cuts = [0] + [cuts[part] for part in stage_parts[:-1]] + [token_count]
    smem = pl.BlockSpec(memory_space=pltpu.SMEM)
    vmem = pl.BlockSpec(memory_space=pltpu.VMEM)
    anywhere = pl.BlockSpec(memory_space=pl.ANY)

    half = owners // 2
    across = [(source, source ^ half) for source in range(owners)]
    far_filters = lax.ppermute(conv_weight, "table", across)

    rows_by_slot = bag_rows.reshape(token_count, bag_width).T
    owner_by_slot = bag_owner.reshape(token_count, bag_width).T
    requests, place = pl.pallas_call(
        functools.partial(prep_kernel, cuts, shard_rows),
        out_shape=(
            jax.ShapeDtypeStruct((owners, 1, capacity), jnp.int32),
            jax.ShapeDtypeStruct((bag_width, token_count), jnp.int32),
        ),
        in_specs=[vmem, vmem],
        out_specs=(vmem, vmem),
        compiler_params=pltpu.CompilerParams(vmem_limit_bytes=8 * megabyte),
        name="prep",
    )(rows_by_slot, owner_by_slot)
    received = lax.all_to_all(requests, "table", split_axis=0, concat_axis=0, tiled=True)
    received = received.reshape(owners * capacity)
    both_filters, own_filters = near_half(conv_weight, far_filters, received)
    flat_table = tables.reshape(-1, row_width)
    returned = []
    sent = []
    for number in range(len(part_ends)):
        piece = cuts[number + 1] - cuts[number]
        earlier = sent[-1:] if sent else [both_filters]
        if number == 1:
            state = carried_rows(returning, home, entry, stores, sent[0])
        if number == 2:
            earlier = earlier + [state]
        sent.append(
            pl.pallas_call(
                functools.partial(gather_kernel, capacity, cuts[number]),
                out_shape=jax.ShapeDtypeStruct((owners, piece, row_width), jnp.bfloat16),
                in_specs=[anywhere] * (2 + len(earlier)),
                out_specs=anywhere,
                scratch_shapes=[
                    pltpu.VMEM(flat_table.shape, jnp.bfloat16),
                    pltpu.VMEM(flat_table.shape, jnp.float32),
                    pltpu.VMEM((piece, row_width), jnp.float32),
                    pltpu.VMEM((owners, piece, row_width), jnp.bfloat16),
                    pltpu.SMEM((owners * capacity,), jnp.int32),
                    pltpu.SemaphoreType.DMA,
                    pltpu.SemaphoreType.DMA((8,)),
                    pltpu.SemaphoreType.DMA((owners,)),
                ],
                compiler_params=pltpu.CompilerParams(vmem_limit_bytes=58 * megabyte),
                cost_estimate=pl.CostEstimate(
                    flops=0, bytes_accessed=20 * megabyte, transcendentals=0
                ),
                name="owner_gather",
            )(received, flat_table, *earlier)
        )
        if returned:
            sent[-1] = tie(sent[-1], returned[-1])
        arrived = lax.all_to_all(sent[-1], "table", split_axis=0, concat_axis=0, tiled=True)
        returned.append(arrived.reshape(owners * piece, row_width))
    filters = all_filters(own_filters, returned[1])

    weight_by_slot = bag_weight.reshape(token_count, bag_width).T
    hidden = None
    for number, part in enumerate(stage_parts):
        first, last = slot_cuts[number], slot_cuts[number + 1]
        slots = last - first
        known = [] if hidden is None else [hidden]
        pieces = returned[:part]
        hidden, state = pl.pallas_call(
            functools.partial(stage_kernel, part, first, len(known)),
            out_shape=(
                jax.ShapeDtypeStruct((token_count, channels), jnp.bfloat16),
                jax.ShapeDtypeStruct(state.shape, jnp.float32),
            ),
            in_specs=[smem] + [vmem] * 3 + [anywhere] + [vmem] * part + [anywhere] * len(known),
            out_specs=(anywhere, vmem),
            scratch_shapes=[
                pltpu.VMEM((owners * cuts[part], row_width), jnp.float32),
                pltpu.VMEM((bag_width, slots, row_width), jnp.float32),
                pltpu.VMEM((filters.shape[1], 3 * channels, channels), filters.dtype),
                pltpu.VMEM((slots + 16, channels), jnp.float32),
                pltpu.VMEM((slots + 16, channels), jnp.float32),
                pltpu.VMEM((slots, channels), jnp.bfloat16),
                pltpu.SemaphoreType.DMA(filters.shape[1::-1]),
                pltpu.SemaphoreType.DMA(((slots + 255) // 256,)),
            ],
            input_output_aliases={5 + part: 0} if known else {},
            compiler_params=pltpu.CompilerParams(vmem_limit_bytes=56 * megabyte),
            cost_estimate=pl.CostEstimate(
                flops=2 * slots * 3 * channels * channels * conv_weight.shape[0],
                bytes_accessed=24 * megabyte,
                transcendentals=0,
            ),
            name="stage",
        )(place, weight_by_slot, state, norm_gain, filters, *pieces, *known)
    return hidden.reshape(samples_here, slot_count, channels)


def solution(mesh):
    in_specs = (
        P(("table", "rep"), None, None),
        P(("table", "rep"), None, None),
        P(("table", "rep"), None, None),
        P(None, "table", None),
        P(("table", "rep")),
        P(("table", "rep")),
        P(("table", "rep")),
        P(("table", "rep"), None, None),
        P(None, "table", None),
        P(),
    )
    out_specs = P(("table", "rep"), None, None)
    return jax.shard_map(local, mesh=mesh, in_specs=in_specs, out_specs=out_specs, check_vma=False)
```

```python
import functools
import jax
import jax.numpy as jnp
from jax import lax
from jax.experimental import pallas as pl
from jax.experimental.pallas import tpu as pltpu
from jax.sharding import PartitionSpec as P

table_of_id = (0, 1, 2, 2, 3, 3, 3, 3)
bag_bounds = ((0, 1), (1, 2), (2, 4), (4, 8))
epsilon = 1e-05
part_ends = (0.25, 2 / 3, 1.0)
stage_parts = (2, 3)
megabyte = 1024 * 1024


def prep_kernel(cuts, shard_rows, rows_ref, owner_ref, request_ref, place_ref):
    owner = owner_ref[...]
    rows = rows_ref[...]
    owners = request_ref.shape[0]
    width, slots = owner.shape
    value_bits = (len(bag_bounds) * shard_rows).bit_length()
    owner_ids = lax.broadcasted_iota(jnp.int32, (owners, slots), 0)
    lane = lax.broadcasted_iota(jnp.int32, (owners, slots), 1)
    value = jnp.zeros((owners, slots), jnp.int32)
    for k in range(width):
        named = owner[k : k + 1, :] == owner_ids
        value = jnp.where(named, rows[k : k + 1, :] + (table_of_id[k] * shard_rows + 1), value)
    present = jnp.where(value > 0, 1, 0)
    rank = present
    step = 1
    while step < slots:
        rank = rank + jnp.where(lane >= step, pltpu.roll(rank, step, 1), 0)
        step *= 2
    rank = rank - present
    place = jnp.zeros((width, slots), jnp.int32)
    for number in range(owners):
        place = jnp.where(owner == number, rank[number : number + 1, :], place)
    landing = jnp.zeros((width, slots), jnp.int32)
    for start, stop in zip(cuts[:-1], cuts[1:]):
        where = owners * start + owner * (stop - start) + place - start
        landing = jnp.where(place >= start, where, landing)
    place_ref[...] = landing
    packed = jnp.where(value > 0, ((lane - rank) << value_bits) + value, 0)
    step = 1
    level = value_bits
    while step < slots:
        moving = jnp.where(((packed >> level) & 1) == 1, packed, 0)
        packed = (packed - moving) + pltpu.roll(moving, slots - step, 1)
        step *= 2
        level += 1
    value = jnp.maximum((packed & ((1 << value_bits) - 1)) - 1, 0)
    for number in range(owners):
        request_ref[number] = value[number : number + 1, : request_ref.shape[2]]


def pass_kernel(*refs):
    pass


def tie(array, *others):
    anywhere = pl.BlockSpec(memory_space=pl.ANY)
    return pl.pallas_call(
        pass_kernel,
        out_shape=jax.ShapeDtypeStruct(array.shape, array.dtype),
        in_specs=[anywhere] * (1 + len(others)),
        out_specs=anywhere,
        input_output_aliases={0: 0},
        name="tie",
    )(array, *others)


def gather_kernel(capacity, first, index_ref, table_ref, *refs):
    out_ref, narrow, wide, picked, packed, index, index_sem, table_sems, out_sems = refs[-9:]
    owners, piece, _ = out_ref.shape
    unroll = 32 if piece % 32 == 0 else 16
    blocks = table_sems.shape[0]
    block_rows = table_ref.shape[0] // blocks
    table_copies = []
    for block in range(blocks):
        part = pl.ds(block * block_rows, block_rows)
        copy = pltpu.make_async_copy(table_ref.at[part, :], narrow.at[part, :], table_sems.at[block])
        copy.start()
        table_copies.append(copy)
    index_copy = pltpu.make_async_copy(index_ref, index, index_sem)
    index_copy.start()
    rows = 256

    for block in range(blocks):
        table_copies[block].wait()

        def widen(step, carry, block=block):
            base = pl.multiple_of(block * block_rows + step * rows, rows)
            wide[pl.ds(base, rows), :] = narrow[pl.ds(base, rows), :].astype(jnp.float32)
            return carry

        lax.fori_loop(0, block_rows // rows, widen, 0)
    index_copy.wait()
    copies = []
    for number in range(owners):
        origin = number * capacity + first

        def some_rows(block, carry, origin=origin):
            base = pl.multiple_of(block * unroll, unroll)
            picks = [index[origin + base + i] for i in range(unroll)]
            found = [wide[pl.ds(pick, 1), :] for pick in picks]
            for i in range(unroll):
                picked[pl.ds(base + i, 1), :] = found[i]
            return carry

        lax.fori_loop(0, piece // unroll, some_rows, 0)
        packed[number] = picked[...].astype(jnp.bfloat16)
        copy = pltpu.make_async_copy(packed.at[number], out_ref.at[number], out_sems.at[number])
        copy.start()
        copies.append(copy)
    for copy in copies:
        copy.wait()


def stage_kernel(
    pieces, first, aliased, place_ref, weight_ref, carried_ref, gain_ref, filter_ref, *refs
):
    piece_refs = refs[:pieces]
    refs = refs[pieces + aliased :]
    out_ref, state_ref, table, picked, filters, first_buf, second_buf, result = refs[:8]
    filter_sems, out_sems = refs[8:]
    width, slots, lanes = picked.shape
    layers = filter_ref.shape[0]
    filter_copies = []
    for layer in range(layers):
        copy = pltpu.make_async_copy(filter_ref.at[layer], filters.at[layer], filter_sems.at[layer])
        copy.start()
        filter_copies.append(copy)
    start = 0
    for piece_ref in piece_refs:
        count = piece_ref.shape[0]
        rows = 256

        def widen(step, carry, piece_ref=piece_ref, start=start):
            base = pl.multiple_of(step * rows, rows)
            table[pl.ds(start + base, rows), :] = piece_ref[pl.ds(base, rows), :].astype(jnp.float32)
            return carry

        lax.fori_loop(0, count // rows, widen, 0)
        start += count

    def some_slots(step, carry):
        base = pl.multiple_of(step * 8, 8)
        for k in range(width):
            picks = [place_ref[k, first + base + i] for i in range(8)]
            rows = [table[pl.ds(pick, 1), :] for pick in picks]
            for i in range(8):
                picked[k, pl.ds(base + i, 1), :] = rows[i]
        return carry

    lax.fori_loop(0, slots // 8, some_slots, 0)
    front = 16
    weights = jnp.transpose(weight_ref[:, first : first + slots])
    for t, (lower, upper) in enumerate(bag_bounds):
        total = picked[lower] * weights[:, lower : lower + 1]
        for k in range(lower + 1, upper):
            total = total + picked[k] * weights[:, k : k + 1]
        total = total.astype(jnp.bfloat16).astype(jnp.float32)
        first_buf[front:, t * lanes : (t + 1) * lanes] = total

    offset = 0
    out_copies = []
    for layer in range(layers):
        dilation = 2**layer
        span = 2 * dilation
        source, target = (first_buf, second_buf) if layer % 2 == 0 else (second_buf, first_buf)
        source[front - span : front, :] = carried_ref[offset : offset + span, :]
        state_ref[offset : offset + span, :] = source[front + slots - span : front + slots, :]
        offset += span
        filter_copies[layer].wait()
        for begin in range(0, slots, 256):
            rows = min(256, slots - begin)
            base = front + begin
            taps = [
                source[base - tap * dilation : base - tap * dilation + rows, :].astype(jnp.bfloat16)
                for tap in range(3)
            ]
            output = jnp.dot(
                jnp.concatenate(taps, axis=1), filters[layer], preferred_element_type=jnp.float32
            )
            mean = jnp.mean(output, axis=-1, keepdims=True)
            centred = output - mean
            spread = jnp.mean(centred * centred, axis=-1, keepdims=True)
            active = jnp.maximum(
                centred * lax.rsqrt(spread + epsilon) * gain_ref[layer : layer + 1, :], 0.0
            )
            if layer % 2 == 1:
                active = active + target[base : base + rows, :]
            active = active.astype(jnp.bfloat16)
            if layer == layers - 1:
                result[begin : begin + rows, :] = active
                copy = pltpu.make_async_copy(
                    result.at[pl.ds(begin, rows), :],
                    out_ref.at[pl.ds(first + begin, rows), :],
                    out_sems.at[len(out_copies)],
                )
                copy.start()
                out_copies.append(copy)
            else:
                target[base : base + rows, :] = active.astype(jnp.float32)
    for copy in out_copies:
        copy.wait()


def carried_rows(returning, home, entry, stores):
    copies = lax.axis_size("rep")
    me = lax.axis_index("rep")
    by_position = stores.transpose(1, 0, 2)
    positions, _, channels = by_position.shape
    carried = jnp.zeros((positions, channels), stores.dtype)
    for shift in range(copies):
        arrived = by_position
        if shift:
            pairs = [(source, (source + shift) % copies) for source in range(copies)]
            arrived = lax.ppermute(by_position, "rep", pairs)
        wanted = (returning[0] > 0) & (home[0] == (me + copies - shift) % copies)
        chosen = lax.dynamic_index_in_dim(arrived, entry[0], 1, keepdims=False)
        carried = jnp.where(wanted, chosen, carried)
    return carried.astype(jnp.float32)


def local(
    bag_rows, bag_owner, bag_weight, tables, returning, home, entry, stores, conv_weight, norm_gain
):
    owners = lax.axis_size("table")
    samples_here, slot_count, bag_width = bag_rows.shape
    token_count = samples_here * slot_count
    shard_rows = tables.shape[1]
    row_width = tables.shape[2]
    channels = conv_weight.shape[-1]
    capacity = min(token_count, (3 * token_count * bag_width + 2 * owners - 1) // (2 * owners))
    cuts = [0] + [round(capacity * end) // 16 * 16 for end in part_ends]
    slot_cuts = [0] + [cuts[part] for part in stage_parts[:-1]] + [token_count]
    smem = pl.BlockSpec(memory_space=pltpu.SMEM)
    vmem = pl.BlockSpec(memory_space=pltpu.VMEM)
    anywhere = pl.BlockSpec(memory_space=pl.ANY)

    filters = lax.all_gather(conv_weight, "table", axis=1, tiled=True)

    rows_by_slot = bag_rows.reshape(token_count, bag_width).T
    owner_by_slot = bag_owner.reshape(token_count, bag_width).T
    requests, place = pl.pallas_call(
        functools.partial(prep_kernel, cuts, shard_rows),
        out_shape=(
            jax.ShapeDtypeStruct((owners, 1, capacity), jnp.int32),
            jax.ShapeDtypeStruct((bag_width, token_count), jnp.int32),
        ),
        in_specs=[vmem, vmem],
        out_specs=(vmem, vmem),
        compiler_params=pltpu.CompilerParams(vmem_limit_bytes=8 * megabyte),
        name="prep",
    )(rows_by_slot, owner_by_slot)
    received = lax.all_to_all(requests, "table", split_axis=0, concat_axis=0, tiled=True)
    received = received.reshape(owners * capacity)
    flat_table = tables.reshape(-1, row_width)
    returned = []
    sent = []
    for number in range(len(part_ends)):
        piece = cuts[number + 1] - cuts[number]
        earlier = sent[-1:]
        sent.append(
            pl.pallas_call(
                functools.partial(gather_kernel, capacity, cuts[number]),
                out_shape=jax.ShapeDtypeStruct((owners, piece, row_width), jnp.bfloat16),
                in_specs=[anywhere] * (2 + len(earlier)),
                out_specs=anywhere,
                scratch_shapes=[
                    pltpu.VMEM(flat_table.shape, jnp.bfloat16),
                    pltpu.VMEM(flat_table.shape, jnp.float32),
                    pltpu.VMEM((piece, row_width), jnp.float32),
                    pltpu.VMEM((owners, piece, row_width), jnp.bfloat16),
                    pltpu.SMEM((owners * capacity,), jnp.int32),
                    pltpu.SemaphoreType.DMA,
                    pltpu.SemaphoreType.DMA((8,)),
                    pltpu.SemaphoreType.DMA((owners,)),
                ],
                compiler_params=pltpu.CompilerParams(vmem_limit_bytes=58 * megabyte),
                cost_estimate=pl.CostEstimate(
                    flops=0, bytes_accessed=20 * megabyte, transcendentals=0
                ),
                name="owner_gather",
            )(received, flat_table, *earlier)
        )
    for number, rows in enumerate(sent):
        if number:
            rows = tie(rows, returned[-1], *sent[number + 1 :])
        arrived = lax.all_to_all(rows, "table", split_axis=0, concat_axis=0, tiled=True)
        returned.append(arrived.reshape(-1, row_width))
    state = carried_rows(returning, home, entry, stores)
    weight_by_slot = bag_weight.reshape(token_count, bag_width).T
    hidden = None
    for number, part in enumerate(stage_parts):
        first, last = slot_cuts[number], slot_cuts[number + 1]
        slots = last - first
        known = [] if hidden is None else [hidden]
        pieces = returned[:part]
        hidden, state = pl.pallas_call(
            functools.partial(stage_kernel, part, first, len(known)),
            out_shape=(
                jax.ShapeDtypeStruct((token_count, channels), jnp.bfloat16),
                jax.ShapeDtypeStruct(state.shape, jnp.float32),
            ),
            in_specs=[smem] + [vmem] * 3 + [anywhere] + [vmem] * part + [anywhere] * len(known),
            out_specs=(anywhere, vmem),
            scratch_shapes=[
                pltpu.VMEM((owners * cuts[part], row_width), jnp.float32),
                pltpu.VMEM((bag_width, slots, row_width), jnp.float32),
                pltpu.VMEM(filters.shape, filters.dtype),
                pltpu.VMEM((slots + 16, channels), jnp.float32),
                pltpu.VMEM((slots + 16, channels), jnp.float32),
                pltpu.VMEM((slots, channels), jnp.bfloat16),
                pltpu.SemaphoreType.DMA(filters.shape[:1]),
                pltpu.SemaphoreType.DMA(((slots + 255) // 256,)),
            ],
            input_output_aliases={5 + part: 0} if known else {},
            compiler_params=pltpu.CompilerParams(vmem_limit_bytes=56 * megabyte),
            cost_estimate=pl.CostEstimate(
                flops=2 * slots * 3 * channels * channels * conv_weight.shape[0],
                bytes_accessed=24 * megabyte,
                transcendentals=0,
            ),
            name="stage",
        )(place, weight_by_slot, state, norm_gain, filters, *pieces, *known)
    return hidden.reshape(samples_here, slot_count, channels)


def solution(mesh):
    in_specs = (
        P(("table", "rep"), None, None),
        P(("table", "rep"), None, None),
        P(("table", "rep"), None, None),
        P(None, "table", None),
        P(("table", "rep")),
        P(("table", "rep")),
        P(("table", "rep")),
        P(("table", "rep"), None, None),
        P(None, "table", None),
        P(),
    )
    out_specs = P(("table", "rep"), None, None)
    return jax.shard_map(local, mesh=mesh, in_specs=in_specs, out_specs=out_specs, check_vma=False)
```

```python
import functools
import jax
import jax.numpy as jnp
from jax import lax
from jax.experimental import pallas as pl
from jax.experimental.pallas import tpu as pltpu
from jax.sharding import PartitionSpec as P

table_of_id = (0, 1, 2, 2, 3, 3, 3, 3)
bag_bounds = ((0, 1), (1, 2), (2, 4), (4, 8))
epsilon = 1e-05
part_ends = (0.25, 2 / 3, 1.0)
stage_parts = (2, 3)
megabyte = 1024 * 1024


def prep_kernel(cuts, shard_rows, rows_ref, owner_ref, request_ref, place_ref):
    owner = owner_ref[...]
    rows = rows_ref[...]
    owners = request_ref.shape[0]
    width, slots = owner.shape
    value_bits = (len(bag_bounds) * shard_rows).bit_length()
    owner_ids = lax.broadcasted_iota(jnp.int32, (owners, slots), 0)
    lane = lax.broadcasted_iota(jnp.int32, (owners, slots), 1)
    value = jnp.zeros((owners, slots), jnp.int32)
    for k in range(width):
        named = owner[k : k + 1, :] == owner_ids
        value = jnp.where(named, rows[k : k + 1, :] + (table_of_id[k] * shard_rows + 1), value)
    present = jnp.where(value > 0, 1, 0)
    rank = present
    step = 1
    while step < slots:
        rank = rank + jnp.where(lane >= step, pltpu.roll(rank, step, 1), 0)
        step *= 2
    rank = rank - present
    place = jnp.zeros((width, slots), jnp.int32)
    for number in range(owners):
        place = jnp.where(owner == number, rank[number : number + 1, :], place)
    landing = jnp.zeros((width, slots), jnp.int32)
    for start, stop in zip(cuts[:-1], cuts[1:]):
        where = owners * start + owner * (stop - start) + place - start
        landing = jnp.where(place >= start, where, landing)
    place_ref[...] = landing
    packed = jnp.where(value > 0, ((lane - rank) << value_bits) + value, 0)
    step = 1
    level = value_bits
    while step < slots:
        moving = jnp.where(((packed >> level) & 1) == 1, packed, 0)
        packed = (packed - moving) + pltpu.roll(moving, slots - step, 1)
        step *= 2
        level += 1
    value = jnp.maximum((packed & ((1 << value_bits) - 1)) - 1, 0)
    for number in range(owners):
        request_ref[number] = value[number : number + 1, : request_ref.shape[2]]


def pass_kernel(*refs):
    pass


def tie(array, *others):
    anywhere = pl.BlockSpec(memory_space=pl.ANY)
    return pl.pallas_call(
        pass_kernel,
        out_shape=jax.ShapeDtypeStruct(array.shape, array.dtype),
        in_specs=[anywhere] * (1 + len(others)),
        out_specs=anywhere,
        input_output_aliases={0: 0},
        name="tie",
    )(array, *others)


def gather_kernel(capacity, first, index_ref, table_ref, *refs):
    out_ref, narrow, wide, picked, packed, index, index_sem, table_sems, out_sems = refs[-9:]
    owners, piece, _ = out_ref.shape
    unroll = 32 if piece % 32 == 0 else 16
    blocks = table_sems.shape[0]
    block_rows = table_ref.shape[0] // blocks
    table_copies = []
    for block in range(blocks):
        part = pl.ds(block * block_rows, block_rows)
        copy = pltpu.make_async_copy(table_ref.at[part, :], narrow.at[part, :], table_sems.at[block])
        copy.start()
        table_copies.append(copy)
    index_copy = pltpu.make_async_copy(index_ref, index, index_sem)
    index_copy.start()
    rows = 256

    for block in range(blocks):
        table_copies[block].wait()

        def widen(step, carry, block=block):
            base = pl.multiple_of(block * block_rows + step * rows, rows)
            wide[pl.ds(base, rows), :] = narrow[pl.ds(base, rows), :].astype(jnp.float32)
            return carry

        lax.fori_loop(0, block_rows // rows, widen, 0)
    index_copy.wait()
    copies = []
    for number in range(owners):
        origin = number * capacity + first

        def some_rows(block, carry, origin=origin):
            base = pl.multiple_of(block * unroll, unroll)
            picks = [index[origin + base + i] for i in range(unroll)]
            found = [wide[pl.ds(pick, 1), :] for pick in picks]
            for i in range(unroll):
                picked[pl.ds(base + i, 1), :] = found[i]
            return carry

        lax.fori_loop(0, piece // unroll, some_rows, 0)
        packed[number] = picked[...].astype(jnp.bfloat16)
        copy = pltpu.make_async_copy(packed.at[number], out_ref.at[number], out_sems.at[number])
        copy.start()
        copies.append(copy)
    for copy in copies:
        copy.wait()


def stage_kernel(
    pieces, sources, first, aliased, place_ref, me_ref, weight_ref, carried_ref, gain_ref, *refs
):
    piece_refs = refs[:pieces]
    filter_refs = refs[pieces : pieces + sources]
    refs = refs[pieces + sources + aliased :]
    out_ref, state_ref, table, picked, filters, first_buf, second_buf, result = refs[:8]
    filter_sems, out_sems = refs[8:]
    width, slots, lanes = picked.shape
    layers = filters.shape[0]
    filter_copies = []
    if sources == 1:
        filter_copies.append(pltpu.make_async_copy(filter_refs[0], filters, filter_sems.at[0]))
    else:
        held, _, depth, _ = filter_refs[0].shape
        for number in range(2 * held):
            owner = me_ref[0] ^ shard_offset(2 * held, number)
            rows = pl.ds(pl.multiple_of(owner * depth, depth), depth)
            source = filter_refs[number // held].at[number % held]
            filter_copies.append(
                pltpu.make_async_copy(source, filters.at[:, rows, :], filter_sems.at[number])
            )
    for copy in filter_copies:
        copy.start()
    start = 0
    for piece_ref in piece_refs:
        count = piece_ref.shape[0]
        rows = 256

        def widen(step, carry, piece_ref=piece_ref, start=start):
            base = pl.multiple_of(step * rows, rows)
            table[pl.ds(start + base, rows), :] = piece_ref[pl.ds(base, rows), :].astype(jnp.float32)
            return carry

        lax.fori_loop(0, count // rows, widen, 0)
        start += count

    def some_slots(step, carry):
        base = pl.multiple_of(step * 8, 8)
        for k in range(width):
            picks = [place_ref[k, first + base + i] for i in range(8)]
            rows = [table[pl.ds(pick, 1), :] for pick in picks]
            for i in range(8):
                picked[k, pl.ds(base + i, 1), :] = rows[i]
        return carry

    lax.fori_loop(0, slots // 8, some_slots, 0)
    front = 16
    weights = jnp.transpose(weight_ref[:, first : first + slots])
    for t, (lower, upper) in enumerate(bag_bounds):
        total = picked[lower] * weights[:, lower : lower + 1]
        for k in range(lower + 1, upper):
            total = total + picked[k] * weights[:, k : k + 1]
        total = total.astype(jnp.bfloat16).astype(jnp.float32)
        first_buf[front:, t * lanes : (t + 1) * lanes] = total

    for copy in filter_copies:
        copy.wait()
    offset = 0
    out_copies = []
    for layer in range(layers):
        dilation = 2**layer
        span = 2 * dilation
        source, target = (first_buf, second_buf) if layer % 2 == 0 else (second_buf, first_buf)
        source[front - span : front, :] = carried_ref[offset : offset + span, :]
        state_ref[offset : offset + span, :] = source[front + slots - span : front + slots, :]
        offset += span
        for begin in range(0, slots, 256):
            rows = min(256, slots - begin)
            base = front + begin
            taps = [
                source[base - tap * dilation : base - tap * dilation + rows, :].astype(jnp.bfloat16)
                for tap in range(3)
            ]
            output = jnp.dot(
                jnp.concatenate(taps, axis=1), filters[layer], preferred_element_type=jnp.float32
            )
            mean = jnp.mean(output, axis=-1, keepdims=True)
            centred = output - mean
            spread = jnp.mean(centred * centred, axis=-1, keepdims=True)
            active = jnp.maximum(
                centred * lax.rsqrt(spread + epsilon) * gain_ref[layer : layer + 1, :], 0.0
            )
            if layer % 2 == 1:
                active = active + target[base : base + rows, :]
            active = active.astype(jnp.bfloat16)
            if layer == layers - 1:
                result[begin : begin + rows, :] = active
                copy = pltpu.make_async_copy(
                    result.at[pl.ds(begin, rows), :],
                    out_ref.at[pl.ds(first + begin, rows), :],
                    out_sems.at[len(out_copies)],
                )
                copy.start()
                out_copies.append(copy)
            else:
                target[base : base + rows, :] = active.astype(jnp.float32)
    for copy in out_copies:
        copy.wait()


def swap_filters(shards, distance, after):
    owners = lax.axis_size("table")
    shards = tie(shards, after)
    pairs = [(source, source ^ distance) for source in range(owners)]
    return shards, lax.ppermute(shards, "table", pairs)


def shard_offset(owners, number):
    offset = 0
    bit = owners // 2
    while bit:
        offset += bit * (number % 2)
        number //= 2
        bit //= 2
    return offset


def carried_rows(returning, home, entry, stores):
    copies = lax.axis_size("rep")
    me = lax.axis_index("rep")
    by_position = stores.transpose(1, 0, 2)
    positions, _, channels = by_position.shape
    carried = jnp.zeros((positions, channels), stores.dtype)
    for shift in range(copies):
        arrived = by_position
        if shift:
            pairs = [(source, (source + shift) % copies) for source in range(copies)]
            arrived = lax.ppermute(by_position, "rep", pairs)
        wanted = (returning[0] > 0) & (home[0] == (me + copies - shift) % copies)
        chosen = lax.dynamic_index_in_dim(arrived, entry[0], 1, keepdims=False)
        carried = jnp.where(wanted, chosen, carried)
    return carried.astype(jnp.float32)


def local(
    bag_rows, bag_owner, bag_weight, tables, returning, home, entry, stores, conv_weight, norm_gain
):
    owners = lax.axis_size("table")
    samples_here, slot_count, bag_width = bag_rows.shape
    token_count = samples_here * slot_count
    shard_rows = tables.shape[1]
    row_width = tables.shape[2]
    channels = conv_weight.shape[-1]
    capacity = min(token_count, (3 * token_count * bag_width + 2 * owners - 1) // (2 * owners))
    cuts = [0] + [round(capacity * end) // 16 * 16 for end in part_ends]
    slot_cuts = [0] + [cuts[part] for part in stage_parts[:-1]] + [token_count]
    smem = pl.BlockSpec(memory_space=pltpu.SMEM)
    vmem = pl.BlockSpec(memory_space=pltpu.VMEM)
    anywhere = pl.BlockSpec(memory_space=pl.ANY)

    me = lax.axis_index("table").astype(jnp.int32).reshape(1)
    rows_by_slot = bag_rows.reshape(token_count, bag_width).T
    owner_by_slot = bag_owner.reshape(token_count, bag_width).T
    requests, place = pl.pallas_call(
        functools.partial(prep_kernel, cuts, shard_rows),
        out_shape=(
            jax.ShapeDtypeStruct((owners, 1, capacity), jnp.int32),
            jax.ShapeDtypeStruct((bag_width, token_count), jnp.int32),
        ),
        in_specs=[vmem, vmem],
        out_specs=(vmem, vmem),
        compiler_params=pltpu.CompilerParams(vmem_limit_bytes=8 * megabyte),
        name="prep",
    )(rows_by_slot, owner_by_slot)
    received = lax.all_to_all(requests, "table", split_axis=0, concat_axis=0, tiled=True)
    received = received.reshape(owners * capacity)
    flat_table = tables.reshape(-1, row_width)
    returned = []
    sent = []
    for number in range(len(part_ends)):
        piece = cuts[number + 1] - cuts[number]
        earlier = sent[-1:]
        sent.append(
            pl.pallas_call(
                functools.partial(gather_kernel, capacity, cuts[number]),
                out_shape=jax.ShapeDtypeStruct((owners, piece, row_width), jnp.bfloat16),
                in_specs=[anywhere] * (2 + len(earlier)),
                out_specs=anywhere,
                scratch_shapes=[
                    pltpu.VMEM(flat_table.shape, jnp.bfloat16),
                    pltpu.VMEM(flat_table.shape, jnp.float32),
                    pltpu.VMEM((piece, row_width), jnp.float32),
                    pltpu.VMEM((owners, piece, row_width), jnp.bfloat16),
                    pltpu.SMEM((owners * capacity,), jnp.int32),
                    pltpu.SemaphoreType.DMA,
                    pltpu.SemaphoreType.DMA((8,)),
                    pltpu.SemaphoreType.DMA((owners,)),
                ],
                compiler_params=pltpu.CompilerParams(vmem_limit_bytes=58 * megabyte),
                cost_estimate=pl.CostEstimate(
                    flops=0, bytes_accessed=20 * megabyte, transcendentals=0
                ),
                name="owner_gather",
            )(received, flat_table, *earlier)
        )
    for number, rows in enumerate(sent):
        if number:
            rows = tie(rows, returned[-1], *sent[number + 1 :])
        arrived = lax.all_to_all(rows, "table", split_axis=0, concat_axis=0, tiled=True)
        returned.append(arrived.reshape(-1, row_width))
    swaps = owners.bit_length() - 1
    gates = [place, sent[0]] + [returned[0]] * (swaps - 3) + [returned[1]]
    filters = [conv_weight[None]]
    for step in range(swaps):
        shards = jnp.concatenate(filters, axis=0)
        filters = list(swap_filters(shards, owners >> (step + 1), gates[step]))
    if conv_weight.shape[1] % 16:
        offsets = [shard_offset(owners, number) for number in range(owners)]
        order = jnp.array([offsets.index(owner) for owner in range(owners)], jnp.int32)
        sources = order[jnp.arange(owners, dtype=jnp.int32) ^ me]
        whole = jnp.concatenate(filters, axis=0)[sources]
        filters = [whole.transpose(1, 0, 2, 3).reshape(conv_weight.shape[0], -1, channels)]
    state = carried_rows(returning, home, entry, stores)
    weight_by_slot = bag_weight.reshape(token_count, bag_width).T
    hidden = None
    for number, part in enumerate(stage_parts):
        first, last = slot_cuts[number], slot_cuts[number + 1]
        slots = last - first
        known = [] if hidden is None else [hidden]
        pieces = returned[:part]
        hidden, state = pl.pallas_call(
            functools.partial(stage_kernel, part, len(filters), first, len(known)),
            out_shape=(
                jax.ShapeDtypeStruct((token_count, channels), jnp.bfloat16),
                jax.ShapeDtypeStruct(state.shape, jnp.float32),
            ),
            in_specs=[smem] * 2
            + [vmem] * (3 + part)
            + [anywhere] * (len(filters) + len(known)),
            out_specs=(anywhere, vmem),
            scratch_shapes=[
                pltpu.VMEM((owners * cuts[part], row_width), jnp.float32),
                pltpu.VMEM((bag_width, slots, row_width), jnp.float32),
                pltpu.VMEM((conv_weight.shape[0], 3 * channels, channels), jnp.bfloat16),
                pltpu.VMEM((slots + 16, channels), jnp.float32),
                pltpu.VMEM((slots + 16, channels), jnp.float32),
                pltpu.VMEM((slots, channels), jnp.bfloat16),
                pltpu.SemaphoreType.DMA((owners,)),
                pltpu.SemaphoreType.DMA(((slots + 255) // 256,)),
            ],
            input_output_aliases={5 + part + len(filters): 0} if known else {},
            compiler_params=pltpu.CompilerParams(vmem_limit_bytes=56 * megabyte),
            cost_estimate=pl.CostEstimate(
                flops=2 * slots * 3 * channels * channels * conv_weight.shape[0],
                bytes_accessed=24 * megabyte,
                transcendentals=0,
            ),
            name="stage",
        )(place, me, weight_by_slot, state, norm_gain, *pieces, *filters, *known)
    return hidden.reshape(samples_here, slot_count, channels)


def solution(mesh):
    in_specs = (
        P(("table", "rep"), None, None),
        P(("table", "rep"), None, None),
        P(("table", "rep"), None, None),
        P(None, "table", None),
        P(("table", "rep")),
        P(("table", "rep")),
        P(("table", "rep")),
        P(("table", "rep"), None, None),
        P(None, "table", None),
        P(),
    )
    out_specs = P(("table", "rep"), None, None)
    return jax.shard_map(local, mesh=mesh, in_specs=in_specs, out_specs=out_specs, check_vma=False)
```

```python
import functools
import jax
import jax.numpy as jnp
from jax import lax
from jax.experimental import pallas as pl
from jax.experimental.pallas import tpu as pltpu
from jax.sharding import PartitionSpec as P

table_of_id = (0, 1, 2, 2, 3, 3, 3, 3)
bag_bounds = ((0, 1), (1, 2), (2, 4), (4, 8))
epsilon = 1e-05
part_ends = (0.25, 2 / 3, 1.0)
stage_parts = (2, 3)
megabyte = 1024 * 1024


def prep_kernel(cuts, shard_rows, rows_ref, owner_ref, request_ref, place_ref):
    owner = owner_ref[...]
    rows = rows_ref[...]
    owners = request_ref.shape[0]
    width, slots = owner.shape
    value_bits = (len(bag_bounds) * shard_rows).bit_length()
    owner_ids = lax.broadcasted_iota(jnp.int32, (owners, slots), 0)
    lane = lax.broadcasted_iota(jnp.int32, (owners, slots), 1)
    value = jnp.zeros((owners, slots), jnp.int32)
    for k in range(width):
        named = owner[k : k + 1, :] == owner_ids
        value = jnp.where(named, rows[k : k + 1, :] + (table_of_id[k] * shard_rows + 1), value)
    present = jnp.where(value > 0, 1, 0)
    rank = present
    step = 1
    while step < slots:
        rank = rank + jnp.where(lane >= step, pltpu.roll(rank, step, 1), 0)
        step *= 2
    rank = rank - present
    place = jnp.zeros((width, slots), jnp.int32)
    for number in range(owners):
        place = jnp.where(owner == number, rank[number : number + 1, :], place)
    landing = jnp.zeros((width, slots), jnp.int32)
    for start, stop in zip(cuts[:-1], cuts[1:]):
        where = owners * start + owner * (stop - start) + place - start
        landing = jnp.where(place >= start, where, landing)
    place_ref[...] = landing
    packed = jnp.where(value > 0, ((lane - rank) << value_bits) + value, 0)
    step = 1
    level = value_bits
    while step < slots:
        moving = jnp.where(((packed >> level) & 1) == 1, packed, 0)
        packed = (packed - moving) + pltpu.roll(moving, slots - step, 1)
        step *= 2
        level += 1
    value = jnp.maximum((packed & ((1 << value_bits) - 1)) - 1, 0)
    for number in range(owners):
        request_ref[number] = value[number : number + 1, : request_ref.shape[2]]


def pass_kernel(*refs):
    pass


def tie(array, *others):
    anywhere = pl.BlockSpec(memory_space=pl.ANY)
    return pl.pallas_call(
        pass_kernel,
        out_shape=jax.ShapeDtypeStruct(array.shape, array.dtype),
        in_specs=[anywhere] * (1 + len(others)),
        out_specs=anywhere,
        input_output_aliases={0: 0},
        name="tie",
    )(array, *others)


def gather_kernel(capacity, first, index_ref, table_ref, *refs):
    out_ref, narrow, wide, picked, packed, index, index_sem, table_sems, out_sems = refs[-9:]
    owners, piece, _ = out_ref.shape
    unroll = 32 if piece % 32 == 0 else 16
    blocks = table_sems.shape[0]
    block_rows = table_ref.shape[0] // blocks
    table_copies = []
    for block in range(blocks):
        part = pl.ds(block * block_rows, block_rows)
        copy = pltpu.make_async_copy(table_ref.at[part, :], narrow.at[part, :], table_sems.at[block])
        copy.start()
        table_copies.append(copy)
    index_copy = pltpu.make_async_copy(index_ref, index, index_sem)
    index_copy.start()
    rows = 256

    for block in range(blocks):
        table_copies[block].wait()

        def widen(step, carry, block=block):
            base = pl.multiple_of(block * block_rows + step * rows, rows)
            wide[pl.ds(base, rows), :] = narrow[pl.ds(base, rows), :].astype(jnp.float32)
            return carry

        lax.fori_loop(0, block_rows // rows, widen, 0)
    index_copy.wait()
    copies = []
    for number in range(owners):
        origin = number * capacity + first

        def some_rows(block, carry, origin=origin):
            base = pl.multiple_of(block * unroll, unroll)
            picks = [index[origin + base + i] for i in range(unroll)]
            found = [wide[pl.ds(pick, 1), :] for pick in picks]
            for i in range(unroll):
                picked[pl.ds(base + i, 1), :] = found[i]
            return carry

        lax.fori_loop(0, piece // unroll, some_rows, 0)
        packed[number] = picked[...].astype(jnp.bfloat16)
        copy = pltpu.make_async_copy(packed.at[number], out_ref.at[number], out_sems.at[number])
        copy.start()
        copies.append(copy)
    for copy in copies:
        copy.wait()


def stage_kernel(
    pieces, sources, first, aliased, place_ref, me_ref, weight_ref, carried_ref, gain_ref, *refs
):
    piece_refs = refs[:pieces]
    filter_refs = refs[pieces : pieces + sources]
    refs = refs[pieces + sources + aliased :]
    out_ref, state_ref, table, picked, filters, first_buf, second_buf, result = refs[:8]
    filter_sems, out_sems = refs[8:]
    width, slots, lanes = picked.shape
    layers = filters.shape[0]
    filter_copies = []
    if sources == 1:
        filter_copies.append(pltpu.make_async_copy(filter_refs[0], filters, filter_sems.at[0]))
    else:
        held, half, depth, _ = filter_refs[0].shape
        for group in range(4):
            layer = (me_ref[1] ^ (group // 2)) * half
            for number in range(held):
                owner = me_ref[0] ^ (shard_offset(held, number) + group % 2)
                rows = pl.ds(pl.multiple_of(owner * depth, depth), depth)
                filter_copies.append(
                    pltpu.make_async_copy(
                        filter_refs[group].at[number],
                        filters.at[pl.ds(layer, half), rows, :],
                        filter_sems.at[group * held + number],
                    )
                )
    for copy in filter_copies:
        copy.start()
    start = 0
    for piece_ref in piece_refs:
        count = piece_ref.shape[0]
        rows = 256

        def widen(step, carry, piece_ref=piece_ref, start=start):
            base = pl.multiple_of(step * rows, rows)
            table[pl.ds(start + base, rows), :] = piece_ref[pl.ds(base, rows), :].astype(jnp.float32)
            return carry

        lax.fori_loop(0, count // rows, widen, 0)
        start += count

    def some_slots(step, carry):
        base = pl.multiple_of(step * 8, 8)
        for k in range(width):
            picks = [place_ref[k, first + base + i] for i in range(8)]
            rows = [table[pl.ds(pick, 1), :] for pick in picks]
            for i in range(8):
                picked[k, pl.ds(base + i, 1), :] = rows[i]
        return carry

    lax.fori_loop(0, slots // 8, some_slots, 0)
    front = 16
    weights = jnp.transpose(weight_ref[:, first : first + slots])
    for t, (lower, upper) in enumerate(bag_bounds):
        total = picked[lower] * weights[:, lower : lower + 1]
        for k in range(lower + 1, upper):
            total = total + picked[k] * weights[:, k : k + 1]
        total = total.astype(jnp.bfloat16).astype(jnp.float32)
        first_buf[front:, t * lanes : (t + 1) * lanes] = total

    for copy in filter_copies:
        copy.wait()
    offset = 0
    out_copies = []
    for layer in range(layers):
        dilation = 2**layer
        span = 2 * dilation
        source, target = (first_buf, second_buf) if layer % 2 == 0 else (second_buf, first_buf)
        source[front - span : front, :] = carried_ref[offset : offset + span, :]
        state_ref[offset : offset + span, :] = source[front + slots - span : front + slots, :]
        offset += span
        for begin in range(0, slots, 256):
            rows = min(256, slots - begin)
            base = front + begin
            taps = [
                source[base - tap * dilation : base - tap * dilation + rows, :].astype(jnp.bfloat16)
                for tap in range(3)
            ]
            output = jnp.dot(
                jnp.concatenate(taps, axis=1), filters[layer], preferred_element_type=jnp.float32
            )
            mean = jnp.mean(output, axis=-1, keepdims=True)
            centred = output - mean
            spread = jnp.mean(centred * centred, axis=-1, keepdims=True)
            active = jnp.maximum(
                centred * lax.rsqrt(spread + epsilon) * gain_ref[layer : layer + 1, :], 0.0
            )
            if layer % 2 == 1:
                active = active + target[base : base + rows, :]
            active = active.astype(jnp.bfloat16)
            if layer == layers - 1:
                result[begin : begin + rows, :] = active
                copy = pltpu.make_async_copy(
                    result.at[pl.ds(begin, rows), :],
                    out_ref.at[pl.ds(first + begin, rows), :],
                    out_sems.at[len(out_copies)],
                )
                copy.start()
                out_copies.append(copy)
            else:
                target[base : base + rows, :] = active.astype(jnp.float32)
    for copy in out_copies:
        copy.wait()


def swapped(array, axis, distance):
    pairs = [(source, source ^ distance) for source in range(lax.axis_size(axis))]
    return lax.ppermute(array, axis, pairs)


def shard_offset(held, number):
    offset = 0
    bit = held
    while bit > 1:
        offset += bit * (number % 2)
        number //= 2
        bit //= 2
    return offset


def carried_rows(returning, home, entry, stores):
    copies = lax.axis_size("rep")
    me = lax.axis_index("rep")
    by_position = stores.transpose(1, 0, 2)
    positions, _, channels = by_position.shape
    carried = jnp.zeros((positions, channels), stores.dtype)
    for shift in range(copies):
        arrived = by_position
        if shift:
            pairs = [(source, (source + shift) % copies) for source in range(copies)]
            arrived = lax.ppermute(by_position, "rep", pairs)
        wanted = (returning[0] > 0) & (home[0] == (me + copies - shift) % copies)
        chosen = lax.dynamic_index_in_dim(arrived, entry[0], 1, keepdims=False)
        carried = jnp.where(wanted, chosen, carried)
    return carried.astype(jnp.float32)


def local(
    bag_rows, bag_owner, bag_weight, tables, returning, home, entry, stores, conv_weight, norm_gain
):
    owners = lax.axis_size("table")
    samples_here, slot_count, bag_width = bag_rows.shape
    token_count = samples_here * slot_count
    shard_rows = tables.shape[1]
    row_width = tables.shape[2]
    channels = conv_weight.shape[-1]
    capacity = min(token_count, (3 * token_count * bag_width + 2 * owners - 1) // (2 * owners))
    cuts = [0] + [round(capacity * end) // 16 * 16 for end in part_ends]
    slot_cuts = [0] + [cuts[part] for part in stage_parts[:-1]] + [token_count]
    smem = pl.BlockSpec(memory_space=pltpu.SMEM)
    vmem = pl.BlockSpec(memory_space=pltpu.VMEM)
    anywhere = pl.BlockSpec(memory_space=pl.ANY)

    me = jnp.stack([lax.axis_index("table"), lax.axis_index("rep") % 2]).astype(jnp.int32)
    half = conv_weight.shape[0] // 2
    first_shard = lax.dynamic_slice_in_dim(conv_weight, me[1] * half, half, 0)[None]
    second_shard = swapped(first_shard, "table", owners // 2)
    state = carried_rows(returning, home, entry, stores)
    rows_by_slot = bag_rows.reshape(token_count, bag_width).T
    owner_by_slot = bag_owner.reshape(token_count, bag_width).T
    requests, place = pl.pallas_call(
        functools.partial(prep_kernel, cuts, shard_rows),
        out_shape=(
            jax.ShapeDtypeStruct((owners, 1, capacity), jnp.int32),
            jax.ShapeDtypeStruct((bag_width, token_count), jnp.int32),
        ),
        in_specs=[vmem, vmem],
        out_specs=(vmem, vmem),
        compiler_params=pltpu.CompilerParams(vmem_limit_bytes=8 * megabyte),
        name="prep",
    )(rows_by_slot, owner_by_slot)
    received = lax.all_to_all(requests, "table", split_axis=0, concat_axis=0, tiled=True)
    received = received.reshape(owners * capacity)
    flat_table = tables.reshape(-1, row_width)
    returned = []
    sent = []
    for number in range(len(part_ends)):
        piece = cuts[number + 1] - cuts[number]
        earlier = sent[-1:] if sent else [second_shard]
        if number == 2:
            earlier = earlier + [state]
        sent.append(
            pl.pallas_call(
                functools.partial(gather_kernel, capacity, cuts[number]),
                out_shape=jax.ShapeDtypeStruct((owners, piece, row_width), jnp.bfloat16),
                in_specs=[anywhere] * (2 + len(earlier)),
                out_specs=anywhere,
                scratch_shapes=[
                    pltpu.VMEM(flat_table.shape, jnp.bfloat16),
                    pltpu.VMEM(flat_table.shape, jnp.float32),
                    pltpu.VMEM((piece, row_width), jnp.float32),
                    pltpu.VMEM((owners, piece, row_width), jnp.bfloat16),
                    pltpu.SMEM((owners * capacity,), jnp.int32),
                    pltpu.SemaphoreType.DMA,
                    pltpu.SemaphoreType.DMA((8,)),
                    pltpu.SemaphoreType.DMA((owners,)),
                ],
                compiler_params=pltpu.CompilerParams(vmem_limit_bytes=58 * megabyte),
                cost_estimate=pl.CostEstimate(
                    flops=0, bytes_accessed=20 * megabyte, transcendentals=0
                ),
                name="owner_gather",
            )(received, flat_table, *earlier)
        )
    for number, rows in enumerate(sent):
        if number:
            rows = tie(rows, returned[-1], *sent[number + 1 :])
        arrived = lax.all_to_all(rows, "table", split_axis=0, concat_axis=0, tiled=True)
        returned.append(arrived.reshape(-1, row_width))
    shards = jnp.concatenate([first_shard, second_shard], axis=0)
    distance = owners // 4
    while distance > 1:
        shards = tie(shards, sent[0] if distance == owners // 4 else sent[1])
        shards = jnp.concatenate([shards, swapped(shards, "table", distance)], axis=0)
        distance //= 2
    shards = tie(shards, returned[0])
    others = swapped(shards, "rep", 1)
    near_shards = swapped(shards, "table", 1)
    others = tie(others, returned[1])
    near_others = swapped(others, "table", 1)
    filters = [shards, near_shards, others, near_others]
    if conv_weight.shape[1] % 16:
        offsets = [shard_offset(owners // 2, number) for number in range(owners // 2)]
        offsets = offsets + [offset + 1 for offset in offsets]
        order = jnp.array([offsets.index(owner) for owner in range(owners)], jnp.int32)
        sources = order[jnp.arange(owners, dtype=jnp.int32) ^ me[0]]
        mine = jnp.concatenate(filters[:2], axis=0)[sources]
        rest = jnp.concatenate(filters[2:], axis=0)[sources]
        low, high = jnp.where(me[1] == 0, mine, rest), jnp.where(me[1] == 0, rest, mine)
        whole = jnp.concatenate([low, high], axis=1).transpose(1, 0, 2, 3)
        filters = [whole.reshape(conv_weight.shape[0], -1, channels)]
    weight_by_slot = bag_weight.reshape(token_count, bag_width).T
    hidden = None
    for number, part in enumerate(stage_parts):
        first, last = slot_cuts[number], slot_cuts[number + 1]
        slots = last - first
        known = [] if hidden is None else [hidden]
        pieces = returned[:part]
        hidden, state = pl.pallas_call(
            functools.partial(stage_kernel, part, len(filters), first, len(known)),
            out_shape=(
                jax.ShapeDtypeStruct((token_count, channels), jnp.bfloat16),
                jax.ShapeDtypeStruct(state.shape, jnp.float32),
            ),
            in_specs=[smem] * 2
            + [vmem] * (3 + part)
            + [anywhere] * (len(filters) + len(known)),
            out_specs=(anywhere, vmem),
            scratch_shapes=[
                pltpu.VMEM((owners * cuts[part], row_width), jnp.float32),
                pltpu.VMEM((bag_width, slots, row_width), jnp.float32),
                pltpu.VMEM((conv_weight.shape[0], 3 * channels, channels), jnp.bfloat16),
                pltpu.VMEM((slots + 16, channels), jnp.float32),
                pltpu.VMEM((slots + 16, channels), jnp.float32),
                pltpu.VMEM((slots, channels), jnp.bfloat16),
                pltpu.SemaphoreType.DMA((2 * owners,)),
                pltpu.SemaphoreType.DMA(((slots + 255) // 256,)),
            ],
            input_output_aliases={5 + part + len(filters): 0} if known else {},
            compiler_params=pltpu.CompilerParams(vmem_limit_bytes=56 * megabyte),
            cost_estimate=pl.CostEstimate(
                flops=2 * slots * 3 * channels * channels * conv_weight.shape[0],
                bytes_accessed=24 * megabyte,
                transcendentals=0,
            ),
            name="stage",
        )(place, me, weight_by_slot, state, norm_gain, *pieces, *filters, *known)
    return hidden.reshape(samples_here, slot_count, channels)


def solution(mesh):
    in_specs = (
        P(("table", "rep"), None, None),
        P(("table", "rep"), None, None),
        P(("table", "rep"), None, None),
        P(None, "table", None),
        P(("table", "rep")),
        P(("table", "rep")),
        P(("table", "rep")),
        P(("table", "rep"), None, None),
        P(None, "table", None),
        P(),
    )
    out_specs = P(("table", "rep"), None, None)
    return jax.shard_map(local, mesh=mesh, in_specs=in_specs, out_specs=out_specs, check_vma=False)
```

```python
import functools
import jax
import jax.numpy as jnp
from jax import lax
from jax.experimental import pallas as pl
from jax.experimental.pallas import tpu as pltpu
from jax.sharding import PartitionSpec as P

table_of_id = (0, 1, 2, 2, 3, 3, 3, 3)
bag_bounds = ((0, 1), (1, 2), (2, 4), (4, 8))
epsilon = 1e-05
part_ends = (0.25, 2 / 3, 1.0)
stage_parts = (2, 3)
megabyte = 1024 * 1024


def prep_kernel(cuts, shard_rows, rows_ref, owner_ref, request_ref, place_ref):
    owner = owner_ref[...]
    rows = rows_ref[...]
    owners = request_ref.shape[0]
    width, slots = owner.shape
    value_bits = (len(bag_bounds) * shard_rows).bit_length()
    owner_ids = lax.broadcasted_iota(jnp.int32, (owners, slots), 0)
    lane = lax.broadcasted_iota(jnp.int32, (owners, slots), 1)
    value = jnp.zeros((owners, slots), jnp.int32)
    for k in range(width):
        named = owner[k : k + 1, :] == owner_ids
        value = jnp.where(named, rows[k : k + 1, :] + (table_of_id[k] * shard_rows + 1), value)
    present = jnp.where(value > 0, 1, 0)
    rank = present
    step = 1
    while step < slots:
        rank = rank + jnp.where(lane >= step, pltpu.roll(rank, step, 1), 0)
        step *= 2
    rank = rank - present
    place = jnp.zeros((width, slots), jnp.int32)
    for number in range(owners):
        place = jnp.where(owner == number, rank[number : number + 1, :], place)
    landing = jnp.zeros((width, slots), jnp.int32)
    for start, stop in zip(cuts[:-1], cuts[1:]):
        where = owners * start + owner * (stop - start) + place - start
        landing = jnp.where(place >= start, where, landing)
    place_ref[...] = landing
    packed = jnp.where(value > 0, ((lane - rank) << value_bits) + value, 0)
    step = 1
    level = value_bits
    while step < slots:
        moving = jnp.where(((packed >> level) & 1) == 1, packed, 0)
        packed = (packed - moving) + pltpu.roll(moving, slots - step, 1)
        step *= 2
        level += 1
    value = jnp.maximum((packed & ((1 << value_bits) - 1)) - 1, 0)
    for number in range(owners):
        request_ref[number] = value[number : number + 1, : request_ref.shape[2]]


def pass_kernel(*refs):
    pass


def tie(array, *others):
    anywhere = pl.BlockSpec(memory_space=pl.ANY)
    return pl.pallas_call(
        pass_kernel,
        out_shape=jax.ShapeDtypeStruct(array.shape, array.dtype),
        in_specs=[anywhere] * (1 + len(others)),
        out_specs=anywhere,
        input_output_aliases={0: 0},
        name="tie",
    )(array, *others)


def gather_kernel(capacity, first, index_ref, table_ref, *refs):
    out_ref, narrow, wide, picked, packed, index, index_sem, table_sems, out_sems = refs[-9:]
    owners, piece, _ = out_ref.shape
    unroll = 32 if piece % 32 == 0 else 16
    blocks = table_sems.shape[0]
    block_rows = table_ref.shape[0] // blocks
    table_copies = []
    for block in range(blocks):
        part = pl.ds(block * block_rows, block_rows)
        copy = pltpu.make_async_copy(table_ref.at[part, :], narrow.at[part, :], table_sems.at[block])
        copy.start()
        table_copies.append(copy)
    index_copy = pltpu.make_async_copy(index_ref, index, index_sem)
    index_copy.start()
    rows = 256

    for block in range(blocks):
        table_copies[block].wait()

        def widen(step, carry, block=block):
            base = pl.multiple_of(block * block_rows + step * rows, rows)
            wide[pl.ds(base, rows), :] = narrow[pl.ds(base, rows), :].astype(jnp.float32)
            return carry

        lax.fori_loop(0, block_rows // rows, widen, 0)
    index_copy.wait()
    copies = []
    for number in range(owners):
        origin = number * capacity + first

        def some_rows(block, carry, origin=origin):
            base = pl.multiple_of(block * unroll, unroll)
            picks = [index[origin + base + i] for i in range(unroll)]
            found = [wide[pl.ds(pick, 1), :] for pick in picks]
            for i in range(unroll):
                picked[pl.ds(base + i, 1), :] = found[i]
            return carry

        lax.fori_loop(0, piece // unroll, some_rows, 0)
        packed[number] = picked[...].astype(jnp.bfloat16)
        copy = pltpu.make_async_copy(packed.at[number], out_ref.at[number], out_sems.at[number])
        copy.start()
        copies.append(copy)
    for copy in copies:
        copy.wait()


def stage_kernel(
    pieces, sources, first, aliased, place_ref, me_ref, weight_ref, carried_ref, gain_ref, *refs
):
    piece_refs = refs[:pieces]
    filter_refs = refs[pieces : pieces + sources]
    refs = refs[pieces + sources + aliased :]
    out_ref, state_ref, table, picked, filters, first_buf, second_buf, result = refs[:8]
    filter_sems, out_sems = refs[8:]
    width, slots, lanes = picked.shape
    layers = filters.shape[0]
    filter_copies = []
    if sources == 1:
        filter_copies.append(pltpu.make_async_copy(filter_refs[0], filters, filter_sems.at[0]))
    else:
        held, half, depth, _ = filter_refs[0].shape
        for group, filter_ref in enumerate(filter_refs):
            bits, base = block_place(group, me_ref[1])
            for number in range(held):
                owner = me_ref[0] ^ (shard_offset(held, number) + bits)
                rows = pl.ds(pl.multiple_of(owner * depth, depth), depth)
                layer = pl.ds(base * (half // 2), filter_ref.shape[1])
                filter_copies.append(
                    pltpu.make_async_copy(
                        filter_ref.at[number],
                        filters.at[layer, rows, :],
                        filter_sems.at[group * held + number],
                    )
                )
    for copy in filter_copies:
        copy.start()
    start = 0
    for piece_ref in piece_refs:
        count = piece_ref.shape[0]
        rows = 256

        def widen(step, carry, piece_ref=piece_ref, start=start):
            base = pl.multiple_of(step * rows, rows)
            table[pl.ds(start + base, rows), :] = piece_ref[pl.ds(base, rows), :].astype(jnp.float32)
            return carry

        lax.fori_loop(0, count // rows, widen, 0)
        start += count

    def some_slots(step, carry):
        base = pl.multiple_of(step * 8, 8)
        for k in range(width):
            picks = [place_ref[k, first + base + i] for i in range(8)]
            rows = [table[pl.ds(pick, 1), :] for pick in picks]
            for i in range(8):
                picked[k, pl.ds(base + i, 1), :] = rows[i]
        return carry

    lax.fori_loop(0, slots // 8, some_slots, 0)
    front = 16
    weights = jnp.transpose(weight_ref[:, first : first + slots])
    for t, (lower, upper) in enumerate(bag_bounds):
        total = picked[lower] * weights[:, lower : lower + 1]
        for k in range(lower + 1, upper):
            total = total + picked[k] * weights[:, k : k + 1]
        total = total.astype(jnp.bfloat16).astype(jnp.float32)
        first_buf[front:, t * lanes : (t + 1) * lanes] = total

    for copy in filter_copies:
        copy.wait()
    offset = 0
    out_copies = []
    for layer in range(layers):
        dilation = 2**layer
        span = 2 * dilation
        source, target = (first_buf, second_buf) if layer % 2 == 0 else (second_buf, first_buf)
        source[front - span : front, :] = carried_ref[offset : offset + span, :]
        state_ref[offset : offset + span, :] = source[front + slots - span : front + slots, :]
        offset += span
        for begin in range(0, slots, 256):
            rows = min(256, slots - begin)
            base = front + begin
            taps = [
                source[base - tap * dilation : base - tap * dilation + rows, :].astype(jnp.bfloat16)
                for tap in range(3)
            ]
            output = jnp.dot(
                jnp.concatenate(taps, axis=1), filters[layer], preferred_element_type=jnp.float32
            )
            mean = jnp.mean(output, axis=-1, keepdims=True)
            centred = output - mean
            spread = jnp.mean(centred * centred, axis=-1, keepdims=True)
            active = jnp.maximum(
                centred * lax.rsqrt(spread + epsilon) * gain_ref[layer : layer + 1, :], 0.0
            )
            if layer % 2 == 1:
                active = active + target[base : base + rows, :]
            active = active.astype(jnp.bfloat16)
            if layer == layers - 1:
                result[begin : begin + rows, :] = active
                copy = pltpu.make_async_copy(
                    result.at[pl.ds(begin, rows), :],
                    out_ref.at[pl.ds(first + begin, rows), :],
                    out_sems.at[len(out_copies)],
                )
                copy.start()
                out_copies.append(copy)
            else:
                target[base : base + rows, :] = active.astype(jnp.float32)
    for copy in out_copies:
        copy.wait()


def swapped(array, axis, distance):
    pairs = [(source, source ^ distance) for source in range(lax.axis_size(axis))]
    return lax.ppermute(array, axis, pairs)


def shard_offset(held, number):
    offset = 0
    bit = 2 * held
    while bit > 2:
        offset += bit * (number % 2)
        number //= 2
        bit //= 2
    return offset


def block_place(number, side):
    kind = number % 5
    bits = (2 if kind in (1, 3, 4) else 0) + number // 5
    base = 2 * (side if kind < 2 else 1 - side) + (1 if kind == 4 else 0)
    return bits, base


def ordered_filters(blocks, me):
    count = blocks[0].shape[0]
    owners = 4 * count
    quarter = blocks[0].shape[1] // 2
    layers = 4 * quarter
    whole = jnp.zeros((owners, layers) + blocks[0].shape[2:], blocks[0].dtype)
    for number, block in enumerate(blocks):
        bits, base = block_place(number, me[1])
        for shard in range(count):
            owner = me[0] ^ (shard_offset(count, shard) + bits)
            whole = lax.dynamic_update_slice(
                whole, block[shard][None], (owner, base * quarter, 0, 0)
            )
    return whole.transpose(1, 0, 2, 3).reshape(layers, -1, whole.shape[-1])


def carried_rows(returning, home, entry, stores):
    copies = lax.axis_size("rep")
    me = lax.axis_index("rep")
    by_position = stores.transpose(1, 0, 2)
    positions, _, channels = by_position.shape
    carried = jnp.zeros((positions, channels), stores.dtype)
    for shift in range(copies):
        arrived = by_position
        if shift:
            pairs = [(source, (source + shift) % copies) for source in range(copies)]
            arrived = lax.ppermute(by_position, "rep", pairs)
        wanted = (returning[0] > 0) & (home[0] == (me + copies - shift) % copies)
        chosen = lax.dynamic_index_in_dim(arrived, entry[0], 1, keepdims=False)
        carried = jnp.where(wanted, chosen, carried)
    return carried.astype(jnp.float32)


def local(
    bag_rows, bag_owner, bag_weight, tables, returning, home, entry, stores, conv_weight, norm_gain
):
    owners = lax.axis_size("table")
    samples_here, slot_count, bag_width = bag_rows.shape
    token_count = samples_here * slot_count
    shard_rows = tables.shape[1]
    row_width = tables.shape[2]
    channels = conv_weight.shape[-1]
    capacity = min(token_count, (3 * token_count * bag_width + 2 * owners - 1) // (2 * owners))
    cuts = [0] + [round(capacity * end) // 16 * 16 for end in part_ends]
    slot_cuts = [0] + [cuts[part] for part in stage_parts[:-1]] + [token_count]
    smem = pl.BlockSpec(memory_space=pltpu.SMEM)
    vmem = pl.BlockSpec(memory_space=pltpu.VMEM)
    anywhere = pl.BlockSpec(memory_space=pl.ANY)

    me = jnp.stack([lax.axis_index("table"), lax.axis_index("rep") % 2]).astype(jnp.int32)
    half = conv_weight.shape[0] // 2
    first_shard = lax.dynamic_slice_in_dim(conv_weight, me[1] * half, half, 0)[None]
    second_shard = swapped(first_shard, "table", owners // 2)
    state = carried_rows(returning, home, entry, stores)
    rows_by_slot = bag_rows.reshape(token_count, bag_width).T
    owner_by_slot = bag_owner.reshape(token_count, bag_width).T
    requests, place = pl.pallas_call(
        functools.partial(prep_kernel, cuts, shard_rows),
        out_shape=(
            jax.ShapeDtypeStruct((owners, 1, capacity), jnp.int32),
            jax.ShapeDtypeStruct((bag_width, token_count), jnp.int32),
        ),
        in_specs=[vmem, vmem],
        out_specs=(vmem, vmem),
        compiler_params=pltpu.CompilerParams(vmem_limit_bytes=8 * megabyte),
        name="prep",
    )(rows_by_slot, owner_by_slot)
    received = lax.all_to_all(requests, "table", split_axis=0, concat_axis=0, tiled=True)
    received = received.reshape(owners * capacity)
    flat_table = tables.reshape(-1, row_width)
    returned = []
    sent = []
    line = jnp.concatenate([first_shard, second_shard], axis=0)
    for number in range(len(part_ends)):
        piece = cuts[number + 1] - cuts[number]
        earlier = sent[-1:] if sent else [second_shard]
        if number == 1:
            line = tie(line, sent[0])
            distance = owners // 4
            while distance > 2:
                line = jnp.concatenate([line, swapped(line, "table", distance)], axis=0)
                distance //= 2
        if number == 2:
            earlier = earlier + [state, line]
        sent.append(
            pl.pallas_call(
                functools.partial(gather_kernel, capacity, cuts[number]),
                out_shape=jax.ShapeDtypeStruct((owners, piece, row_width), jnp.bfloat16),
                in_specs=[anywhere] * (2 + len(earlier)),
                out_specs=anywhere,
                scratch_shapes=[
                    pltpu.VMEM(flat_table.shape, jnp.bfloat16),
                    pltpu.VMEM(flat_table.shape, jnp.float32),
                    pltpu.VMEM((piece, row_width), jnp.float32),
                    pltpu.VMEM((owners, piece, row_width), jnp.bfloat16),
                    pltpu.SMEM((owners * capacity,), jnp.int32),
                    pltpu.SemaphoreType.DMA,
                    pltpu.SemaphoreType.DMA((8,)),
                    pltpu.SemaphoreType.DMA((owners,)),
                ],
                compiler_params=pltpu.CompilerParams(vmem_limit_bytes=58 * megabyte),
                cost_estimate=pl.CostEstimate(
                    flops=0, bytes_accessed=20 * megabyte, transcendentals=0
                ),
                name="owner_gather",
            )(received, flat_table, *earlier)
        )
    for number, rows in enumerate(sent):
        if number:
            rows = tie(rows, returned[-1], *sent[number + 1 :])
        arrived = lax.all_to_all(rows, "table", split_axis=0, concat_axis=0, tiled=True)
        returned.append(arrived.reshape(-1, row_width))
    by_table = swapped(line, "table", 2)
    by_rep = swapped(line, "rep", 1)
    corner_low = swapped(by_rep[:, : half // 2], "table", 2)
    corner_high = swapped(by_table[:, half // 2 :], "rep", 1)
    corner_low, corner_high = tie(corner_low, returned[1]), tie(corner_high, returned[1])
    blocks = [line, by_table, by_rep, corner_low, corner_high]
    filters = blocks + [swapped(block, "table", 1) for block in blocks]
    if conv_weight.shape[1] % 16:
        filters = [ordered_filters(filters, me)]
    weight_by_slot = bag_weight.reshape(token_count, bag_width).T
    hidden = None
    for number, part in enumerate(stage_parts):
        first, last = slot_cuts[number], slot_cuts[number + 1]
        slots = last - first
        known = [] if hidden is None else [hidden]
        pieces = returned[:part]
        hidden, state = pl.pallas_call(
            functools.partial(stage_kernel, part, len(filters), first, len(known)),
            out_shape=(
                jax.ShapeDtypeStruct((token_count, channels), jnp.bfloat16),
                jax.ShapeDtypeStruct(state.shape, jnp.float32),
            ),
            in_specs=[smem] * 2
            + [vmem] * (3 + part)
            + [anywhere] * (len(filters) + len(known)),
            out_specs=(anywhere, vmem),
            scratch_shapes=[
                pltpu.VMEM((owners * cuts[part], row_width), jnp.float32),
                pltpu.VMEM((bag_width, slots, row_width), jnp.float32),
                pltpu.VMEM((conv_weight.shape[0], 3 * channels, channels), jnp.bfloat16),
                pltpu.VMEM((slots + 16, channels), jnp.float32),
                pltpu.VMEM((slots + 16, channels), jnp.float32),
                pltpu.VMEM((slots, channels), jnp.bfloat16),
                pltpu.SemaphoreType.DMA((10 * (owners // 4),)),
                pltpu.SemaphoreType.DMA(((slots + 255) // 256,)),
            ],
            input_output_aliases={5 + part + len(filters): 0} if known else {},
            compiler_params=pltpu.CompilerParams(vmem_limit_bytes=56 * megabyte),
            cost_estimate=pl.CostEstimate(
                flops=2 * slots * 3 * channels * channels * conv_weight.shape[0],
                bytes_accessed=24 * megabyte,
                transcendentals=0,
            ),
            name="stage",
        )(place, me, weight_by_slot, state, norm_gain, *pieces, *filters, *known)
    return hidden.reshape(samples_here, slot_count, channels)


def solution(mesh):
    in_specs = (
        P(("table", "rep"), None, None),
        P(("table", "rep"), None, None),
        P(("table", "rep"), None, None),
        P(None, "table", None),
        P(("table", "rep")),
        P(("table", "rep")),
        P(("table", "rep")),
        P(("table", "rep"), None, None),
        P(None, "table", None),
        P(),
    )
    out_specs = P(("table", "rep"), None, None)
    return jax.shard_map(local, mesh=mesh, in_specs=in_specs, out_specs=out_specs, check_vma=False)
```

```python
import functools
import jax
import jax.numpy as jnp
from jax import lax
from jax.experimental import pallas as pl
from jax.experimental.pallas import tpu as pltpu
from jax.sharding import PartitionSpec as P

table_of_id = (0, 1, 2, 2, 3, 3, 3, 3)
bag_bounds = ((0, 1), (1, 2), (2, 4), (4, 8))
epsilon = 1e-05
part_ends = (0.25, 2 / 3, 1.0)
stage_parts = (2, 3)
megabyte = 1024 * 1024


def prep_kernel(cuts, shard_rows, rows_ref, owner_ref, request_ref, place_ref):
    owner = owner_ref[...]
    rows = rows_ref[...]
    owners = request_ref.shape[0]
    width, slots = owner.shape
    value_bits = (len(bag_bounds) * shard_rows).bit_length()
    owner_ids = lax.broadcasted_iota(jnp.int32, (owners, slots), 0)
    lane = lax.broadcasted_iota(jnp.int32, (owners, slots), 1)
    value = jnp.zeros((owners, slots), jnp.int32)
    for k in range(width):
        named = owner[k : k + 1, :] == owner_ids
        value = jnp.where(named, rows[k : k + 1, :] + (table_of_id[k] * shard_rows + 1), value)
    present = jnp.where(value > 0, 1, 0)
    rank = present
    step = 1
    while step < slots:
        rank = rank + jnp.where(lane >= step, pltpu.roll(rank, step, 1), 0)
        step *= 2
    rank = rank - present
    place = jnp.zeros((width, slots), jnp.int32)
    for number in range(owners):
        place = jnp.where(owner == number, rank[number : number + 1, :], place)
    landing = jnp.zeros((width, slots), jnp.int32)
    for start, stop in zip(cuts[:-1], cuts[1:]):
        where = owners * start + owner * (stop - start) + place - start
        landing = jnp.where(place >= start, where, landing)
    place_ref[...] = landing
    packed = jnp.where(value > 0, ((lane - rank) << value_bits) + value, 0)
    step = 1
    level = value_bits
    while step < slots:
        moving = jnp.where(((packed >> level) & 1) == 1, packed, 0)
        packed = (packed - moving) + pltpu.roll(moving, slots - step, 1)
        step *= 2
        level += 1
    value = jnp.maximum((packed & ((1 << value_bits) - 1)) - 1, 0)
    for number in range(owners):
        request_ref[number] = value[number : number + 1, : request_ref.shape[2]]


def pass_kernel(*refs):
    pass


def tie(array, *others):
    anywhere = pl.BlockSpec(memory_space=pl.ANY)
    return pl.pallas_call(
        pass_kernel,
        out_shape=jax.ShapeDtypeStruct(array.shape, array.dtype),
        in_specs=[anywhere] * (1 + len(others)),
        out_specs=anywhere,
        input_output_aliases={0: 0},
        name="tie",
    )(array, *others)


def gather_kernel(capacity, first, index_ref, table_ref, *refs):
    out_ref, narrow, wide, picked, packed, index, index_sem, table_sems, out_sems = refs[-9:]
    owners, piece, _ = out_ref.shape
    unroll = 32 if piece % 32 == 0 else 16
    blocks = table_sems.shape[0]
    block_rows = table_ref.shape[0] // blocks
    table_copies = []
    for block in range(blocks):
        part = pl.ds(block * block_rows, block_rows)
        copy = pltpu.make_async_copy(table_ref.at[part, :], narrow.at[part, :], table_sems.at[block])
        copy.start()
        table_copies.append(copy)
    index_copy = pltpu.make_async_copy(index_ref, index, index_sem)
    index_copy.start()
    rows = 256

    for block in range(blocks):
        table_copies[block].wait()

        def widen(step, carry, block=block):
            base = pl.multiple_of(block * block_rows + step * rows, rows)
            wide[pl.ds(base, rows), :] = narrow[pl.ds(base, rows), :].astype(jnp.float32)
            return carry

        lax.fori_loop(0, block_rows // rows, widen, 0)
    index_copy.wait()
    copies = []
    for number in range(owners):
        origin = number * capacity + first

        def some_rows(block, carry, origin=origin):
            base = pl.multiple_of(block * unroll, unroll)
            picks = [index[origin + base + i] for i in range(unroll)]
            found = [wide[pl.ds(pick, 1), :] for pick in picks]
            for i in range(unroll):
                picked[pl.ds(base + i, 1), :] = found[i]
            return carry

        lax.fori_loop(0, piece // unroll, some_rows, 0)
        packed[number] = picked[...].astype(jnp.bfloat16)
        copy = pltpu.make_async_copy(packed.at[number], out_ref.at[number], out_sems.at[number])
        copy.start()
        copies.append(copy)
    for copy in copies:
        copy.wait()


def stage_kernel(
    pieces, sources, first, aliased, place_ref, me_ref, weight_ref, carried_ref, gain_ref, *refs
):
    piece_refs = refs[:pieces]
    filter_refs = refs[pieces : pieces + sources]
    refs = refs[pieces + sources + aliased :]
    out_ref, state_ref, table, picked, filters, first_buf, second_buf, result = refs[:8]
    filter_sems, out_sems = refs[8:]
    width, slots, lanes = picked.shape
    layers = filters.shape[0]
    filter_copies = []
    if sources == 1:
        filter_copies.append(pltpu.make_async_copy(filter_refs[0], filters, filter_sems.at[0]))
    else:
        held, half, depth, _ = filter_refs[0].shape
        for group, filter_ref in enumerate(filter_refs):
            bits, base = block_place(group, me_ref[1])
            for number in range(held):
                owner = me_ref[0] ^ (4 * number + bits)
                rows = pl.ds(pl.multiple_of(owner * depth, depth), depth)
                layer = pl.ds(base * (half // 2), filter_ref.shape[1])
                filter_copies.append(
                    pltpu.make_async_copy(
                        filter_ref.at[number],
                        filters.at[layer, rows, :],
                        filter_sems.at[group * held + number],
                    )
                )
    for copy in filter_copies:
        copy.start()
    start = 0
    for piece_ref in piece_refs:
        count = piece_ref.shape[0]
        rows = 256

        def widen(step, carry, piece_ref=piece_ref, start=start):
            base = pl.multiple_of(step * rows, rows)
            table[pl.ds(start + base, rows), :] = piece_ref[pl.ds(base, rows), :].astype(jnp.float32)
            return carry

        lax.fori_loop(0, count // rows, widen, 0)
        start += count

    def some_slots(step, carry):
        base = pl.multiple_of(step * 8, 8)
        for k in range(width):
            picks = [place_ref[k, first + base + i] for i in range(8)]
            rows = [table[pl.ds(pick, 1), :] for pick in picks]
            for i in range(8):
                picked[k, pl.ds(base + i, 1), :] = rows[i]
        return carry

    lax.fori_loop(0, slots // 8, some_slots, 0)
    front = 16
    weights = jnp.transpose(weight_ref[:, first : first + slots])
    for t, (lower, upper) in enumerate(bag_bounds):
        total = picked[lower] * weights[:, lower : lower + 1]
        for k in range(lower + 1, upper):
            total = total + picked[k] * weights[:, k : k + 1]
        total = total.astype(jnp.bfloat16).astype(jnp.float32)
        first_buf[front:, t * lanes : (t + 1) * lanes] = total

    for copy in filter_copies:
        copy.wait()
    offset = 0
    out_copies = []
    for layer in range(layers):
        dilation = 2**layer
        span = 2 * dilation
        source, target = (first_buf, second_buf) if layer % 2 == 0 else (second_buf, first_buf)
        source[front - span : front, :] = carried_ref[offset : offset + span, :]
        state_ref[offset : offset + span, :] = source[front + slots - span : front + slots, :]
        offset += span
        for begin in range(0, slots, 256):
            rows = min(256, slots - begin)
            base = front + begin
            taps = [
                source[base - tap * dilation : base - tap * dilation + rows, :].astype(jnp.bfloat16)
                for tap in range(3)
            ]
            output = jnp.dot(
                jnp.concatenate(taps, axis=1), filters[layer], preferred_element_type=jnp.float32
            )
            mean = jnp.mean(output, axis=-1, keepdims=True)
            centred = output - mean
            spread = jnp.mean(centred * centred, axis=-1, keepdims=True)
            active = jnp.maximum(
                centred * lax.rsqrt(spread + epsilon) * gain_ref[layer : layer + 1, :], 0.0
            )
            if layer % 2 == 1:
                active = active + target[base : base + rows, :]
            active = active.astype(jnp.bfloat16)
            if layer == layers - 1:
                result[begin : begin + rows, :] = active
                copy = pltpu.make_async_copy(
                    result.at[pl.ds(begin, rows), :],
                    out_ref.at[pl.ds(first + begin, rows), :],
                    out_sems.at[len(out_copies)],
                )
                copy.start()
                out_copies.append(copy)
            else:
                target[base : base + rows, :] = active.astype(jnp.float32)
    for copy in out_copies:
        copy.wait()


def swapped(array, axis, distance):
    pairs = [(source, source ^ distance) for source in range(lax.axis_size(axis))]
    return lax.ppermute(array, axis, pairs)


def block_place(number, side):
    kind = number % 5
    bits = (2 if kind in (1, 3, 4) else 0) + number // 5
    base = 2 * (side if kind < 2 else 1 - side) + (1 if kind == 4 else 0)
    return bits, base


def ordered_filters(blocks, me):
    count = blocks[0].shape[0]
    owners = 4 * count
    quarter = blocks[0].shape[1] // 2
    layers = 4 * quarter
    whole = jnp.zeros((owners, layers) + blocks[0].shape[2:], blocks[0].dtype)
    for number, block in enumerate(blocks):
        bits, base = block_place(number, me[1])
        for shard in range(count):
            owner = me[0] ^ (4 * shard + bits)
            whole = lax.dynamic_update_slice(
                whole, block[shard][None], (owner, base * quarter, 0, 0)
            )
    return whole.transpose(1, 0, 2, 3).reshape(layers, -1, whole.shape[-1])


def carried_rows(returning, home, entry, stores):
    copies = lax.axis_size("rep")
    me = lax.axis_index("rep")
    by_position = stores.transpose(1, 0, 2)
    positions, _, channels = by_position.shape
    carried = jnp.zeros((positions, channels), stores.dtype)
    for shift in range(copies):
        arrived = by_position
        if shift:
            pairs = [(source, (source + shift) % copies) for source in range(copies)]
            arrived = lax.ppermute(by_position, "rep", pairs)
        wanted = (returning[0] > 0) & (home[0] == (me + copies - shift) % copies)
        chosen = lax.dynamic_index_in_dim(arrived, entry[0], 1, keepdims=False)
        carried = jnp.where(wanted, chosen, carried)
    return carried.astype(jnp.float32)


def local(
    bag_rows, bag_owner, bag_weight, tables, returning, home, entry, stores, conv_weight, norm_gain
):
    owners = lax.axis_size("table")
    samples_here, slot_count, bag_width = bag_rows.shape
    token_count = samples_here * slot_count
    shard_rows = tables.shape[1]
    row_width = tables.shape[2]
    channels = conv_weight.shape[-1]
    capacity = min(token_count, (3 * token_count * bag_width + 2 * owners - 1) // (2 * owners))
    cuts = [0] + [round(capacity * end) // 16 * 16 for end in part_ends]
    slot_cuts = [0] + [cuts[part] for part in stage_parts[:-1]] + [token_count]
    smem = pl.BlockSpec(memory_space=pltpu.SMEM)
    vmem = pl.BlockSpec(memory_space=pltpu.VMEM)
    anywhere = pl.BlockSpec(memory_space=pl.ANY)

    me = jnp.stack([lax.axis_index("table"), lax.axis_index("rep") % 2]).astype(jnp.int32)
    half = conv_weight.shape[0] // 2
    shard = lax.dynamic_slice_in_dim(conv_weight, me[1] * half, half, 0)
    line = [shard] + [swapped(shard, "table", 4 * step) for step in range(1, owners // 4)]
    state = carried_rows(returning, home, entry, stores)
    rows_by_slot = bag_rows.reshape(token_count, bag_width).T
    owner_by_slot = bag_owner.reshape(token_count, bag_width).T
    requests, place = pl.pallas_call(
        functools.partial(prep_kernel, cuts, shard_rows),
        out_shape=(
            jax.ShapeDtypeStruct((owners, 1, capacity), jnp.int32),
            jax.ShapeDtypeStruct((bag_width, token_count), jnp.int32),
        ),
        in_specs=[vmem, vmem],
        out_specs=(vmem, vmem),
        compiler_params=pltpu.CompilerParams(vmem_limit_bytes=8 * megabyte),
        name="prep",
    )(rows_by_slot, owner_by_slot)
    received = lax.all_to_all(requests, "table", split_axis=0, concat_axis=0, tiled=True)
    received = received.reshape(owners * capacity)
    flat_table = tables.reshape(-1, row_width)
    returned = []
    sent = []
    for number in range(len(part_ends)):
        piece = cuts[number + 1] - cuts[number]
        earlier = sent[-1:] if sent else line[1:]
        if number == 2:
            earlier = earlier + [state]
        sent.append(
            pl.pallas_call(
                functools.partial(gather_kernel, capacity, cuts[number]),
                out_shape=jax.ShapeDtypeStruct((owners, piece, row_width), jnp.bfloat16),
                in_specs=[anywhere] * (2 + len(earlier)),
                out_specs=anywhere,
                scratch_shapes=[
                    pltpu.VMEM(flat_table.shape, jnp.bfloat16),
                    pltpu.VMEM(flat_table.shape, jnp.float32),
                    pltpu.VMEM((piece, row_width), jnp.float32),
                    pltpu.VMEM((owners, piece, row_width), jnp.bfloat16),
                    pltpu.SMEM((owners * capacity,), jnp.int32),
                    pltpu.SemaphoreType.DMA,
                    pltpu.SemaphoreType.DMA((8,)),
                    pltpu.SemaphoreType.DMA((owners,)),
                ],
                compiler_params=pltpu.CompilerParams(vmem_limit_bytes=58 * megabyte),
                cost_estimate=pl.CostEstimate(
                    flops=0, bytes_accessed=20 * megabyte, transcendentals=0
                ),
                name="owner_gather",
            )(received, flat_table, *earlier)
        )
    line = tie(jnp.stack(line), sent[0])
    by_table = swapped(line, "table", 2)
    by_rep = swapped(line, "rep", 1)
    corner_low = swapped(by_rep[:, : half // 2], "table", 2)
    corner_high = swapped(by_table[:, half // 2 :], "rep", 1)
    gates = [[], [sent[2], by_table, by_rep], [corner_low, corner_high]]
    for rows, gate in zip(sent, gates):
        if returned:
            rows = tie(rows, returned[-1], *gate)
        arrived = lax.all_to_all(rows, "table", split_axis=0, concat_axis=0, tiled=True)
        returned.append(arrived.reshape(-1, row_width))
    blocks = [line, by_table, by_rep, corner_low, corner_high]
    filters = blocks + [swapped(block, "table", 1) for block in blocks]
    if conv_weight.shape[1] % 16:
        filters = [ordered_filters(filters, me)]
    weight_by_slot = bag_weight.reshape(token_count, bag_width).T
    hidden = None
    for number, part in enumerate(stage_parts):
        first, last = slot_cuts[number], slot_cuts[number + 1]
        slots = last - first
        known = [] if hidden is None else [hidden]
        pieces = returned[:part]
        hidden, state = pl.pallas_call(
            functools.partial(stage_kernel, part, len(filters), first, len(known)),
            out_shape=(
                jax.ShapeDtypeStruct((token_count, channels), jnp.bfloat16),
                jax.ShapeDtypeStruct(state.shape, jnp.float32),
            ),
            in_specs=[smem] * 2
            + [vmem] * (3 + part)
            + [anywhere] * (len(filters) + len(known)),
            out_specs=(anywhere, vmem),
            scratch_shapes=[
                pltpu.VMEM((owners * cuts[part], row_width), jnp.float32),
                pltpu.VMEM((bag_width, slots, row_width), jnp.float32),
                pltpu.VMEM((conv_weight.shape[0], 3 * channels, channels), jnp.bfloat16),
                pltpu.VMEM((slots + 16, channels), jnp.float32),
                pltpu.VMEM((slots + 16, channels), jnp.float32),
                pltpu.VMEM((slots, channels), jnp.bfloat16),
                pltpu.SemaphoreType.DMA((10 * (owners // 4),)),
                pltpu.SemaphoreType.DMA(((slots + 255) // 256,)),
            ],
            input_output_aliases={5 + part + len(filters): 0} if known else {},
            compiler_params=pltpu.CompilerParams(vmem_limit_bytes=56 * megabyte),
            cost_estimate=pl.CostEstimate(
                flops=2 * slots * 3 * channels * channels * conv_weight.shape[0],
                bytes_accessed=24 * megabyte,
                transcendentals=0,
            ),
            name="stage",
        )(place, me, weight_by_slot, state, norm_gain, *pieces, *filters, *known)
    return hidden.reshape(samples_here, slot_count, channels)


def solution(mesh):
    in_specs = (
        P(("table", "rep"), None, None),
        P(("table", "rep"), None, None),
        P(("table", "rep"), None, None),
        P(None, "table", None),
        P(("table", "rep")),
        P(("table", "rep")),
        P(("table", "rep")),
        P(("table", "rep"), None, None),
        P(None, "table", None),
        P(),
    )
    out_specs = P(("table", "rep"), None, None)
    return jax.shard_map(local, mesh=mesh, in_specs=in_specs, out_specs=out_specs, check_vma=False)
```

```python
import functools
import jax
import jax.numpy as jnp
from jax import lax
from jax.experimental import pallas as pl
from jax.experimental.pallas import tpu as pltpu
from jax.sharding import PartitionSpec as P

table_of_id = (0, 1, 2, 2, 3, 3, 3, 3)
bag_bounds = ((0, 1), (1, 2), (2, 4), (4, 8))
epsilon = 1e-05
part_ends = (0.25, 2 / 3, 1.0)
stage_parts = (2, 3)
megabyte = 1024 * 1024


def prep_kernel(cuts, shard_rows, rows_ref, owner_ref, request_ref, place_ref):
    owner = owner_ref[...]
    rows = rows_ref[...]
    owners = request_ref.shape[0]
    width, slots = owner.shape
    value_bits = (len(bag_bounds) * shard_rows).bit_length()
    owner_ids = lax.broadcasted_iota(jnp.int32, (owners, slots), 0)
    lane = lax.broadcasted_iota(jnp.int32, (owners, slots), 1)
    value = jnp.zeros((owners, slots), jnp.int32)
    for k in range(width):
        named = owner[k : k + 1, :] == owner_ids
        value = jnp.where(named, rows[k : k + 1, :] + (table_of_id[k] * shard_rows + 1), value)
    present = jnp.where(value > 0, 1, 0)
    rank = present
    step = 1
    while step < slots:
        rank = rank + jnp.where(lane >= step, pltpu.roll(rank, step, 1), 0)
        step *= 2
    rank = rank - present
    place = jnp.zeros((width, slots), jnp.int32)
    for number in range(owners):
        place = jnp.where(owner == number, rank[number : number + 1, :], place)
    landing = jnp.zeros((width, slots), jnp.int32)
    for start, stop in zip(cuts[:-1], cuts[1:]):
        where = owners * start + owner * (stop - start) + place - start
        landing = jnp.where(place >= start, where, landing)
    place_ref[...] = landing
    packed = jnp.where(value > 0, ((lane - rank) << value_bits) + value, 0)
    step = 1
    level = value_bits
    while step < slots:
        moving = jnp.where(((packed >> level) & 1) == 1, packed, 0)
        packed = (packed - moving) + pltpu.roll(moving, slots - step, 1)
        step *= 2
        level += 1
    value = jnp.maximum((packed & ((1 << value_bits) - 1)) - 1, 0)
    for number in range(owners):
        request_ref[number] = value[number : number + 1, : request_ref.shape[2]]


def pass_kernel(*refs):
    pass


def tie(array, *others):
    anywhere = pl.BlockSpec(memory_space=pl.ANY)
    return pl.pallas_call(
        pass_kernel,
        out_shape=jax.ShapeDtypeStruct(array.shape, array.dtype),
        in_specs=[anywhere] * (1 + len(others)),
        out_specs=anywhere,
        input_output_aliases={0: 0},
        name="tie",
    )(array, *others)


def gather_kernel(capacity, first, index_ref, table_ref, *refs):
    out_ref, narrow, wide, picked, packed, index, index_sem, table_sems, out_sems = refs[-9:]
    owners, piece, _ = out_ref.shape
    unroll = 32 if piece % 32 == 0 else 16
    blocks = table_sems.shape[0]
    block_rows = table_ref.shape[0] // blocks
    table_copies = []
    for block in range(blocks):
        part = pl.ds(block * block_rows, block_rows)
        copy = pltpu.make_async_copy(table_ref.at[part, :], narrow.at[part, :], table_sems.at[block])
        copy.start()
        table_copies.append(copy)
    index_copy = pltpu.make_async_copy(index_ref, index, index_sem)
    index_copy.start()
    rows = 256

    for block in range(blocks):
        table_copies[block].wait()

        def widen(step, carry, block=block):
            base = pl.multiple_of(block * block_rows + step * rows, rows)
            wide[pl.ds(base, rows), :] = narrow[pl.ds(base, rows), :].astype(jnp.float32)
            return carry

        lax.fori_loop(0, block_rows // rows, widen, 0)
    index_copy.wait()
    copies = []
    for number in range(owners):
        origin = number * capacity + first

        def some_rows(block, carry, origin=origin):
            base = pl.multiple_of(block * unroll, unroll)
            picks = [index[origin + base + i] for i in range(unroll)]
            found = [wide[pl.ds(pick, 1), :] for pick in picks]
            for i in range(unroll):
                picked[pl.ds(base + i, 1), :] = found[i]
            return carry

        lax.fori_loop(0, piece // unroll, some_rows, 0)
        packed[number] = picked[...].astype(jnp.bfloat16)
        copy = pltpu.make_async_copy(packed.at[number], out_ref.at[number], out_sems.at[number])
        copy.start()
        copies.append(copy)
    for copy in copies:
        copy.wait()


def stage_kernel(
    pieces, sources, first, aliased, place_ref, me_ref, weight_ref, carried_ref, gain_ref, *refs
):
    piece_refs = refs[:pieces]
    filter_refs = refs[pieces : pieces + sources]
    refs = refs[pieces + sources + aliased :]
    out_ref, state_ref, table, picked, filters, first_buf, second_buf, result = refs[:8]
    filter_sems, out_sems = refs[8:]
    width, slots, lanes = picked.shape
    layers = filters.shape[0]
    filter_copies = []
    if sources == 1:
        filter_copies.append(pltpu.make_async_copy(filter_refs[0], filters, filter_sems.at[0]))
    else:
        held, half, depth, _ = filter_refs[0].shape
        for group, filter_ref in enumerate(filter_refs):
            bits, base = block_place(group, me_ref[1])
            for number in range(held):
                owner = me_ref[0] ^ (4 * number + bits)
                rows = pl.ds(pl.multiple_of(owner * depth, depth), depth)
                layer = pl.ds(base * (half // 2), filter_ref.shape[1])
                filter_copies.append(
                    pltpu.make_async_copy(
                        filter_ref.at[number],
                        filters.at[layer, rows, :],
                        filter_sems.at[group * held + number],
                    )
                )
    for copy in filter_copies:
        copy.start()
    start = 0
    for piece_ref in piece_refs:
        count = piece_ref.shape[0]
        rows = 256

        def widen(step, carry, piece_ref=piece_ref, start=start):
            base = pl.multiple_of(step * rows, rows)
            table[pl.ds(start + base, rows), :] = piece_ref[pl.ds(base, rows), :].astype(jnp.float32)
            return carry

        lax.fori_loop(0, count // rows, widen, 0)
        start += count

    def some_slots(step, carry):
        base = pl.multiple_of(step * 8, 8)
        for k in range(width):
            picks = [place_ref[k, first + base + i] for i in range(8)]
            rows = [table[pl.ds(pick, 1), :] for pick in picks]
            for i in range(8):
                picked[k, pl.ds(base + i, 1), :] = rows[i]
        return carry

    lax.fori_loop(0, slots // 8, some_slots, 0)
    front = 16
    weights = jnp.transpose(weight_ref[:, first : first + slots])
    for t, (lower, upper) in enumerate(bag_bounds):
        total = picked[lower] * weights[:, lower : lower + 1]
        for k in range(lower + 1, upper):
            total = total + picked[k] * weights[:, k : k + 1]
        total = total.astype(jnp.bfloat16).astype(jnp.float32)
        first_buf[front:, t * lanes : (t + 1) * lanes] = total

    for copy in filter_copies:
        copy.wait()
    offset = 0
    out_copies = []
    for layer in range(layers):
        dilation = 2**layer
        span = 2 * dilation
        source, target = (first_buf, second_buf) if layer % 2 == 0 else (second_buf, first_buf)
        source[front - span : front, :] = carried_ref[offset : offset + span, :]
        state_ref[offset : offset + span, :] = source[front + slots - span : front + slots, :]
        offset += span
        for begin in range(0, slots, 256):
            rows = min(256, slots - begin)
            base = front + begin
            taps = [
                source[base - tap * dilation : base - tap * dilation + rows, :].astype(jnp.bfloat16)
                for tap in range(3)
            ]
            output = jnp.dot(
                jnp.concatenate(taps, axis=1), filters[layer], preferred_element_type=jnp.float32
            )
            mean = jnp.mean(output, axis=-1, keepdims=True)
            centred = output - mean
            spread = jnp.mean(centred * centred, axis=-1, keepdims=True)
            active = jnp.maximum(
                centred * lax.rsqrt(spread + epsilon) * gain_ref[layer : layer + 1, :], 0.0
            )
            if layer % 2 == 1:
                active = active + target[base : base + rows, :]
            active = active.astype(jnp.bfloat16)
            if layer == layers - 1:
                result[begin : begin + rows, :] = active
                copy = pltpu.make_async_copy(
                    result.at[pl.ds(begin, rows), :],
                    out_ref.at[pl.ds(first + begin, rows), :],
                    out_sems.at[len(out_copies)],
                )
                copy.start()
                out_copies.append(copy)
            else:
                target[base : base + rows, :] = active.astype(jnp.float32)
    for copy in out_copies:
        copy.wait()


def swapped(array, axis, distance):
    pairs = [(source, source ^ distance) for source in range(lax.axis_size(axis))]
    return lax.ppermute(array, axis, pairs)


def block_place(number, side):
    kind = number % 5
    bits = (2 if kind in (1, 3, 4) else 0) + number // 5
    base = 2 * (side if kind < 2 else 1 - side) + (1 if kind == 4 else 0)
    return bits, base


def ordered_filters(blocks, me):
    count = blocks[0].shape[0]
    owners = 4 * count
    quarter = blocks[0].shape[1] // 2
    layers = 4 * quarter
    whole = jnp.zeros((owners, layers) + blocks[0].shape[2:], blocks[0].dtype)
    for number, block in enumerate(blocks):
        bits, base = block_place(number, me[1])
        for shard in range(count):
            owner = me[0] ^ (4 * shard + bits)
            whole = lax.dynamic_update_slice(
                whole, block[shard][None], (owner, base * quarter, 0, 0)
            )
    return whole.transpose(1, 0, 2, 3).reshape(layers, -1, whole.shape[-1])


def carried_rows(returning, home, entry, stores):
    copies = lax.axis_size("rep")
    me = lax.axis_index("rep")
    by_position = stores.transpose(1, 0, 2)
    positions, _, channels = by_position.shape
    carried = jnp.zeros((positions, channels), stores.dtype)
    for shift in range(copies):
        arrived = by_position
        if shift:
            pairs = [(source, (source + shift) % copies) for source in range(copies)]
            arrived = lax.ppermute(by_position, "rep", pairs)
        wanted = (returning[0] > 0) & (home[0] == (me + copies - shift) % copies)
        chosen = lax.dynamic_index_in_dim(arrived, entry[0], 1, keepdims=False)
        carried = jnp.where(wanted, chosen, carried)
    return carried.astype(jnp.float32)


def local(
    bag_rows, bag_owner, bag_weight, tables, returning, home, entry, stores, conv_weight, norm_gain
):
    owners = lax.axis_size("table")
    samples_here, slot_count, bag_width = bag_rows.shape
    token_count = samples_here * slot_count
    shard_rows = tables.shape[1]
    row_width = tables.shape[2]
    channels = conv_weight.shape[-1]
    capacity = min(token_count, (3 * token_count * bag_width + 2 * owners - 1) // (2 * owners))
    cuts = [0] + [round(capacity * end) // 16 * 16 for end in part_ends]
    slot_cuts = [0] + [cuts[part] for part in stage_parts[:-1]] + [token_count]
    smem = pl.BlockSpec(memory_space=pltpu.SMEM)
    vmem = pl.BlockSpec(memory_space=pltpu.VMEM)
    anywhere = pl.BlockSpec(memory_space=pl.ANY)

    me = jnp.stack([lax.axis_index("table"), lax.axis_index("rep") % 2]).astype(jnp.int32)
    half = conv_weight.shape[0] // 2
    shard = lax.dynamic_slice_in_dim(conv_weight, me[1] * half, half, 0)
    middle = owners // 8
    line = [shard] + [swapped(shard, "table", 4 * step) for step in range(1, middle + 1)]
    state = carried_rows(returning, home, entry, stores)
    rows_by_slot = bag_rows.reshape(token_count, bag_width).T
    owner_by_slot = bag_owner.reshape(token_count, bag_width).T
    requests, place = pl.pallas_call(
        functools.partial(prep_kernel, cuts, shard_rows),
        out_shape=(
            jax.ShapeDtypeStruct((owners, 1, capacity), jnp.int32),
            jax.ShapeDtypeStruct((bag_width, token_count), jnp.int32),
        ),
        in_specs=[vmem, vmem],
        out_specs=(vmem, vmem),
        compiler_params=pltpu.CompilerParams(vmem_limit_bytes=8 * megabyte),
        name="prep",
    )(rows_by_slot, owner_by_slot)
    received = lax.all_to_all(requests, "table", split_axis=0, concat_axis=0, tiled=True)
    received = received.reshape(owners * capacity)
    flat_table = tables.reshape(-1, row_width)
    returned = []
    sent = []
    for number in range(len(part_ends)):
        piece = cuts[number + 1] - cuts[number]
        if number == 1:
            line = line + [swapped(line[middle], "table", 4 * step) for step in range(1, middle)]
            sent[0] = tie(sent[0], *line[middle + 1 :])
        earlier = sent[-1:] if sent else line[1:]
        sent.append(
            pl.pallas_call(
                functools.partial(gather_kernel, capacity, cuts[number]),
                out_shape=jax.ShapeDtypeStruct((owners, piece, row_width), jnp.bfloat16),
                in_specs=[anywhere] * (2 + len(earlier)),
                out_specs=anywhere,
                scratch_shapes=[
                    pltpu.VMEM(flat_table.shape, jnp.bfloat16),
                    pltpu.VMEM(flat_table.shape, jnp.float32),
                    pltpu.VMEM((piece, row_width), jnp.float32),
                    pltpu.VMEM((owners, piece, row_width), jnp.bfloat16),
                    pltpu.SMEM((owners * capacity,), jnp.int32),
                    pltpu.SemaphoreType.DMA,
                    pltpu.SemaphoreType.DMA((8,)),
                    pltpu.SemaphoreType.DMA((owners,)),
                ],
                compiler_params=pltpu.CompilerParams(vmem_limit_bytes=58 * megabyte),
                cost_estimate=pl.CostEstimate(
                    flops=0, bytes_accessed=20 * megabyte, transcendentals=0
                ),
                name="owner_gather",
            )(received, flat_table, *earlier)
        )
    line = tie(jnp.stack(line), sent[0])
    by_table = swapped(line, "table", 2)
    by_rep = swapped(line, "rep", 1)
    corner_low = swapped(by_rep[:, : half // 2], "table", 2)
    corner_high = swapped(by_table[:, half // 2 :], "rep", 1)
    near = [swapped(block, "table", 1) for block in (line, by_table, by_rep)]
    gates = [[], [sent[2], by_table, by_rep], [state, corner_low, corner_high] + near]
    for rows, gate in zip(sent, gates):
        if returned:
            rows = tie(rows, returned[-1], *gate)
        arrived = lax.all_to_all(rows, "table", split_axis=0, concat_axis=0, tiled=True)
        returned.append(arrived.reshape(-1, row_width))
    near = near + [swapped(block, "table", 1) for block in (corner_low, corner_high)]
    filters = [line, by_table, by_rep, corner_low, corner_high] + near
    if conv_weight.shape[1] % 16:
        filters = [ordered_filters(filters, me)]
    weight_by_slot = bag_weight.reshape(token_count, bag_width).T
    hidden = None
    for number, part in enumerate(stage_parts):
        first, last = slot_cuts[number], slot_cuts[number + 1]
        slots = last - first
        known = [] if hidden is None else [hidden]
        pieces = returned[:part]
        hidden, state = pl.pallas_call(
            functools.partial(stage_kernel, part, len(filters), first, len(known)),
            out_shape=(
                jax.ShapeDtypeStruct((token_count, channels), jnp.bfloat16),
                jax.ShapeDtypeStruct(state.shape, jnp.float32),
            ),
            in_specs=[smem] * 2
            + [vmem] * (3 + part)
            + [anywhere] * (len(filters) + len(known)),
            out_specs=(anywhere, vmem),
            scratch_shapes=[
                pltpu.VMEM((owners * cuts[part], row_width), jnp.float32),
                pltpu.VMEM((bag_width, slots, row_width), jnp.float32),
                pltpu.VMEM((conv_weight.shape[0], 3 * channels, channels), jnp.bfloat16),
                pltpu.VMEM((slots + 16, channels), jnp.float32),
                pltpu.VMEM((slots + 16, channels), jnp.float32),
                pltpu.VMEM((slots, channels), jnp.bfloat16),
                pltpu.SemaphoreType.DMA((10 * (owners // 4),)),
                pltpu.SemaphoreType.DMA(((slots + 255) // 256,)),
            ],
            input_output_aliases={5 + part + len(filters): 0} if known else {},
            compiler_params=pltpu.CompilerParams(vmem_limit_bytes=56 * megabyte),
            cost_estimate=pl.CostEstimate(
                flops=2 * slots * 3 * channels * channels * conv_weight.shape[0],
                bytes_accessed=24 * megabyte,
                transcendentals=0,
            ),
            name="stage",
        )(place, me, weight_by_slot, state, norm_gain, *pieces, *filters, *known)
    return hidden.reshape(samples_here, slot_count, channels)


def solution(mesh):
    in_specs = (
        P(("table", "rep"), None, None),
        P(("table", "rep"), None, None),
        P(("table", "rep"), None, None),
        P(None, "table", None),
        P(("table", "rep")),
        P(("table", "rep")),
        P(("table", "rep")),
        P(("table", "rep"), None, None),
        P(None, "table", None),
        P(),
    )
    out_specs = P(("table", "rep"), None, None)
    return jax.shard_map(local, mesh=mesh, in_specs=in_specs, out_specs=out_specs, check_vma=False)
```

```python
import functools
import jax
import jax.numpy as jnp
from jax import lax
from jax.experimental import pallas as pl
from jax.experimental.pallas import tpu as pltpu
from jax.sharding import PartitionSpec as P

table_of_id = (0, 1, 2, 2, 3, 3, 3, 3)
bag_bounds = ((0, 1), (1, 2), (2, 4), (4, 8))
epsilon = 1e-05
part_ends = (0.25, 0.75, 1.0)
stage_parts = (2, 3)
megabyte = 1024 * 1024


def prep_kernel(cuts, shard_rows, rows_ref, owner_ref, request_ref, place_ref):
    owner = owner_ref[...]
    rows = rows_ref[...]
    owners = request_ref.shape[0]
    width, slots = owner.shape
    value_bits = (len(bag_bounds) * shard_rows).bit_length()
    owner_ids = lax.broadcasted_iota(jnp.int32, (owners, slots), 0)
    lane = lax.broadcasted_iota(jnp.int32, (owners, slots), 1)
    value = jnp.zeros((owners, slots), jnp.int32)
    for k in range(width):
        named = owner[k : k + 1, :] == owner_ids
        value = jnp.where(named, rows[k : k + 1, :] + (table_of_id[k] * shard_rows + 1), value)
    present = jnp.where(value > 0, 1, 0)
    rank = present
    step = 1
    while step < slots:
        rank = rank + jnp.where(lane >= step, pltpu.roll(rank, step, 1), 0)
        step *= 2
    rank = rank - present
    place = jnp.zeros((width, slots), jnp.int32)
    for number in range(owners):
        place = jnp.where(owner == number, rank[number : number + 1, :], place)
    landing = jnp.zeros((width, slots), jnp.int32)
    for start, stop in zip(cuts[:-1], cuts[1:]):
        where = owners * start + owner * (stop - start) + place - start
        landing = jnp.where(place >= start, where, landing)
    place_ref[...] = landing
    packed = jnp.where(value > 0, ((lane - rank) << value_bits) + value, 0)
    step = 1
    level = value_bits
    while step < slots:
        moving = jnp.where(((packed >> level) & 1) == 1, packed, 0)
        packed = (packed - moving) + pltpu.roll(moving, slots - step, 1)
        step *= 2
        level += 1
    value = jnp.maximum((packed & ((1 << value_bits) - 1)) - 1, 0)
    for number in range(owners):
        request_ref[number] = value[number : number + 1, : request_ref.shape[2]]


def pass_kernel(*refs):
    pass


def tie(array, *others):
    anywhere = pl.BlockSpec(memory_space=pl.ANY)
    return pl.pallas_call(
        pass_kernel,
        out_shape=jax.ShapeDtypeStruct(array.shape, array.dtype),
        in_specs=[anywhere] * (1 + len(others)),
        out_specs=anywhere,
        input_output_aliases={0: 0},
        name="tie",
    )(array, *others)


def gather_kernel(capacity, first, index_ref, table_ref, *refs):
    out_ref, narrow, wide, picked, packed, index, index_sem, table_sems, out_sems = refs[-9:]
    owners, piece, _ = out_ref.shape
    unroll = 32 if piece % 32 == 0 else 16
    blocks = table_sems.shape[0]
    block_rows = table_ref.shape[0] // blocks
    table_copies = []
    for block in range(blocks):
        part = pl.ds(block * block_rows, block_rows)
        copy = pltpu.make_async_copy(table_ref.at[part, :], narrow.at[part, :], table_sems.at[block])
        copy.start()
        table_copies.append(copy)
    index_copy = pltpu.make_async_copy(index_ref, index, index_sem)
    index_copy.start()
    rows = 256

    for block in range(blocks):
        table_copies[block].wait()

        def widen(step, carry, block=block):
            base = pl.multiple_of(block * block_rows + step * rows, rows)
            wide[pl.ds(base, rows), :] = narrow[pl.ds(base, rows), :].astype(jnp.float32)
            return carry

        lax.fori_loop(0, block_rows // rows, widen, 0)
    index_copy.wait()
    copies = []
    for number in range(owners):
        origin = number * capacity + first

        def some_rows(block, carry, origin=origin):
            base = pl.multiple_of(block * unroll, unroll)
            picks = [index[origin + base + i] for i in range(unroll)]
            found = [wide[pl.ds(pick, 1), :] for pick in picks]
            for i in range(unroll):
                picked[pl.ds(base + i, 1), :] = found[i]
            return carry

        lax.fori_loop(0, piece // unroll, some_rows, 0)
        packed[number] = picked[...].astype(jnp.bfloat16)
        copy = pltpu.make_async_copy(packed.at[number], out_ref.at[number], out_sems.at[number])
        copy.start()
        copies.append(copy)
    for copy in copies:
        copy.wait()


def stage_kernel(
    pieces, sources, first, aliased, place_ref, me_ref, weight_ref, carried_ref, gain_ref, *refs
):
    piece_refs = refs[:pieces]
    filter_refs = refs[pieces : pieces + sources]
    refs = refs[pieces + sources + aliased :]
    out_ref, state_ref, table, picked, filters, first_buf, second_buf, result = refs[:8]
    filter_sems, out_sems = refs[8:]
    width, slots, lanes = picked.shape
    layers = filters.shape[0]
    filter_copies = []
    if sources == 1:
        filter_copies.append(pltpu.make_async_copy(filter_refs[0], filters, filter_sems.at[0]))
    else:
        held, half, depth, _ = filter_refs[0].shape
        for group, filter_ref in enumerate(filter_refs):
            bits, base = block_place(group, me_ref[1])
            for number in range(held):
                owner = me_ref[0] ^ (4 * number + bits)
                rows = pl.ds(pl.multiple_of(owner * depth, depth), depth)
                layer = pl.ds(base * (half // 2), filter_ref.shape[1])
                filter_copies.append(
                    pltpu.make_async_copy(
                        filter_ref.at[number],
                        filters.at[layer, rows, :],
                        filter_sems.at[group * held + number],
                    )
                )
    for copy in filter_copies:
        copy.start()
    start = 0
    for piece_ref in piece_refs:
        count = piece_ref.shape[0]
        rows = 256

        def widen(step, carry, piece_ref=piece_ref, start=start):
            base = pl.multiple_of(step * rows, rows)
            table[pl.ds(start + base, rows), :] = piece_ref[pl.ds(base, rows), :].astype(jnp.float32)
            return carry

        lax.fori_loop(0, count // rows, widen, 0)
        start += count

    def some_slots(step, carry):
        base = pl.multiple_of(step * 8, 8)
        for k in range(width):
            picks = [place_ref[k, first + base + i] for i in range(8)]
            rows = [table[pl.ds(pick, 1), :] for pick in picks]
            for i in range(8):
                picked[k, pl.ds(base + i, 1), :] = rows[i]
        return carry

    lax.fori_loop(0, slots // 8, some_slots, 0)
    front = 16
    weights = jnp.transpose(weight_ref[:, first : first + slots])
    for t, (lower, upper) in enumerate(bag_bounds):
        total = picked[lower] * weights[:, lower : lower + 1]
        for k in range(lower + 1, upper):
            total = total + picked[k] * weights[:, k : k + 1]
        total = total.astype(jnp.bfloat16).astype(jnp.float32)
        first_buf[front:, t * lanes : (t + 1) * lanes] = total

    for copy in filter_copies:
        copy.wait()
    offset = 0
    out_copies = []
    for layer in range(layers):
        dilation = 2**layer
        span = 2 * dilation
        source, target = (first_buf, second_buf) if layer % 2 == 0 else (second_buf, first_buf)
        source[front - span : front, :] = carried_ref[offset : offset + span, :]
        state_ref[offset : offset + span, :] = source[front + slots - span : front + slots, :]
        offset += span
        for begin in range(0, slots, 256):
            rows = min(256, slots - begin)
            base = front + begin
            taps = [
                source[base - tap * dilation : base - tap * dilation + rows, :].astype(jnp.bfloat16)
                for tap in range(3)
            ]
            output = jnp.dot(
                jnp.concatenate(taps, axis=1), filters[layer], preferred_element_type=jnp.float32
            )
            mean = jnp.mean(output, axis=-1, keepdims=True)
            centred = output - mean
            spread = jnp.mean(centred * centred, axis=-1, keepdims=True)
            active = jnp.maximum(
                centred * lax.rsqrt(spread + epsilon) * gain_ref[layer : layer + 1, :], 0.0
            )
            if layer % 2 == 1:
                active = active + target[base : base + rows, :]
            active = active.astype(jnp.bfloat16)
            if layer == layers - 1:
                result[begin : begin + rows, :] = active
                copy = pltpu.make_async_copy(
                    result.at[pl.ds(begin, rows), :],
                    out_ref.at[pl.ds(first + begin, rows), :],
                    out_sems.at[len(out_copies)],
                )
                copy.start()
                out_copies.append(copy)
            else:
                target[base : base + rows, :] = active.astype(jnp.float32)
    for copy in out_copies:
        copy.wait()


def swapped(array, axis, distance):
    pairs = [(source, source ^ distance) for source in range(lax.axis_size(axis))]
    return lax.ppermute(array, axis, pairs)


def block_place(number, side):
    kind = number % 6
    bits = (2 if kind > 1 else 0) + number // 6
    base = 2 * (side if kind in (0, 2, 3) else 1 - side) + (1 if kind in (3, 5) else 0)
    return bits, base


def ordered_filters(blocks, me):
    count = blocks[0].shape[0]
    owners = 4 * count
    quarter = blocks[0].shape[1] // 2
    layers = 4 * quarter
    whole = jnp.zeros((owners, layers) + blocks[0].shape[2:], blocks[0].dtype)
    for number, block in enumerate(blocks):
        bits, base = block_place(number, me[1])
        for shard in range(count):
            owner = me[0] ^ (4 * shard + bits)
            whole = lax.dynamic_update_slice(
                whole, block[shard][None], (owner, base * quarter, 0, 0)
            )
    return whole.transpose(1, 0, 2, 3).reshape(layers, -1, whole.shape[-1])


def carried_rows(returning, home, entry, stores):
    copies = lax.axis_size("rep")
    me = lax.axis_index("rep")
    by_position = stores.transpose(1, 0, 2)
    positions, _, channels = by_position.shape
    carried = jnp.zeros((positions, channels), stores.dtype)
    for shift in range(copies):
        arrived = by_position
        if shift:
            pairs = [(source, (source + shift) % copies) for source in range(copies)]
            arrived = lax.ppermute(by_position, "rep", pairs)
        wanted = (returning[0] > 0) & (home[0] == (me + copies - shift) % copies)
        chosen = lax.dynamic_index_in_dim(arrived, entry[0], 1, keepdims=False)
        carried = jnp.where(wanted, chosen, carried)
    return carried.astype(jnp.float32)


def local(
    bag_rows, bag_owner, bag_weight, tables, returning, home, entry, stores, conv_weight, norm_gain
):
    owners = lax.axis_size("table")
    samples_here, slot_count, bag_width = bag_rows.shape
    token_count = samples_here * slot_count
    shard_rows = tables.shape[1]
    row_width = tables.shape[2]
    channels = conv_weight.shape[-1]
    capacity = min(token_count, (3 * token_count * bag_width + 2 * owners - 1) // (2 * owners))
    cuts = [0] + [round(capacity * end) // 16 * 16 for end in part_ends]
    slot_cuts = [0] + [cuts[part] for part in stage_parts[:-1]] + [token_count]
    smem = pl.BlockSpec(memory_space=pltpu.SMEM)
    vmem = pl.BlockSpec(memory_space=pltpu.VMEM)
    anywhere = pl.BlockSpec(memory_space=pl.ANY)

    me = jnp.stack([lax.axis_index("table"), lax.axis_index("rep") % 2]).astype(jnp.int32)
    half = conv_weight.shape[0] // 2
    shard = lax.dynamic_slice_in_dim(conv_weight, me[1] * half, half, 0)
    middle = owners // 8
    line = [shard] + [swapped(shard, "table", 4 * step) for step in range(1, middle + 1)]
    state = carried_rows(returning, home, entry, stores)
    rows_by_slot = bag_rows.reshape(token_count, bag_width).T
    owner_by_slot = bag_owner.reshape(token_count, bag_width).T
    requests, place = pl.pallas_call(
        functools.partial(prep_kernel, cuts, shard_rows),
        out_shape=(
            jax.ShapeDtypeStruct((owners, 1, capacity), jnp.int32),
            jax.ShapeDtypeStruct((bag_width, token_count), jnp.int32),
        ),
        in_specs=[vmem, vmem],
        out_specs=(vmem, vmem),
        compiler_params=pltpu.CompilerParams(vmem_limit_bytes=8 * megabyte),
        name="prep",
    )(rows_by_slot, owner_by_slot)
    received = lax.all_to_all(requests, "table", split_axis=0, concat_axis=0, tiled=True)
    received = received.reshape(owners * capacity)
    flat_table = tables.reshape(-1, row_width)
    returned = []
    sent = []
    for number in range(len(part_ends)):
        piece = cuts[number + 1] - cuts[number]
        if number == 1:
            middle_shard = tie(line[middle], received)
            line = line + [swapped(middle_shard, "table", 4 * step) for step in range(1, middle)]
            line[middle] = middle_shard
            sent[0] = tie(sent[0], *line[middle + 1 :])
        earlier = sent[-1:] if sent else line[1:]
        sent.append(
            pl.pallas_call(
                functools.partial(gather_kernel, capacity, cuts[number]),
                out_shape=jax.ShapeDtypeStruct((owners, piece, row_width), jnp.bfloat16),
                in_specs=[anywhere] * (2 + len(earlier)),
                out_specs=anywhere,
                scratch_shapes=[
                    pltpu.VMEM(flat_table.shape, jnp.bfloat16),
                    pltpu.VMEM(flat_table.shape, jnp.float32),
                    pltpu.VMEM((piece, row_width), jnp.float32),
                    pltpu.VMEM((owners, piece, row_width), jnp.bfloat16),
                    pltpu.SMEM((owners * capacity,), jnp.int32),
                    pltpu.SemaphoreType.DMA,
                    pltpu.SemaphoreType.DMA((8,)),
                    pltpu.SemaphoreType.DMA((owners,)),
                ],
                compiler_params=pltpu.CompilerParams(vmem_limit_bytes=58 * megabyte),
                cost_estimate=pl.CostEstimate(
                    flops=0, bytes_accessed=20 * megabyte, transcendentals=0
                ),
                name="owner_gather",
            )(received, flat_table, *earlier)
        )
    line = tie(jnp.stack(line), sent[0])
    by_rep = swapped(line, "rep", 1)
    table_low = swapped(line[:, : half // 2], "table", 2)
    table_high = swapped(line[:, half // 2 :], "table", 2)
    corner_low = swapped(table_low, "rep", 1)
    corner_high = swapped(table_high, "rep", 1)
    near = [swapped(block, "table", 1) for block in (line, by_rep, table_low)]
    gates = [[], [sent[2], by_rep, table_low], [state, corner_low, corner_high] + near]
    for rows, gate in zip(sent, gates):
        if returned:
            rows = tie(rows, returned[-1], *gate)
        arrived = lax.all_to_all(rows, "table", split_axis=0, concat_axis=0, tiled=True)
        returned.append(arrived.reshape(-1, row_width))
    late = [table_high, corner_low, corner_high]
    filters = [line, by_rep, table_low] + late + near
    filters = filters + [swapped(block, "table", 1) for block in late]
    if conv_weight.shape[1] % 16:
        filters = [ordered_filters(filters, me)]
    weight_by_slot = bag_weight.reshape(token_count, bag_width).T
    hidden = None
    for number, part in enumerate(stage_parts):
        first, last = slot_cuts[number], slot_cuts[number + 1]
        slots = last - first
        known = [] if hidden is None else [hidden]
        pieces = returned[:part]
        hidden, state = pl.pallas_call(
            functools.partial(stage_kernel, part, len(filters), first, len(known)),
            out_shape=(
                jax.ShapeDtypeStruct((token_count, channels), jnp.bfloat16),
                jax.ShapeDtypeStruct(state.shape, jnp.float32),
            ),
            in_specs=[smem] * 2
            + [vmem] * (3 + part)
            + [anywhere] * (len(filters) + len(known)),
            out_specs=(anywhere, vmem),
            scratch_shapes=[
                pltpu.VMEM((owners * cuts[part], row_width), jnp.float32),
                pltpu.VMEM((bag_width, slots, row_width), jnp.float32),
                pltpu.VMEM((conv_weight.shape[0], 3 * channels, channels), jnp.bfloat16),
                pltpu.VMEM((slots + 16, channels), jnp.float32),
                pltpu.VMEM((slots + 16, channels), jnp.float32),
                pltpu.VMEM((slots, channels), jnp.bfloat16),
                pltpu.SemaphoreType.DMA((12 * (owners // 4),)),
                pltpu.SemaphoreType.DMA(((slots + 255) // 256,)),
            ],
            input_output_aliases={5 + part + len(filters): 0} if known else {},
            compiler_params=pltpu.CompilerParams(vmem_limit_bytes=56 * megabyte),
            cost_estimate=pl.CostEstimate(
                flops=2 * slots * 3 * channels * channels * conv_weight.shape[0],
                bytes_accessed=24 * megabyte,
                transcendentals=0,
            ),
            name="stage",
        )(place, me, weight_by_slot, state, norm_gain, *pieces, *filters, *known)
    return hidden.reshape(samples_here, slot_count, channels)


def solution(mesh):
    in_specs = (
        P(("table", "rep"), None, None),
        P(("table", "rep"), None, None),
        P(("table", "rep"), None, None),
        P(None, "table", None),
        P(("table", "rep")),
        P(("table", "rep")),
        P(("table", "rep")),
        P(("table", "rep"), None, None),
        P(None, "table", None),
        P(),
    )
    out_specs = P(("table", "rep"), None, None)
    return jax.shard_map(local, mesh=mesh, in_specs=in_specs, out_specs=out_specs, check_vma=False)
```

```python
import functools
import jax
import jax.numpy as jnp
from jax import lax
from jax.experimental import pallas as pl
from jax.experimental.pallas import tpu as pltpu
from jax.sharding import PartitionSpec as P

table_of_id = (0, 1, 2, 2, 3, 3, 3, 3)
bag_bounds = ((0, 1), (1, 2), (2, 4), (4, 8))
epsilon = 1e-05
part_ends = (0.25, 0.75, 1.0)
stage_parts = (2, 3)
megabyte = 1024 * 1024


def prep_kernel(cuts, shard_rows, rows_ref, owner_ref, request_ref, place_ref):
    owner = owner_ref[...]
    rows = rows_ref[...]
    owners = request_ref.shape[0]
    width, slots = owner.shape
    value_bits = (len(bag_bounds) * shard_rows).bit_length()
    owner_ids = lax.broadcasted_iota(jnp.int32, (owners, slots), 0)
    lane = lax.broadcasted_iota(jnp.int32, (owners, slots), 1)
    value = jnp.zeros((owners, slots), jnp.int32)
    for k in range(width):
        named = owner[k : k + 1, :] == owner_ids
        value = jnp.where(named, rows[k : k + 1, :] + (table_of_id[k] * shard_rows + 1), value)
    present = jnp.where(value > 0, 1, 0)
    rank = present
    step = 1
    while step < slots:
        rank = rank + jnp.where(lane >= step, pltpu.roll(rank, step, 1), 0)
        step *= 2
    rank = rank - present
    place = jnp.zeros((width, slots), jnp.int32)
    for number in range(owners):
        place = jnp.where(owner == number, rank[number : number + 1, :], place)
    landing = jnp.zeros((width, slots), jnp.int32)
    for start, stop in zip(cuts[:-1], cuts[1:]):
        where = owners * start + owner * (stop - start) + place - start
        landing = jnp.where(place >= start, where, landing)
    place_ref[...] = landing
    packed = jnp.where(value > 0, ((lane - rank) << value_bits) + value, 0)
    step = 1
    level = value_bits
    while step < slots:
        moving = jnp.where(((packed >> level) & 1) == 1, packed, 0)
        packed = (packed - moving) + pltpu.roll(moving, slots - step, 1)
        step *= 2
        level += 1
    value = jnp.maximum((packed & ((1 << value_bits) - 1)) - 1, 0)
    for number in range(owners):
        request_ref[number] = value[number : number + 1, : request_ref.shape[2]]


def pass_kernel(*refs):
    pass


def tie(array, *others):
    anywhere = pl.BlockSpec(memory_space=pl.ANY)
    return pl.pallas_call(
        pass_kernel,
        out_shape=jax.ShapeDtypeStruct(array.shape, array.dtype),
        in_specs=[anywhere] * (1 + len(others)),
        out_specs=anywhere,
        input_output_aliases={0: 0},
        name="tie",
    )(array, *others)


def gather_kernel(capacity, first, index_ref, table_ref, *refs):
    out_ref, narrow, wide, picked, packed, index, index_sem, table_sems, out_sems = refs[-9:]
    owners, piece, _ = out_ref.shape
    unroll = 32 if piece % 32 == 0 else 16
    blocks = table_sems.shape[0]
    block_rows = table_ref.shape[0] // blocks
    table_copies = []
    for block in range(blocks):
        part = pl.ds(block * block_rows, block_rows)
        copy = pltpu.make_async_copy(table_ref.at[part, :], narrow.at[part, :], table_sems.at[block])
        copy.start()
        table_copies.append(copy)
    index_copy = pltpu.make_async_copy(index_ref, index, index_sem)
    index_copy.start()
    rows = 256

    for block in range(blocks):
        table_copies[block].wait()

        def widen(step, carry, block=block):
            base = pl.multiple_of(block * block_rows + step * rows, rows)
            wide[pl.ds(base, rows), :] = narrow[pl.ds(base, rows), :].astype(jnp.float32)
            return carry

        lax.fori_loop(0, block_rows // rows, widen, 0)
    index_copy.wait()
    copies = []
    for number in range(owners):
        origin = number * capacity + first

        def some_rows(block, carry, origin=origin):
            base = pl.multiple_of(block * unroll, unroll)
            picks = [index[origin + base + i] for i in range(unroll)]
            found = [wide[pl.ds(pick, 1), :] for pick in picks]
            for i in range(unroll):
                picked[pl.ds(base + i, 1), :] = found[i]
            return carry

        lax.fori_loop(0, piece // unroll, some_rows, 0)
        packed[number] = picked[...].astype(jnp.bfloat16)
        copy = pltpu.make_async_copy(packed.at[number], out_ref.at[number], out_sems.at[number])
        copy.start()
        copies.append(copy)
    for copy in copies:
        copy.wait()


def pool_slots(first, place_ref, weight_ref, piece_refs, table, picked, put):
    width, slots, lanes = picked.shape
    start = 0
    for piece_ref in piece_refs:
        count = piece_ref.shape[0]
        rows = 256

        def widen(step, carry, piece_ref=piece_ref, start=start):
            base = pl.multiple_of(step * rows, rows)
            table[pl.ds(start + base, rows), :] = piece_ref[pl.ds(base, rows), :].astype(jnp.float32)
            return carry

        lax.fori_loop(0, count // rows, widen, 0)
        start += count

    def some_slots(step, carry):
        base = pl.multiple_of(step * 8, 8)
        for k in range(width):
            picks = [place_ref[k, first + base + i] for i in range(8)]
            rows = [table[pl.ds(pick, 1), :] for pick in picks]
            for i in range(8):
                picked[k, pl.ds(base + i, 1), :] = rows[i]
        return carry

    lax.fori_loop(0, slots // 8, some_slots, 0)
    weights = jnp.transpose(weight_ref[:, first : first + slots])
    for t, (lower, upper) in enumerate(bag_bounds):
        total = picked[lower] * weights[:, lower : lower + 1]
        for k in range(lower + 1, upper):
            total = total + picked[k] * weights[:, k : k + 1]
        put(slice(t * lanes, (t + 1) * lanes), total.astype(jnp.bfloat16))


def pool_kernel(first, place_ref, weight_ref, *refs):
    out_ref, table, picked = refs[-3:]

    def put(columns, total):
        out_ref[:, columns] = total

    pool_slots(first, place_ref, weight_ref, refs[:-3], table, picked, put)


def stage_kernel(
    pieces, sources, first, aliased, pooled, place_ref, me_ref, weight_ref, carried_ref, gain_ref, *refs
):
    piece_refs = refs[:pieces]
    filter_refs = refs[pieces : pieces + sources]
    refs = refs[pieces + sources + aliased :]
    out_ref, state_ref, table, picked, filters, first_buf, second_buf, result = refs[:8]
    filter_sems, out_sems = refs[8:]
    slots = result.shape[0]
    layers = filters.shape[0]
    filter_copies = []
    if sources == 1:
        filter_copies.append(pltpu.make_async_copy(filter_refs[0], filters, filter_sems.at[0]))
    else:
        held, half, depth, _ = filter_refs[0].shape
        for group, filter_ref in enumerate(filter_refs):
            bits, base = block_place(group, me_ref[1])
            for number in range(held):
                owner = me_ref[0] ^ (4 * number + bits)
                rows = pl.ds(pl.multiple_of(owner * depth, depth), depth)
                layer = pl.ds(base * (half // 2), filter_ref.shape[1])
                filter_copies.append(
                    pltpu.make_async_copy(
                        filter_ref.at[number],
                        filters.at[layer, rows, :],
                        filter_sems.at[group * held + number],
                    )
                )
    for copy in filter_copies:
        copy.start()
    front = 16
    if pooled:
        first_buf[front:, :] = piece_refs[0][...].astype(jnp.float32)
    else:

        def put(columns, total):
            first_buf[front:, columns] = total.astype(jnp.float32)

        pool_slots(first, place_ref, weight_ref, piece_refs, table, picked, put)

    for copy in filter_copies:
        copy.wait()
    offset = 0
    out_copies = []
    for layer in range(layers):
        dilation = 2**layer
        span = 2 * dilation
        source, target = (first_buf, second_buf) if layer % 2 == 0 else (second_buf, first_buf)
        source[front - span : front, :] = carried_ref[offset : offset + span, :]
        state_ref[offset : offset + span, :] = source[front + slots - span : front + slots, :]
        offset += span
        for begin in range(0, slots, 256):
            rows = min(256, slots - begin)
            base = front + begin
            taps = [
                source[base - tap * dilation : base - tap * dilation + rows, :].astype(jnp.bfloat16)
                for tap in range(3)
            ]
            output = jnp.dot(
                jnp.concatenate(taps, axis=1), filters[layer], preferred_element_type=jnp.float32
            )
            mean = jnp.mean(output, axis=-1, keepdims=True)
            centred = output - mean
            spread = jnp.mean(centred * centred, axis=-1, keepdims=True)
            active = jnp.maximum(
                centred * lax.rsqrt(spread + epsilon) * gain_ref[layer : layer + 1, :], 0.0
            )
            if layer % 2 == 1:
                active = active + target[base : base + rows, :]
            active = active.astype(jnp.bfloat16)
            if layer == layers - 1:
                result[begin : begin + rows, :] = active
                copy = pltpu.make_async_copy(
                    result.at[pl.ds(begin, rows), :],
                    out_ref.at[pl.ds(first + begin, rows), :],
                    out_sems.at[len(out_copies)],
                )
                copy.start()
                out_copies.append(copy)
            else:
                target[base : base + rows, :] = active.astype(jnp.float32)
    for copy in out_copies:
        copy.wait()


def swapped(array, axis, distance):
    pairs = [(source, source ^ distance) for source in range(lax.axis_size(axis))]
    return lax.ppermute(array, axis, pairs)


def block_place(number, side):
    kind = number % 5
    bits = (2 if kind in (1, 3, 4) else 0) + number // 5
    base = 2 * (side if kind < 2 else 1 - side) + (1 if kind == 4 else 0)
    return bits, base


def ordered_filters(blocks, me):
    count = blocks[0].shape[0]
    owners = 4 * count
    quarter = blocks[0].shape[1] // 2
    layers = 4 * quarter
    whole = jnp.zeros((owners, layers) + blocks[0].shape[2:], blocks[0].dtype)
    for number, block in enumerate(blocks):
        bits, base = block_place(number, me[1])
        for shard in range(count):
            owner = me[0] ^ (4 * shard + bits)
            whole = lax.dynamic_update_slice(
                whole, block[shard][None], (owner, base * quarter, 0, 0)
            )
    return whole.transpose(1, 0, 2, 3).reshape(layers, -1, whole.shape[-1])


def carried_rows(returning, home, entry, stores):
    copies = lax.axis_size("rep")
    me = lax.axis_index("rep")
    by_position = stores.transpose(1, 0, 2)
    positions, _, channels = by_position.shape
    carried = jnp.zeros((positions, channels), stores.dtype)
    for shift in range(copies):
        arrived = by_position
        if shift:
            pairs = [(source, (source + shift) % copies) for source in range(copies)]
            arrived = lax.ppermute(by_position, "rep", pairs)
        wanted = (returning[0] > 0) & (home[0] == (me + copies - shift) % copies)
        chosen = lax.dynamic_index_in_dim(arrived, entry[0], 1, keepdims=False)
        carried = jnp.where(wanted, chosen, carried)
    return carried.astype(jnp.float32)


def local(
    bag_rows, bag_owner, bag_weight, tables, returning, home, entry, stores, conv_weight, norm_gain
):
    owners = lax.axis_size("table")
    samples_here, slot_count, bag_width = bag_rows.shape
    token_count = samples_here * slot_count
    shard_rows = tables.shape[1]
    row_width = tables.shape[2]
    channels = conv_weight.shape[-1]
    capacity = min(token_count, (3 * token_count * bag_width + 2 * owners - 1) // (2 * owners))
    cuts = [0] + [round(capacity * end) // 16 * 16 for end in part_ends]
    slot_cuts = [0] + [cuts[part] for part in stage_parts[:-1]] + [token_count]
    smem = pl.BlockSpec(memory_space=pltpu.SMEM)
    vmem = pl.BlockSpec(memory_space=pltpu.VMEM)
    anywhere = pl.BlockSpec(memory_space=pl.ANY)

    me = jnp.stack([lax.axis_index("table"), lax.axis_index("rep") % 2]).astype(jnp.int32)
    half = conv_weight.shape[0] // 2
    shard = lax.dynamic_slice_in_dim(conv_weight, me[1] * half, half, 0)
    middle = owners // 8
    line = [shard] + [swapped(shard, "table", 4 * step) for step in range(1, middle + 1)]
    state = carried_rows(returning, home, entry, stores)
    rows_by_slot = bag_rows.reshape(token_count, bag_width).T
    owner_by_slot = bag_owner.reshape(token_count, bag_width).T
    requests, place = pl.pallas_call(
        functools.partial(prep_kernel, cuts, shard_rows),
        out_shape=(
            jax.ShapeDtypeStruct((owners, 1, capacity), jnp.int32),
            jax.ShapeDtypeStruct((bag_width, token_count), jnp.int32),
        ),
        in_specs=[vmem, vmem],
        out_specs=(vmem, vmem),
        compiler_params=pltpu.CompilerParams(vmem_limit_bytes=8 * megabyte),
        name="prep",
    )(rows_by_slot, owner_by_slot)
    received = lax.all_to_all(requests, "table", split_axis=0, concat_axis=0, tiled=True)
    received = received.reshape(owners * capacity)
    flat_table = tables.reshape(-1, row_width)
    returned = []
    sent = []
    for number in range(len(part_ends)):
        piece = cuts[number + 1] - cuts[number]
        if number == 1:
            middle_shard = tie(line[middle], received)
            line = line + [swapped(middle_shard, "table", 4 * step) for step in range(1, middle)]
            line[middle] = middle_shard
        earlier = sent[-1:] if sent else line[1:]
        sent.append(
            pl.pallas_call(
                functools.partial(gather_kernel, capacity, cuts[number]),
                out_shape=jax.ShapeDtypeStruct((owners, piece, row_width), jnp.bfloat16),
                in_specs=[anywhere] * (2 + len(earlier)),
                out_specs=anywhere,
                scratch_shapes=[
                    pltpu.VMEM(flat_table.shape, jnp.bfloat16),
                    pltpu.VMEM(flat_table.shape, jnp.float32),
                    pltpu.VMEM((piece, row_width), jnp.float32),
                    pltpu.VMEM((owners, piece, row_width), jnp.bfloat16),
                    pltpu.SMEM((owners * capacity,), jnp.int32),
                    pltpu.SemaphoreType.DMA,
                    pltpu.SemaphoreType.DMA((8,)),
                    pltpu.SemaphoreType.DMA((owners,)),
                ],
                compiler_params=pltpu.CompilerParams(vmem_limit_bytes=58 * megabyte),
                cost_estimate=pl.CostEstimate(
                    flops=0, bytes_accessed=20 * megabyte, transcendentals=0
                ),
                name="owner_gather",
            )(received, flat_table, *earlier)
        )
    line = jnp.stack(line)
    by_table = swapped(line, "table", 2)
    by_rep = swapped(line, "rep", 1)
    corner_low = swapped(by_rep[:, : half // 2], "table", 2)
    corner_high = swapped(by_table[:, half // 2 :], "rep", 1)
    gates = [[], [sent[2]], [state, by_table, by_rep]]
    for rows, gate in zip(sent, gates):
        if returned:
            rows = tie(rows, returned[-1], *gate)
        arrived = lax.all_to_all(rows, "table", split_axis=0, concat_axis=0, tiled=True)
        returned.append(arrived.reshape(-1, row_width))
    filters = [line, by_table, by_rep, corner_low, corner_high]
    filters = filters + [swapped(block, "table", 1) for block in filters]
    if conv_weight.shape[1] % 16:
        filters = [ordered_filters(filters, me)]
    weight_by_slot = bag_weight.reshape(token_count, bag_width).T
    hidden = None
    for number, part in enumerate(stage_parts):
        first, last = slot_cuts[number], slot_cuts[number + 1]
        slots = last - first
        known = [] if hidden is None else [hidden]
        pieces = returned[:part]
        table_rows = owners * cuts[part]
        if number == 0:
            pieces = [
                pl.pallas_call(
                    functools.partial(pool_kernel, first),
                    out_shape=jax.ShapeDtypeStruct((slots, channels), jnp.bfloat16),
                    in_specs=[smem] + [vmem] * (1 + part),
                    out_specs=vmem,
                    scratch_shapes=[
                        pltpu.VMEM((table_rows, row_width), jnp.float32),
                        pltpu.VMEM((bag_width, slots, row_width), jnp.float32),
                    ],
                    compiler_params=pltpu.CompilerParams(vmem_limit_bytes=32 * megabyte),
                    cost_estimate=pl.CostEstimate(
                        flops=0, bytes_accessed=24 * megabyte, transcendentals=0
                    ),
                    name="pool",
                )(place, weight_by_slot, *pieces)
            ]
            table_rows = 8
        hidden, state = pl.pallas_call(
            functools.partial(
                stage_kernel, len(pieces), len(filters), first, len(known), number == 0
            ),
            out_shape=(
                jax.ShapeDtypeStruct((token_count, channels), jnp.bfloat16),
                jax.ShapeDtypeStruct(state.shape, jnp.float32),
            ),
            in_specs=[smem] * 2
            + [vmem] * (3 + len(pieces))
            + [anywhere] * (len(filters) + len(known)),
            out_specs=(anywhere, vmem),
            scratch_shapes=[
                pltpu.VMEM((table_rows, row_width), jnp.float32),
                pltpu.VMEM((bag_width, slots, row_width), jnp.float32),
                pltpu.VMEM((conv_weight.shape[0], 3 * channels, channels), jnp.bfloat16),
                pltpu.VMEM((slots + 16, channels), jnp.float32),
                pltpu.VMEM((slots + 16, channels), jnp.float32),
                pltpu.VMEM((slots, channels), jnp.bfloat16),
                pltpu.SemaphoreType.DMA((10 * (owners // 4),)),
                pltpu.SemaphoreType.DMA(((slots + 255) // 256,)),
            ],
            input_output_aliases={5 + len(pieces) + len(filters): 0} if known else {},
            compiler_params=pltpu.CompilerParams(vmem_limit_bytes=56 * megabyte),
            cost_estimate=pl.CostEstimate(
                flops=2 * slots * 3 * channels * channels * conv_weight.shape[0],
                bytes_accessed=24 * megabyte,
                transcendentals=0,
            ),
            name="stage",
        )(place, me, weight_by_slot, state, norm_gain, *pieces, *filters, *known)
    return hidden.reshape(samples_here, slot_count, channels)


def solution(mesh):
    in_specs = (
        P(("table", "rep"), None, None),
        P(("table", "rep"), None, None),
        P(("table", "rep"), None, None),
        P(None, "table", None),
        P(("table", "rep")),
        P(("table", "rep")),
        P(("table", "rep")),
        P(("table", "rep"), None, None),
        P(None, "table", None),
        P(),
    )
    out_specs = P(("table", "rep"), None, None)
    return jax.shard_map(local, mesh=mesh, in_specs=in_specs, out_specs=out_specs, check_vma=False)
```

```python
import functools
import jax
import jax.numpy as jnp
from jax import lax
from jax.experimental import pallas as pl
from jax.experimental.pallas import tpu as pltpu
from jax.sharding import PartitionSpec as P

table_of_id = (0, 1, 2, 2, 3, 3, 3, 3)
bag_bounds = ((0, 1), (1, 2), (2, 4), (4, 8))
epsilon = 1e-05
part_ends = (0.25, 0.75, 1.0)
stage_parts = (2, 3)
megabyte = 1024 * 1024


def prep_kernel(cuts, shard_rows, rows_ref, owner_ref, request_ref, place_ref):
    owner = owner_ref[...]
    rows = rows_ref[...]
    owners = request_ref.shape[0]
    width, slots = owner.shape
    value_bits = (len(bag_bounds) * shard_rows).bit_length()
    owner_ids = lax.broadcasted_iota(jnp.int32, (owners, slots), 0)
    lane = lax.broadcasted_iota(jnp.int32, (owners, slots), 1)
    value = jnp.zeros((owners, slots), jnp.int32)
    for k in range(width):
        named = owner[k : k + 1, :] == owner_ids
        value = jnp.where(named, rows[k : k + 1, :] + (table_of_id[k] * shard_rows + 1), value)
    present = jnp.where(value > 0, 1, 0)
    rank = present
    step = 1
    while step < slots:
        rank = rank + jnp.where(lane >= step, pltpu.roll(rank, step, 1), 0)
        step *= 2
    rank = rank - present
    place = jnp.zeros((width, slots), jnp.int32)
    for number in range(owners):
        place = jnp.where(owner == number, rank[number : number + 1, :], place)
    landing = jnp.zeros((width, slots), jnp.int32)
    for start, stop in zip(cuts[:-1], cuts[1:]):
        where = owners * start + owner * (stop - start) + place - start
        landing = jnp.where(place >= start, where, landing)
    place_ref[...] = landing
    packed = jnp.where(value > 0, ((lane - rank) << value_bits) + value, 0)
    step = 1
    level = value_bits
    while step < slots:
        moving = jnp.where(((packed >> level) & 1) == 1, packed, 0)
        packed = (packed - moving) + pltpu.roll(moving, slots - step, 1)
        step *= 2
        level += 1
    value = jnp.maximum((packed & ((1 << value_bits) - 1)) - 1, 0)
    for number in range(owners):
        request_ref[number] = value[number : number + 1, : request_ref.shape[2]]


def pass_kernel(*refs):
    pass


def tie(array, *others):
    anywhere = pl.BlockSpec(memory_space=pl.ANY)
    return pl.pallas_call(
        pass_kernel,
        out_shape=jax.ShapeDtypeStruct(array.shape, array.dtype),
        in_specs=[anywhere] * (1 + len(others)),
        out_specs=anywhere,
        input_output_aliases={0: 0},
        name="tie",
    )(array, *others)


def gather_kernel(capacity, first, index_ref, table_ref, *refs):
    out_ref, narrow, wide, picked, packed, index, index_sem, table_sems, out_sems = refs[-9:]
    owners, piece, _ = out_ref.shape
    unroll = 32 if piece % 32 == 0 else 16
    blocks = table_sems.shape[0]
    block_rows = table_ref.shape[0] // blocks
    table_copies = []
    for block in range(blocks):
        part = pl.ds(block * block_rows, block_rows)
        copy = pltpu.make_async_copy(table_ref.at[part, :], narrow.at[part, :], table_sems.at[block])
        copy.start()
        table_copies.append(copy)
    index_copy = pltpu.make_async_copy(index_ref, index, index_sem)
    index_copy.start()
    rows = 256

    for block in range(blocks):
        table_copies[block].wait()

        def widen(step, carry, block=block):
            base = pl.multiple_of(block * block_rows + step * rows, rows)
            wide[pl.ds(base, rows), :] = narrow[pl.ds(base, rows), :].astype(jnp.float32)
            return carry

        lax.fori_loop(0, block_rows // rows, widen, 0)
    index_copy.wait()
    copies = []
    for number in range(owners):
        origin = number * capacity + first

        def some_rows(block, carry, origin=origin):
            base = pl.multiple_of(block * unroll, unroll)
            picks = [index[origin + base + i] for i in range(unroll)]
            found = [wide[pl.ds(pick, 1), :] for pick in picks]
            for i in range(unroll):
                picked[pl.ds(base + i, 1), :] = found[i]
            return carry

        lax.fori_loop(0, piece // unroll, some_rows, 0)
        packed[number] = picked[...].astype(jnp.bfloat16)
        copy = pltpu.make_async_copy(packed.at[number], out_ref.at[number], out_sems.at[number])
        copy.start()
        copies.append(copy)
    for copy in copies:
        copy.wait()


def pool_slots(first, place_ref, weight_ref, piece_refs, table, picked, put):
    width, slots, lanes = picked.shape
    start = 0
    for piece_ref in piece_refs:
        count = piece_ref.shape[0]
        rows = 256

        def widen(step, carry, piece_ref=piece_ref, start=start):
            base = pl.multiple_of(step * rows, rows)
            table[pl.ds(start + base, rows), :] = piece_ref[pl.ds(base, rows), :].astype(jnp.float32)
            return carry

        lax.fori_loop(0, count // rows, widen, 0)
        start += count

    def some_slots(step, carry):
        base = pl.multiple_of(step * 8, 8)
        for k in range(width):
            picks = [place_ref[k, first + base + i] for i in range(8)]
            rows = [table[pl.ds(pick, 1), :] for pick in picks]
            for i in range(8):
                picked[k, pl.ds(base + i, 1), :] = rows[i]
        return carry

    lax.fori_loop(0, slots // 8, some_slots, 0)
    weights = jnp.transpose(weight_ref[:, first : first + slots])
    for t, (lower, upper) in enumerate(bag_bounds):
        total = picked[lower] * weights[:, lower : lower + 1]
        for k in range(lower + 1, upper):
            total = total + picked[k] * weights[:, k : k + 1]
        put(slice(t * lanes, (t + 1) * lanes), total.astype(jnp.bfloat16))


def pool_kernel(place_ref, weight_ref, *refs):
    out_ref, table, picked = refs[-3:]

    def put(columns, total):
        out_ref[:, columns] = total

    pool_slots(0, place_ref, weight_ref, refs[:-3], table, picked, put)


def stage_kernel(
    pieces, sources, first, aliased, pooled, place_ref, me_ref, weight_ref, carried_ref, gain_ref, *refs
):
    piece_refs = refs[:pieces]
    filter_refs = refs[pieces : pieces + sources]
    refs = refs[pieces + sources + aliased :]
    out_ref, state_ref, table, picked, filters, first_buf, second_buf, result = refs[:8]
    filter_sems, out_sems = refs[8:]
    slots = result.shape[0]
    layers = filters.shape[0]
    filter_copies = []
    if sources == 1:
        filter_copies.append(pltpu.make_async_copy(filter_refs[0], filters, filter_sems.at[0]))
    else:
        held, half, depth, _ = filter_refs[0].shape
        for group, filter_ref in enumerate(filter_refs):
            bits, side, start = block_place(group, me_ref[1], held)
            for number in range(filter_ref.shape[0]):
                owner = me_ref[0] ^ (4 * (start + number) + bits)
                rows = pl.ds(pl.multiple_of(owner * depth, depth), depth)
                filter_copies.append(
                    pltpu.make_async_copy(
                        filter_ref.at[number],
                        filters.at[pl.ds(side * half, half), rows, :],
                        filter_sems.at[len(filter_copies)],
                    )
                )
    for copy in filter_copies:
        copy.start()
    front = 16
    if pooled:
        first_buf[front:, :] = piece_refs[0][...].astype(jnp.float32)
    else:

        def put(columns, total):
            first_buf[front:, columns] = total.astype(jnp.float32)

        pool_slots(first, place_ref, weight_ref, piece_refs, table, picked, put)

    for copy in filter_copies:
        copy.wait()
    offset = 0
    out_copies = []
    for layer in range(layers):
        dilation = 2**layer
        span = 2 * dilation
        source, target = (first_buf, second_buf) if layer % 2 == 0 else (second_buf, first_buf)
        source[front - span : front, :] = carried_ref[offset : offset + span, :]
        state_ref[offset : offset + span, :] = source[front + slots - span : front + slots, :]
        offset += span
        for begin in range(0, slots, 256):
            rows = min(256, slots - begin)
            base = front + begin
            taps = [
                source[base - tap * dilation : base - tap * dilation + rows, :].astype(jnp.bfloat16)
                for tap in range(3)
            ]
            output = jnp.dot(
                jnp.concatenate(taps, axis=1), filters[layer], preferred_element_type=jnp.float32
            )
            mean = jnp.mean(output, axis=-1, keepdims=True)
            centred = output - mean
            spread = jnp.mean(centred * centred, axis=-1, keepdims=True)
            active = jnp.maximum(
                centred * lax.rsqrt(spread + epsilon) * gain_ref[layer : layer + 1, :], 0.0
            )
            if layer % 2 == 1:
                active = active + target[base : base + rows, :]
            active = active.astype(jnp.bfloat16)
            if layer == layers - 1:
                result[begin : begin + rows, :] = active
                copy = pltpu.make_async_copy(
                    result.at[pl.ds(begin, rows), :],
                    out_ref.at[pl.ds(first + begin, rows), :],
                    out_sems.at[len(out_copies)],
                )
                copy.start()
                out_copies.append(copy)
            else:
                target[base : base + rows, :] = active.astype(jnp.float32)
    for copy in out_copies:
        copy.wait()


def swapped(array, axis, distance):
    pairs = [(source, source ^ distance) for source in range(lax.axis_size(axis))]
    return lax.ppermute(array, axis, pairs)


def block_place(number, side, held):
    kind = number % 5
    bits = (2 if kind in (1, 3, 4) else 0) + number // 5
    return bits, side if kind < 2 else 1 - side, held // 2 if kind == 4 else 0


def ordered_filters(blocks, me):
    count = blocks[0].shape[0]
    owners = 4 * count
    half = blocks[0].shape[1]
    layers = 2 * half
    whole = jnp.zeros((owners, layers) + blocks[0].shape[2:], blocks[0].dtype)
    for number, block in enumerate(blocks):
        bits, side, start = block_place(number, me[1], count)
        for shard in range(block.shape[0]):
            owner = me[0] ^ (4 * (start + shard) + bits)
            whole = lax.dynamic_update_slice(whole, block[shard][None], (owner, side * half, 0, 0))
    return whole.transpose(1, 0, 2, 3).reshape(layers, -1, whole.shape[-1])


def carried_rows(returning, home, entry, stores):
    copies = lax.axis_size("rep")
    me = lax.axis_index("rep")
    by_position = stores.transpose(1, 0, 2)
    positions, _, channels = by_position.shape
    carried = jnp.zeros((positions, channels), stores.dtype)
    for shift in range(copies):
        arrived = by_position
        if shift:
            pairs = [(source, (source + shift) % copies) for source in range(copies)]
            arrived = lax.ppermute(by_position, "rep", pairs)
        wanted = (returning[0] > 0) & (home[0] == (me + copies - shift) % copies)
        chosen = lax.dynamic_index_in_dim(arrived, entry[0], 1, keepdims=False)
        carried = jnp.where(wanted, chosen, carried)
    return carried.astype(jnp.float32)


def local(
    bag_rows, bag_owner, bag_weight, tables, returning, home, entry, stores, conv_weight, norm_gain
):
    owners = lax.axis_size("table")
    samples_here, slot_count, bag_width = bag_rows.shape
    token_count = samples_here * slot_count
    shard_rows = tables.shape[1]
    row_width = tables.shape[2]
    channels = conv_weight.shape[-1]
    capacity = min(token_count, (3 * token_count * bag_width + 2 * owners - 1) // (2 * owners))
    cuts = [0] + [round(capacity * end) // 16 * 16 for end in part_ends]
    slot_cuts = [0] + [cuts[part] for part in stage_parts[:-1]] + [token_count]
    smem = pl.BlockSpec(memory_space=pltpu.SMEM)
    vmem = pl.BlockSpec(memory_space=pltpu.VMEM)
    anywhere = pl.BlockSpec(memory_space=pl.ANY)

    me = jnp.stack([lax.axis_index("table"), lax.axis_index("rep") % 2]).astype(jnp.int32)
    half = conv_weight.shape[0] // 2
    shard = lax.dynamic_slice_in_dim(conv_weight, me[1] * half, half, 0)
    middle = owners // 8
    line = [shard] + [swapped(shard, "table", 4 * step) for step in range(1, middle + 1)]
    state = carried_rows(returning, home, entry, stores)
    rows_by_slot = bag_rows.reshape(token_count, bag_width).T
    owner_by_slot = bag_owner.reshape(token_count, bag_width).T
    requests, place = pl.pallas_call(
        functools.partial(prep_kernel, cuts, shard_rows),
        out_shape=(
            jax.ShapeDtypeStruct((owners, 1, capacity), jnp.int32),
            jax.ShapeDtypeStruct((bag_width, token_count), jnp.int32),
        ),
        in_specs=[vmem, vmem],
        out_specs=(vmem, vmem),
        compiler_params=pltpu.CompilerParams(vmem_limit_bytes=8 * megabyte),
        name="prep",
    )(rows_by_slot, owner_by_slot)
    received = lax.all_to_all(requests, "table", split_axis=0, concat_axis=0, tiled=True)
    received = received.reshape(owners * capacity)
    flat_table = tables.reshape(-1, row_width)
    returned = []
    sent = []
    for number in range(len(part_ends)):
        piece = cuts[number + 1] - cuts[number]
        if number == 1:
            middle_shard = tie(line[middle], received)
            forwarded = [swapped(middle_shard, "table", 4 * step) for step in range(1, middle)]
            line = line[:middle] + [middle_shard] + forwarded
        earlier = sent[-1:] if sent else line[1:]
        sent.append(
            pl.pallas_call(
                functools.partial(gather_kernel, capacity, cuts[number]),
                out_shape=jax.ShapeDtypeStruct((owners, piece, row_width), jnp.bfloat16),
                in_specs=[anywhere] * (2 + len(earlier)),
                out_specs=anywhere,
                scratch_shapes=[
                    pltpu.VMEM(flat_table.shape, jnp.bfloat16),
                    pltpu.VMEM(flat_table.shape, jnp.float32),
                    pltpu.VMEM((piece, row_width), jnp.float32),
                    pltpu.VMEM((owners, piece, row_width), jnp.bfloat16),
                    pltpu.SMEM((owners * capacity,), jnp.int32),
                    pltpu.SemaphoreType.DMA,
                    pltpu.SemaphoreType.DMA((8,)),
                    pltpu.SemaphoreType.DMA((owners,)),
                ],
                compiler_params=pltpu.CompilerParams(vmem_limit_bytes=58 * megabyte),
                cost_estimate=pl.CostEstimate(
                    flops=0, bytes_accessed=20 * megabyte, transcendentals=0
                ),
                name="owner_gather",
            )(received, flat_table, *earlier)
        )
    line = jnp.stack(line)
    by_table = swapped(line, "table", 2)
    by_rep = swapped(line, "rep", 1)
    corner_low = swapped(by_rep[: owners // 8], "table", 2)
    corner_high = swapped(by_table[owners // 8 :], "rep", 1)
    gates = [[], [sent[2]] + forwarded, [state, by_table, by_rep]]
    for rows, gate in zip(sent, gates):
        if returned:
            rows = tie(rows, returned[-1], *gate)
        arrived = lax.all_to_all(rows, "table", split_axis=0, concat_axis=0, tiled=True)
        returned.append(arrived.reshape(-1, row_width))
    weight_by_slot = bag_weight.reshape(token_count, bag_width).T
    part = stage_parts[0]
    pooled = pl.pallas_call(
        pool_kernel,
        out_shape=jax.ShapeDtypeStruct((cuts[part], channels), jnp.bfloat16),
        in_specs=[smem] + [vmem] * (1 + part),
        out_specs=vmem,
        scratch_shapes=[
            pltpu.VMEM((owners * cuts[part], row_width), jnp.float32),
            pltpu.VMEM((bag_width, cuts[part], row_width), jnp.float32),
        ],
        compiler_params=pltpu.CompilerParams(vmem_limit_bytes=32 * megabyte),
        cost_estimate=pl.CostEstimate(
            flops=0, bytes_accessed=24 * megabyte, transcendentals=0
        ),
        name="pool",
    )(place, weight_by_slot, *returned[:part])
    corner_low, corner_high = tie(corner_low, pooled), tie(corner_high, pooled)
    filters = [line, by_table, by_rep, corner_low, corner_high]
    filters = filters + [swapped(block, "table", 1) for block in filters]
    if conv_weight.shape[1] % 16:
        filters = [ordered_filters(filters, me)]

    hidden = None
    for number, part in enumerate(stage_parts):
        first, last = slot_cuts[number], slot_cuts[number + 1]
        slots = last - first
        known = [] if hidden is None else [hidden]
        pieces = returned[:part]
        table_rows = owners * cuts[part]
        if number == 0:
            pieces = [pooled]
            table_rows = 8
        hidden, state = pl.pallas_call(
            functools.partial(
                stage_kernel, len(pieces), len(filters), first, len(known), number == 0
            ),
            out_shape=(
                jax.ShapeDtypeStruct((token_count, channels), jnp.bfloat16),
                jax.ShapeDtypeStruct(state.shape, jnp.float32),
            ),
            in_specs=[smem] * 2
            + [vmem] * (3 + len(pieces))
            + [anywhere] * (len(filters) + len(known)),
            out_specs=(anywhere, vmem),
            scratch_shapes=[
                pltpu.VMEM((table_rows, row_width), jnp.float32),
                pltpu.VMEM((bag_width, slots, row_width), jnp.float32),
                pltpu.VMEM((conv_weight.shape[0], 3 * channels, channels), jnp.bfloat16),
                pltpu.VMEM((slots + 16, channels), jnp.float32),
                pltpu.VMEM((slots + 16, channels), jnp.float32),
                pltpu.VMEM((slots, channels), jnp.bfloat16),
                pltpu.SemaphoreType.DMA((2 * owners,)),
                pltpu.SemaphoreType.DMA(((slots + 255) // 256,)),
            ],
            input_output_aliases={5 + len(pieces) + len(filters): 0} if known else {},
            compiler_params=pltpu.CompilerParams(vmem_limit_bytes=56 * megabyte),
            cost_estimate=pl.CostEstimate(
                flops=2 * slots * 3 * channels * channels * conv_weight.shape[0],
                bytes_accessed=24 * megabyte,
                transcendentals=0,
            ),
            name="stage",
        )(place, me, weight_by_slot, state, norm_gain, *pieces, *filters, *known)
    return hidden.reshape(samples_here, slot_count, channels)


def solution(mesh):
    in_specs = (
        P(("table", "rep"), None, None),
        P(("table", "rep"), None, None),
        P(("table", "rep"), None, None),
        P(None, "table", None),
        P(("table", "rep")),
        P(("table", "rep")),
        P(("table", "rep")),
        P(("table", "rep"), None, None),
        P(None, "table", None),
        P(),
    )
    out_specs = P(("table", "rep"), None, None)
    return jax.shard_map(local, mesh=mesh, in_specs=in_specs, out_specs=out_specs, check_vma=False)
```

```python
import functools
import jax
import jax.numpy as jnp
from jax import lax
from jax.experimental import pallas as pl
from jax.experimental.pallas import tpu as pltpu
from jax.sharding import PartitionSpec as P

table_of_id = (0, 1, 2, 2, 3, 3, 3, 3)
bag_bounds = ((0, 1), (1, 2), (2, 4), (4, 8))
epsilon = 1e-05
part_ends = (0.25, 0.75, 1.0)
megabyte = 1024 * 1024


def prep_kernel(cuts, shard_rows, rows_ref, owner_ref, request_ref, place_ref):
    owner = owner_ref[...]
    rows = rows_ref[...]
    owners = request_ref.shape[0]
    width, slots = owner.shape
    value_bits = (len(bag_bounds) * shard_rows).bit_length()
    owner_ids = lax.broadcasted_iota(jnp.int32, (owners, slots), 0)
    lane = lax.broadcasted_iota(jnp.int32, (owners, slots), 1)
    value = jnp.zeros((owners, slots), jnp.int32)
    for k in range(width):
        named = owner[k : k + 1, :] == owner_ids
        value = jnp.where(named, rows[k : k + 1, :] + (table_of_id[k] * shard_rows + 1), value)
    present = jnp.where(value > 0, 1, 0)
    rank = present
    step = 1
    while step < slots:
        rank = rank + jnp.where(lane >= step, pltpu.roll(rank, step, 1), 0)
        step *= 2
    rank = rank - present
    place = jnp.zeros((width, slots), jnp.int32)
    for number in range(owners):
        place = jnp.where(owner == number, rank[number : number + 1, :], place)
    landing = jnp.zeros((width, slots), jnp.int32)
    for start, stop in zip(cuts[:-1], cuts[1:]):
        where = owners * start + owner * (stop - start) + place - start
        landing = jnp.where(place >= start, where, landing)
    place_ref[...] = landing
    packed = jnp.where(value > 0, ((lane - rank) << value_bits) + value, 0)
    step = 1
    level = value_bits
    while step < slots:
        moving = jnp.where(((packed >> level) & 1) == 1, packed, 0)
        packed = (packed - moving) + pltpu.roll(moving, slots - step, 1)
        step *= 2
        level += 1
    value = jnp.maximum((packed & ((1 << value_bits) - 1)) - 1, 0)
    for number in range(owners):
        request_ref[number] = value[number : number + 1, : request_ref.shape[2]]


def pass_kernel(*refs):
    pass


def tie(array, *others):
    anywhere = pl.BlockSpec(memory_space=pl.ANY)
    return pl.pallas_call(
        pass_kernel,
        out_shape=jax.ShapeDtypeStruct(array.shape, array.dtype),
        in_specs=[anywhere] * (1 + len(others)),
        out_specs=anywhere,
        input_output_aliases={0: 0},
        name="tie",
    )(array, *others)


def gather_kernel(capacity, first, index_ref, table_ref, *refs):
    out_ref, narrow, wide, picked, packed, index, index_sem, table_sems, out_sems = refs[-9:]
    owners, piece, _ = out_ref.shape
    unroll = 32 if piece % 32 == 0 else 16
    blocks = table_sems.shape[0]
    block_rows = table_ref.shape[0] // blocks
    table_copies = []
    for block in range(blocks):
        part = pl.ds(block * block_rows, block_rows)
        copy = pltpu.make_async_copy(table_ref.at[part, :], narrow.at[part, :], table_sems.at[block])
        copy.start()
        table_copies.append(copy)
    index_copy = pltpu.make_async_copy(index_ref, index, index_sem)
    index_copy.start()
    rows = 256

    for block in range(blocks):
        table_copies[block].wait()

        def widen(step, carry, block=block):
            base = pl.multiple_of(block * block_rows + step * rows, rows)
            wide[pl.ds(base, rows), :] = narrow[pl.ds(base, rows), :].astype(jnp.float32)
            return carry

        lax.fori_loop(0, block_rows // rows, widen, 0)
    index_copy.wait()
    copies = []
    for number in range(owners):
        origin = number * capacity + first

        def some_rows(block, carry, origin=origin):
            base = pl.multiple_of(block * unroll, unroll)
            picks = [index[origin + base + i] for i in range(unroll)]
            found = [wide[pl.ds(pick, 1), :] for pick in picks]
            for i in range(unroll):
                picked[pl.ds(base + i, 1), :] = found[i]
            return carry

        lax.fori_loop(0, piece // unroll, some_rows, 0)
        packed[number] = picked[...].astype(jnp.bfloat16)
        copy = pltpu.make_async_copy(packed.at[number], out_ref.at[number], out_sems.at[number])
        copy.start()
        copies.append(copy)
    for copy in copies:
        copy.wait()


def pool_slots(first, place_ref, weight_ref, piece_refs, table, picked, put):
    width, slots, lanes = picked.shape
    start = 0
    for piece_ref in piece_refs:
        count = piece_ref.shape[0]
        rows = 256

        def widen(step, carry, piece_ref=piece_ref, start=start):
            base = pl.multiple_of(step * rows, rows)
            table[pl.ds(start + base, rows), :] = piece_ref[pl.ds(base, rows), :].astype(jnp.float32)
            return carry

        lax.fori_loop(0, count // rows, widen, 0)
        start += count

    def some_slots(step, carry):
        base = pl.multiple_of(step * 8, 8)
        for k in range(width):
            picks = [place_ref[k, first + base + i] for i in range(8)]
            rows = [table[pl.ds(pick, 1), :] for pick in picks]
            for i in range(8):
                picked[k, pl.ds(base + i, 1), :] = rows[i]
        return carry

    lax.fori_loop(0, slots // 8, some_slots, 0)
    weights = jnp.transpose(weight_ref[:, first : first + slots])
    for t, (lower, upper) in enumerate(bag_bounds):
        total = picked[lower] * weights[:, lower : lower + 1]
        for k in range(lower + 1, upper):
            total = total + picked[k] * weights[:, k : k + 1]
        put(slice(t * lanes, (t + 1) * lanes), total.astype(jnp.bfloat16))


def pool_kernel(place_ref, weight_ref, *refs):
    out_ref, table, picked = refs[-3:]

    def put(columns, total):
        out_ref[:, columns] = total

    pool_slots(0, place_ref, weight_ref, refs[:-3], table, picked, put)


def stage_kernel(
    pieces, sources, place_ref, me_ref, weight_ref, carried_ref, gain_ref, pooled_ref, *refs
):
    piece_refs = refs[:pieces]
    filter_refs = refs[pieces : pieces + sources]
    out_ref, table, picked, filters, first_buf, second_buf, result = refs[pieces + sources :][:7]
    filter_sems, out_sems = refs[pieces + sources :][7:]
    slots = result.shape[0]
    layers = filters.shape[0]
    filter_copies = []
    if sources == 1:
        filter_copies.append(pltpu.make_async_copy(filter_refs[0], filters, filter_sems.at[0]))
    else:
        held, half, depth, _ = filter_refs[0].shape
        for group, filter_ref in enumerate(filter_refs):
            bits, side = block_place(group, me_ref[1])
            for number in range(filter_ref.shape[0]):
                owner = me_ref[0] ^ (4 * number + bits)
                rows = pl.ds(pl.multiple_of(owner * depth, depth), depth)
                filter_copies.append(
                    pltpu.make_async_copy(
                        filter_ref.at[number],
                        filters.at[pl.ds(side * half, half), rows, :],
                        filter_sems.at[len(filter_copies)],
                    )
                )
    for copy in filter_copies:
        copy.start()
    front = 16
    early = pooled_ref.shape[0]
    first_buf[front : front + early, :] = pooled_ref[...].astype(jnp.float32)

    def put(columns, total):
        first_buf[front + early :, columns] = total.astype(jnp.float32)

    pool_slots(early, place_ref, weight_ref, piece_refs, table, picked, put)
    for copy in filter_copies:
        copy.wait()
    offset = 0
    out_copies = []
    for layer in range(layers):
        dilation = 2**layer
        span = 2 * dilation
        source, target = (first_buf, second_buf) if layer % 2 == 0 else (second_buf, first_buf)
        source[front - span : front, :] = carried_ref[offset : offset + span, :]
        offset += span
        for begin in range(0, slots, 256):
            rows = min(256, slots - begin)
            base = front + begin
            taps = [
                source[base - tap * dilation : base - tap * dilation + rows, :].astype(jnp.bfloat16)
                for tap in range(3)
            ]
            output = jnp.dot(
                jnp.concatenate(taps, axis=1), filters[layer], preferred_element_type=jnp.float32
            )
            mean = jnp.mean(output, axis=-1, keepdims=True)
            centred = output - mean
            spread = jnp.mean(centred * centred, axis=-1, keepdims=True)
            active = jnp.maximum(
                centred * lax.rsqrt(spread + epsilon) * gain_ref[layer : layer + 1, :], 0.0
            )
            if layer % 2 == 1:
                active = active + target[base : base + rows, :]
            active = active.astype(jnp.bfloat16)
            if layer == layers - 1:
                result[begin : begin + rows, :] = active
                copy = pltpu.make_async_copy(
                    result.at[pl.ds(begin, rows), :],
                    out_ref.at[pl.ds(begin, rows), :],
                    out_sems.at[len(out_copies)],
                )
                copy.start()
                out_copies.append(copy)
            else:
                target[base : base + rows, :] = active.astype(jnp.float32)
    for copy in out_copies:
        copy.wait()


def swapped(array, axis, distance):
    pairs = [(source, source ^ distance) for source in range(lax.axis_size(axis))]
    return lax.ppermute(array, axis, pairs)


def block_place(number, side):
    kind = number % 4
    bits = (2 if kind in (1, 3) else 0) + number // 4
    return bits, side if kind < 2 else 1 - side


def ordered_filters(blocks, me):
    count = blocks[0].shape[0]
    owners = 4 * count
    half = blocks[0].shape[1]
    layers = 2 * half
    whole = jnp.zeros((owners, layers) + blocks[0].shape[2:], blocks[0].dtype)
    for number, block in enumerate(blocks):
        bits, side = block_place(number, me[1])
        for shard in range(block.shape[0]):
            owner = me[0] ^ (4 * shard + bits)
            whole = lax.dynamic_update_slice(whole, block[shard][None], (owner, side * half, 0, 0))
    return whole.transpose(1, 0, 2, 3).reshape(layers, -1, whole.shape[-1])


def carried_rows(returning, home, entry, stores):
    copies = lax.axis_size("rep")
    me = lax.axis_index("rep")
    by_position = stores.transpose(1, 0, 2)
    positions, _, channels = by_position.shape
    carried = jnp.zeros((positions, channels), stores.dtype)
    for shift in range(copies):
        arrived = by_position
        if shift:
            pairs = [(source, (source + shift) % copies) for source in range(copies)]
            arrived = lax.ppermute(by_position, "rep", pairs)
        wanted = (returning[0] > 0) & (home[0] == (me + copies - shift) % copies)
        chosen = lax.dynamic_index_in_dim(arrived, entry[0], 1, keepdims=False)
        carried = jnp.where(wanted, chosen, carried)
    return carried.astype(jnp.float32)


def local(
    bag_rows, bag_owner, bag_weight, tables, returning, home, entry, stores, conv_weight, norm_gain
):
    owners = lax.axis_size("table")
    samples_here, slot_count, bag_width = bag_rows.shape
    token_count = samples_here * slot_count
    shard_rows = tables.shape[1]
    row_width = tables.shape[2]
    channels = conv_weight.shape[-1]
    capacity = min(token_count, (3 * token_count * bag_width + 2 * owners - 1) // (2 * owners))
    cuts = [0] + [round(capacity * end) // 16 * 16 for end in part_ends]
    early = cuts[-2]
    late = token_count - early
    smem = pl.BlockSpec(memory_space=pltpu.SMEM)
    vmem = pl.BlockSpec(memory_space=pltpu.VMEM)
    anywhere = pl.BlockSpec(memory_space=pl.ANY)

    me = jnp.stack([lax.axis_index("table"), lax.axis_index("rep") % 2]).astype(jnp.int32)
    half = conv_weight.shape[0] // 2
    shard = lax.dynamic_slice_in_dim(conv_weight, me[1] * half, half, 0)
    middle = owners // 8
    line = [shard] + [swapped(shard, "table", 4 * step) for step in range(1, middle + 1)]
    state = carried_rows(returning, home, entry, stores)
    rows_by_slot = bag_rows.reshape(token_count, bag_width).T
    owner_by_slot = bag_owner.reshape(token_count, bag_width).T
    requests, place = pl.pallas_call(
        functools.partial(prep_kernel, cuts, shard_rows),
        out_shape=(
            jax.ShapeDtypeStruct((owners, 1, capacity), jnp.int32),
            jax.ShapeDtypeStruct((bag_width, token_count), jnp.int32),
        ),
        in_specs=[vmem, vmem],
        out_specs=(vmem, vmem),
        compiler_params=pltpu.CompilerParams(vmem_limit_bytes=8 * megabyte),
        name="prep",
    )(rows_by_slot, owner_by_slot)
    received = lax.all_to_all(requests, "table", split_axis=0, concat_axis=0, tiled=True)
    received = received.reshape(owners * capacity)
    flat_table = tables.reshape(-1, row_width)
    returned = []
    sent = []
    for number in range(len(part_ends)):
        piece = cuts[number + 1] - cuts[number]
        if number == 1:
            middle_shard = tie(line[middle], received)
            forwarded = [swapped(middle_shard, "table", 4 * step) for step in range(1, middle)]
            line = line[:middle] + [middle_shard] + forwarded
        earlier = sent[-1:] if sent else line[1:]
        sent.append(
            pl.pallas_call(
                functools.partial(gather_kernel, capacity, cuts[number]),
                out_shape=jax.ShapeDtypeStruct((owners, piece, row_width), jnp.bfloat16),
                in_specs=[anywhere] * (2 + len(earlier)),
                out_specs=anywhere,
                scratch_shapes=[
                    pltpu.VMEM(flat_table.shape, jnp.bfloat16),
                    pltpu.VMEM(flat_table.shape, jnp.float32),
                    pltpu.VMEM((piece, row_width), jnp.float32),
                    pltpu.VMEM((owners, piece, row_width), jnp.bfloat16),
                    pltpu.SMEM((owners * capacity,), jnp.int32),
                    pltpu.SemaphoreType.DMA,
                    pltpu.SemaphoreType.DMA((8,)),
                    pltpu.SemaphoreType.DMA((owners,)),
                ],
                compiler_params=pltpu.CompilerParams(vmem_limit_bytes=58 * megabyte),
                cost_estimate=pl.CostEstimate(
                    flops=0, bytes_accessed=20 * megabyte, transcendentals=0
                ),
                name="owner_gather",
            )(received, flat_table, *earlier)
        )
    line = jnp.stack(line)
    by_table = swapped(line, "table", 2)
    by_rep = swapped(line, "rep", 1)
    corner = swapped(by_table, "rep", 1)
    gates = [[], [sent[2]] + forwarded, [state, by_table, by_rep]]
    for rows, gate in zip(sent, gates):
        if returned:
            rows = tie(rows, returned[-1], *gate)
        arrived = lax.all_to_all(rows, "table", split_axis=0, concat_axis=0, tiled=True)
        returned.append(arrived.reshape(-1, row_width))
    weight_by_slot = bag_weight.reshape(token_count, bag_width).T
    pooled = pl.pallas_call(
        pool_kernel,
        out_shape=jax.ShapeDtypeStruct((early, channels), jnp.bfloat16),
        in_specs=[smem] + [vmem] * len(returned),
        out_specs=vmem,
        scratch_shapes=[
            pltpu.VMEM((owners * early, row_width), jnp.float32),
            pltpu.VMEM((bag_width, early, row_width), jnp.float32),
        ],
        compiler_params=pltpu.CompilerParams(vmem_limit_bytes=32 * megabyte),
        cost_estimate=pl.CostEstimate(
            flops=0, bytes_accessed=24 * megabyte, transcendentals=0
        ),
        name="pool",
    )(place, weight_by_slot, *returned[:-1])
    corner = tie(corner, pooled)
    filters = [line, by_table, by_rep, corner]
    filters = filters + [swapped(block, "table", 1) for block in filters]
    if conv_weight.shape[1] % 16:
        filters = [ordered_filters(filters, me)]

    hidden = pl.pallas_call(
        functools.partial(stage_kernel, len(returned), len(filters)),
        out_shape=jax.ShapeDtypeStruct((token_count, channels), jnp.bfloat16),
        in_specs=[smem] * 2 + [vmem] * (4 + len(returned)) + [anywhere] * len(filters),
        out_specs=anywhere,
        scratch_shapes=[
            pltpu.VMEM((owners * cuts[-1], row_width), jnp.float32),
            pltpu.VMEM((bag_width, late, row_width), jnp.float32),
            pltpu.VMEM((conv_weight.shape[0], 3 * channels, channels), jnp.bfloat16),
            pltpu.VMEM((token_count + 16, channels), jnp.float32),
            pltpu.VMEM((token_count + 16, channels), jnp.float32),
            pltpu.VMEM((token_count, channels), jnp.bfloat16),
            pltpu.SemaphoreType.DMA((2 * owners,)),
            pltpu.SemaphoreType.DMA(((token_count + 255) // 256,)),
        ],
        compiler_params=pltpu.CompilerParams(vmem_limit_bytes=56 * megabyte),
        cost_estimate=pl.CostEstimate(
            flops=2 * token_count * 3 * channels * channels * conv_weight.shape[0],
            bytes_accessed=24 * megabyte,
            transcendentals=0,
        ),
        name="stage",
    )(place, me, weight_by_slot, state, norm_gain, pooled, *returned, *filters)
    return hidden.reshape(samples_here, slot_count, channels)


def solution(mesh):
    in_specs = (
        P(("table", "rep"), None, None),
        P(("table", "rep"), None, None),
        P(("table", "rep"), None, None),
        P(None, "table", None),
        P(("table", "rep")),
        P(("table", "rep")),
        P(("table", "rep")),
        P(("table", "rep"), None, None),
        P(None, "table", None),
        P(),
    )
    out_specs = P(("table", "rep"), None, None)
    return jax.shard_map(local, mesh=mesh, in_specs=in_specs, out_specs=out_specs, check_vma=False)
```

```python
import functools
import jax
import jax.numpy as jnp
from jax import lax
from jax.experimental import pallas as pl
from jax.experimental.pallas import tpu as pltpu
from jax.sharding import PartitionSpec as P

table_of_id = (0, 1, 2, 2, 3, 3, 3, 3)
bag_bounds = ((0, 1), (1, 2), (2, 4), (4, 8))
epsilon = 1e-05
part_ends = (0.25, 5 / 6, 1.0)
megabyte = 1024 * 1024


def prep_kernel(cuts, shard_rows, rows_hbm, owner_hbm, request_ref, place_ref, *scratch):
    rows_ref, owner_ref, sems = scratch
    rows_copy = pltpu.make_async_copy(rows_hbm, rows_ref, sems.at[0])
    owner_copy = pltpu.make_async_copy(owner_hbm, owner_ref, sems.at[1])
    rows_copy.start()
    owner_copy.start()
    rows_copy.wait()
    owner_copy.wait()
    owner = owner_ref[...]
    rows = rows_ref[...]
    owners = request_ref.shape[0]
    width, slots = owner.shape
    value_bits = (len(bag_bounds) * shard_rows).bit_length()
    owner_ids = lax.broadcasted_iota(jnp.int32, (owners, slots), 0)
    lane = lax.broadcasted_iota(jnp.int32, (owners, slots), 1)
    value = jnp.zeros((owners, slots), jnp.int32)
    for k in range(width):
        named = owner[k : k + 1, :] == owner_ids
        value = jnp.where(named, rows[k : k + 1, :] + (table_of_id[k] * shard_rows + 1), value)
    present = jnp.where(value > 0, 1, 0)
    rank = present
    step = 1
    while step < slots:
        rank = rank + jnp.where(lane >= step, pltpu.roll(rank, step, 1), 0)
        step *= 2
    rank = rank - present
    place = jnp.zeros((width, slots), jnp.int32)
    for number in range(owners):
        place = jnp.where(owner == number, rank[number : number + 1, :], place)
    landing = jnp.zeros((width, slots), jnp.int32)
    for start, stop in zip(cuts[:-1], cuts[1:]):
        where = owners * start + owner * (stop - start) + place - start
        landing = jnp.where(place >= start, where, landing)
    place_ref[...] = landing
    packed = jnp.where(value > 0, ((lane - rank) << value_bits) + value, 0)
    step = 1
    level = value_bits
    while step < slots:
        moving = jnp.where(((packed >> level) & 1) == 1, packed, 0)
        packed = (packed - moving) + pltpu.roll(moving, slots - step, 1)
        step *= 2
        level += 1
    value = jnp.maximum((packed & ((1 << value_bits) - 1)) - 1, 0)
    for number in range(owners):
        request_ref[number] = value[number : number + 1, : request_ref.shape[2]]


def pass_kernel(*refs):
    pass


def tie(array, *others):
    anywhere = pl.BlockSpec(memory_space=pl.ANY)
    return pl.pallas_call(
        pass_kernel,
        out_shape=jax.ShapeDtypeStruct(array.shape, array.dtype),
        in_specs=[anywhere] * (1 + len(others)),
        out_specs=anywhere,
        input_output_aliases={0: 0},
        name="tie",
    )(array, *others)


def gather_kernel(capacity, first, index_ref, table_ref, *refs):
    out_ref, narrow, wide, picked, packed, index, index_sem, table_sems, out_sems = refs[-9:]
    owners, piece, _ = out_ref.shape
    unroll = 32 if piece % 32 == 0 else 16
    blocks = table_sems.shape[0]
    block_rows = table_ref.shape[0] // blocks
    table_copies = []
    for block in range(blocks):
        part = pl.ds(block * block_rows, block_rows)
        copy = pltpu.make_async_copy(table_ref.at[part, :], narrow.at[part, :], table_sems.at[block])
        copy.start()
        table_copies.append(copy)
    index_copy = pltpu.make_async_copy(index_ref, index, index_sem)
    index_copy.start()
    rows = 256

    for block in range(blocks):
        table_copies[block].wait()

        def widen(step, carry, block=block):
            base = pl.multiple_of(block * block_rows + step * rows, rows)
            wide[pl.ds(base, rows), :] = narrow[pl.ds(base, rows), :].astype(jnp.float32)
            return carry

        lax.fori_loop(0, block_rows // rows, widen, 0)
    index_copy.wait()
    copies = []
    for number in range(owners):
        origin = number * capacity + first

        def some_rows(block, carry, origin=origin):
            base = pl.multiple_of(block * unroll, unroll)
            picks = [index[origin + base + i] for i in range(unroll)]
            found = [wide[pl.ds(pick, 1), :] for pick in picks]
            for i in range(unroll):
                picked[pl.ds(base + i, 1), :] = found[i]
            return carry

        lax.fori_loop(0, piece // unroll, some_rows, 0)
        packed[number] = picked[...].astype(jnp.bfloat16)
        copy = pltpu.make_async_copy(packed.at[number], out_ref.at[number], out_sems.at[number])
        copy.start()
        copies.append(copy)
    for copy in copies:
        copy.wait()


def pool_slots(first, place_ref, weight_ref, piece_refs, table, picked, put):
    width, slots, lanes = picked.shape
    start = 0
    for piece_ref in piece_refs:
        count = piece_ref.shape[0]
        rows = 256

        def widen(step, carry, piece_ref=piece_ref, start=start):
            base = pl.multiple_of(step * rows, rows)
            table[pl.ds(start + base, rows), :] = piece_ref[pl.ds(base, rows), :].astype(jnp.float32)
            return carry

        lax.fori_loop(0, count // rows, widen, 0)
        start += count

    def some_slots(step, carry):
        base = pl.multiple_of(step * 8, 8)
        for k in range(width):
            picks = [place_ref[k, first + base + i] for i in range(8)]
            rows = [table[pl.ds(pick, 1), :] for pick in picks]
            for i in range(8):
                picked[k, pl.ds(base + i, 1), :] = rows[i]
        return carry

    lax.fori_loop(0, slots // 8, some_slots, 0)
    weights = jnp.transpose(weight_ref[:, first : first + slots])
    for t, (lower, upper) in enumerate(bag_bounds):
        total = picked[lower] * weights[:, lower : lower + 1]
        for k in range(lower + 1, upper):
            total = total + picked[k] * weights[:, k : k + 1]
        put(slice(t * lanes, (t + 1) * lanes), total.astype(jnp.bfloat16))


def pool_kernel(place_ref, weight_ref, *refs):
    out_ref, table, picked = refs[-3:]

    def put(columns, total):
        out_ref[:, columns] = total

    pool_slots(0, place_ref, weight_ref, refs[:-3], table, picked, put)


def stage_kernel(
    pieces, sources, place_ref, me_ref, weight_ref, carried_ref, gain_ref, pooled_ref, *refs
):
    piece_refs = refs[:pieces]
    filter_refs = refs[pieces : pieces + sources]
    out_ref, table, picked, filters, first_buf, second_buf, result = refs[pieces + sources :][:7]
    filter_sems, out_sems = refs[pieces + sources :][7:]
    slots = result.shape[0]
    layers = filters.shape[0]
    filter_copies = []
    if sources == 1:
        filter_copies.append(pltpu.make_async_copy(filter_refs[0], filters, filter_sems.at[0]))
    else:
        held, half, depth, _ = filter_refs[0].shape
        for group, filter_ref in enumerate(filter_refs):
            bits, side = block_place(group, me_ref[1])
            for number in range(filter_ref.shape[0]):
                owner = me_ref[0] ^ (4 * number + bits)
                rows = pl.ds(pl.multiple_of(owner * depth, depth), depth)
                filter_copies.append(
                    pltpu.make_async_copy(
                        filter_ref.at[number],
                        filters.at[pl.ds(side * half, half), rows, :],
                        filter_sems.at[len(filter_copies)],
                    )
                )
    for copy in filter_copies:
        copy.start()
    front = 16
    early = pooled_ref.shape[0]
    first_buf[front : front + early, :] = pooled_ref[...].astype(jnp.float32)

    def put(columns, total):
        first_buf[front + early :, columns] = total.astype(jnp.float32)

    pool_slots(early, place_ref, weight_ref, piece_refs, table, picked, put)
    for copy in filter_copies:
        copy.wait()
    offset = 0
    out_copies = []
    for layer in range(layers):
        dilation = 2**layer
        span = 2 * dilation
        source, target = (first_buf, second_buf) if layer % 2 == 0 else (second_buf, first_buf)
        source[front - span : front, :] = carried_ref[offset : offset + span, :]
        offset += span
        for begin in range(0, slots, 256):
            rows = min(256, slots - begin)
            base = front + begin
            taps = [
                source[base - tap * dilation : base - tap * dilation + rows, :].astype(jnp.bfloat16)
                for tap in range(3)
            ]
            output = jnp.dot(
                jnp.concatenate(taps, axis=1), filters[layer], preferred_element_type=jnp.float32
            )
            mean = jnp.mean(output, axis=-1, keepdims=True)
            centred = output - mean
            spread = jnp.mean(centred * centred, axis=-1, keepdims=True)
            active = jnp.maximum(
                centred * lax.rsqrt(spread + epsilon) * gain_ref[layer : layer + 1, :], 0.0
            )
            if layer % 2 == 1:
                active = active + target[base : base + rows, :]
            active = active.astype(jnp.bfloat16)
            if layer == layers - 1:
                result[begin : begin + rows, :] = active
                copy = pltpu.make_async_copy(
                    result.at[pl.ds(begin, rows), :],
                    out_ref.at[pl.ds(begin, rows), :],
                    out_sems.at[len(out_copies)],
                )
                copy.start()
                out_copies.append(copy)
            else:
                target[base : base + rows, :] = active.astype(jnp.float32)
    for copy in out_copies:
        copy.wait()


def swapped(array, axis, distance):
    pairs = [(source, source ^ distance) for source in range(lax.axis_size(axis))]
    return lax.ppermute(array, axis, pairs)


def block_place(number, side):
    kind = number % 4
    bits = (2 if kind in (1, 3) else 0) + number // 4
    return bits, side if kind < 2 else 1 - side


def ordered_filters(blocks, me):
    count = blocks[0].shape[0]
    owners = 4 * count
    half = blocks[0].shape[1]
    layers = 2 * half
    whole = jnp.zeros((owners, layers) + blocks[0].shape[2:], blocks[0].dtype)
    for number, block in enumerate(blocks):
        bits, side = block_place(number, me[1])
        for shard in range(block.shape[0]):
            owner = me[0] ^ (4 * shard + bits)
            whole = lax.dynamic_update_slice(whole, block[shard][None], (owner, side * half, 0, 0))
    return whole.transpose(1, 0, 2, 3).reshape(layers, -1, whole.shape[-1])


def carried_rows(returning, home, entry, stores):
    copies = lax.axis_size("rep")
    me = lax.axis_index("rep")
    by_position = stores.transpose(1, 0, 2)
    positions, _, channels = by_position.shape
    carried = jnp.zeros((positions, channels), stores.dtype)
    for shift in range(copies):
        arrived = by_position
        if shift:
            pairs = [(source, (source + shift) % copies) for source in range(copies)]
            arrived = lax.ppermute(by_position, "rep", pairs)
        wanted = (returning[0] > 0) & (home[0] == (me + copies - shift) % copies)
        chosen = lax.dynamic_index_in_dim(arrived, entry[0], 1, keepdims=False)
        carried = jnp.where(wanted, chosen, carried)
    return carried.astype(jnp.float32)


def local(
    bag_rows, bag_owner, bag_weight, tables, returning, home, entry, stores, conv_weight, norm_gain
):
    owners = lax.axis_size("table")
    samples_here, slot_count, bag_width = bag_rows.shape
    token_count = samples_here * slot_count
    shard_rows = tables.shape[1]
    row_width = tables.shape[2]
    channels = conv_weight.shape[-1]
    capacity = min(token_count, (3 * token_count * bag_width + 2 * owners - 1) // (2 * owners))
    cuts = [0] + [round(capacity * end) // 16 * 16 for end in part_ends]
    early = cuts[-2]
    late = token_count - early
    smem = pl.BlockSpec(memory_space=pltpu.SMEM)
    vmem = pl.BlockSpec(memory_space=pltpu.VMEM)
    anywhere = pl.BlockSpec(memory_space=pl.ANY)

    me = jnp.stack([lax.axis_index("table"), lax.axis_index("rep") % 2]).astype(jnp.int32)
    half = conv_weight.shape[0] // 2
    shard = lax.dynamic_slice_in_dim(conv_weight, me[1] * half, half, 0)
    middle = owners // 8
    line = [shard] + [swapped(shard, "table", 4 * step) for step in range(1, middle + 1)]
    state = carried_rows(returning, home, entry, stores)
    rows_by_slot = bag_rows.reshape(token_count, bag_width).T
    owner_by_slot = bag_owner.reshape(token_count, bag_width).T
    requests, place = pl.pallas_call(
        functools.partial(prep_kernel, cuts, shard_rows),
        out_shape=(
            jax.ShapeDtypeStruct((owners, 1, capacity), jnp.int32),
            jax.ShapeDtypeStruct((bag_width, token_count), jnp.int32),
        ),
        in_specs=[anywhere, anywhere],
        out_specs=(vmem, vmem),
        scratch_shapes=[
            pltpu.VMEM(rows_by_slot.shape, jnp.int32),
            pltpu.VMEM(rows_by_slot.shape, jnp.int32),
            pltpu.SemaphoreType.DMA((2,)),
        ],
        compiler_params=pltpu.CompilerParams(vmem_limit_bytes=60 * megabyte),
        name="prep",
    )(rows_by_slot, owner_by_slot)
    received = lax.all_to_all(requests, "table", split_axis=0, concat_axis=0, tiled=True)
    received = received.reshape(owners * capacity)
    flat_table = tables.reshape(-1, row_width)
    returned = []
    sent = []
    for number in range(len(part_ends)):
        piece = cuts[number + 1] - cuts[number]
        if number == 1:
            middle_shard = tie(line[middle], received)
            forwarded = [swapped(middle_shard, "table", 4 * step) for step in range(1, middle)]
            line = line[:middle] + [middle_shard] + forwarded
        earlier = sent[-1:] if sent else line[1:]
        sent.append(
            pl.pallas_call(
                functools.partial(gather_kernel, capacity, cuts[number]),
                out_shape=jax.ShapeDtypeStruct((owners, piece, row_width), jnp.bfloat16),
                in_specs=[anywhere] * (2 + len(earlier)),
                out_specs=anywhere,
                scratch_shapes=[
                    pltpu.VMEM(flat_table.shape, jnp.bfloat16),
                    pltpu.VMEM(flat_table.shape, jnp.float32),
                    pltpu.VMEM((piece, row_width), jnp.float32),
                    pltpu.VMEM((owners, piece, row_width), jnp.bfloat16),
                    pltpu.SMEM((owners * capacity,), jnp.int32),
                    pltpu.SemaphoreType.DMA,
                    pltpu.SemaphoreType.DMA((8,)),
                    pltpu.SemaphoreType.DMA((owners,)),
                ],
                compiler_params=pltpu.CompilerParams(vmem_limit_bytes=58 * megabyte),
                cost_estimate=pl.CostEstimate(
                    flops=0, bytes_accessed=20 * megabyte, transcendentals=0
                ),
                name="owner_gather",
            )(received, flat_table, *earlier)
        )
    line = jnp.stack(line)
    by_table = swapped(line, "table", 2)
    by_rep = swapped(line, "rep", 1)
    corner = swapped(by_table, "rep", 1)
    gates = [[], [sent[2]] + forwarded, [state, by_table, by_rep]]
    for rows, gate in zip(sent, gates):
        if returned:
            rows = tie(rows, returned[-1][:16], *gate)
        arrived = lax.all_to_all(rows, "table", split_axis=0, concat_axis=0, tiled=True)
        returned.append(arrived.reshape(-1, row_width))
    weight_by_slot = bag_weight.reshape(token_count, bag_width).T
    pooled = pl.pallas_call(
        pool_kernel,
        out_shape=jax.ShapeDtypeStruct((early, channels), jnp.bfloat16),
        in_specs=[smem] + [vmem] * len(returned),
        out_specs=vmem,
        scratch_shapes=[
            pltpu.VMEM((owners * early, row_width), jnp.float32),
            pltpu.VMEM((bag_width, early, row_width), jnp.float32),
        ],
        compiler_params=pltpu.CompilerParams(vmem_limit_bytes=32 * megabyte),
        cost_estimate=pl.CostEstimate(
            flops=0, bytes_accessed=24 * megabyte, transcendentals=0
        ),
        name="pool",
    )(place, weight_by_slot, *returned[:-1])
    corner = tie(corner, pooled)
    filters = [line, by_table, by_rep, corner]
    filters = filters + [swapped(block, "table", 1) for block in filters]
    if conv_weight.shape[1] % 16:
        filters = [ordered_filters(filters, me)]

    hidden = pl.pallas_call(
        functools.partial(stage_kernel, len(returned), len(filters)),
        out_shape=jax.ShapeDtypeStruct((token_count, channels), jnp.bfloat16),
        in_specs=[smem] * 2 + [vmem] * (4 + len(returned)) + [anywhere] * len(filters),
        out_specs=anywhere,
        scratch_shapes=[
            pltpu.VMEM((owners * cuts[-1], row_width), jnp.float32),
            pltpu.VMEM((bag_width, late, row_width), jnp.float32),
            pltpu.VMEM((conv_weight.shape[0], 3 * channels, channels), jnp.bfloat16),
            pltpu.VMEM((token_count + 16, channels), jnp.float32),
            pltpu.VMEM((token_count + 16, channels), jnp.float32),
            pltpu.VMEM((token_count, channels), jnp.bfloat16),
            pltpu.SemaphoreType.DMA((2 * owners,)),
            pltpu.SemaphoreType.DMA(((token_count + 255) // 256,)),
        ],
        compiler_params=pltpu.CompilerParams(vmem_limit_bytes=56 * megabyte),
        cost_estimate=pl.CostEstimate(
            flops=2 * token_count * 3 * channels * channels * conv_weight.shape[0],
            bytes_accessed=24 * megabyte,
            transcendentals=0,
        ),
        name="stage",
    )(place, me, weight_by_slot, state, norm_gain, pooled, *returned, *filters)
    return hidden.reshape(samples_here, slot_count, channels)


def solution(mesh):
    in_specs = (
        P(("table", "rep"), None, None),
        P(("table", "rep"), None, None),
        P(("table", "rep"), None, None),
        P(None, "table", None),
        P(("table", "rep")),
        P(("table", "rep")),
        P(("table", "rep")),
        P(("table", "rep"), None, None),
        P(None, "table", None),
        P(),
    )
    out_specs = P(("table", "rep"), None, None)
    return jax.shard_map(local, mesh=mesh, in_specs=in_specs, out_specs=out_specs, check_vma=False)
```

```python
import functools
import jax
import jax.numpy as jnp
from jax import lax
from jax.experimental import pallas as pl
from jax.experimental.pallas import tpu as pltpu
from jax.sharding import PartitionSpec as P

table_of_id = (0, 1, 2, 2, 3, 3, 3, 3)
bag_bounds = ((0, 1), (1, 2), (2, 4), (4, 8))
epsilon = 1e-05
part_ends = (0.25, 5 / 6, 1.0)
megabyte = 1024 * 1024


def prep_kernel(cuts, shard_rows, rows_ref, owner_ref, request_ref, place_ref):
    owner = owner_ref[...]
    rows = rows_ref[...]
    owners = request_ref.shape[0]
    width, slots = owner.shape
    value_bits = (len(bag_bounds) * shard_rows).bit_length()
    owner_ids = lax.broadcasted_iota(jnp.int32, (owners, slots), 0)
    lane = lax.broadcasted_iota(jnp.int32, (owners, slots), 1)
    value = jnp.zeros((owners, slots), jnp.int32)
    for k in range(width):
        named = owner[k : k + 1, :] == owner_ids
        value = jnp.where(named, rows[k : k + 1, :] + (table_of_id[k] * shard_rows + 1), value)
    present = jnp.where(value > 0, 1, 0)
    rank = present
    step = 1
    while step < slots:
        rank = rank + jnp.where(lane >= step, pltpu.roll(rank, step, 1), 0)
        step *= 2
    rank = rank - present
    place = jnp.zeros((width, slots), jnp.int32)
    for number in range(owners):
        place = jnp.where(owner == number, rank[number : number + 1, :], place)
    landing = jnp.zeros((width, slots), jnp.int32)
    for start, stop in zip(cuts[:-1], cuts[1:]):
        where = owners * start + owner * (stop - start) + place - start
        landing = jnp.where(place >= start, where, landing)
    place_ref[...] = landing
    packed = jnp.where(value > 0, ((lane - rank) << value_bits) + value, 0)
    step = 1
    level = value_bits
    while step < slots:
        moving = jnp.where(((packed >> level) & 1) == 1, packed, 0)
        packed = (packed - moving) + pltpu.roll(moving, slots - step, 1)
        step *= 2
        level += 1
    value = jnp.maximum((packed & ((1 << value_bits) - 1)) - 1, 0)
    for number in range(owners):
        request_ref[number] = value[number : number + 1, : request_ref.shape[2]]


def pass_kernel(*refs):
    pass


def tie(array, *others):
    anywhere = pl.BlockSpec(memory_space=pl.ANY)
    return pl.pallas_call(
        pass_kernel,
        out_shape=jax.ShapeDtypeStruct(array.shape, array.dtype),
        in_specs=[anywhere] * (1 + len(others)),
        out_specs=anywhere,
        input_output_aliases={0: 0},
        name="tie",
    )(array, *others)


def gather_kernel(capacity, first, index_ref, table_ref, *refs):
    out_ref, narrow, wide, picked, packed, index, index_sem, table_sems, out_sems = refs[-9:]
    owners, piece, _ = out_ref.shape
    unroll = 32 if piece % 32 == 0 else 16
    blocks = table_sems.shape[0]
    block_rows = table_ref.shape[0] // blocks
    table_copies = []
    for block in range(blocks):
        part = pl.ds(block * block_rows, block_rows)
        copy = pltpu.make_async_copy(table_ref.at[part, :], narrow.at[part, :], table_sems.at[block])
        copy.start()
        table_copies.append(copy)
    index_copy = pltpu.make_async_copy(index_ref, index, index_sem)
    index_copy.start()
    rows = 256

    for block in range(blocks):
        table_copies[block].wait()

        def widen(step, carry, block=block):
            base = pl.multiple_of(block * block_rows + step * rows, rows)
            wide[pl.ds(base, rows), :] = narrow[pl.ds(base, rows), :].astype(jnp.float32)
            return carry

        lax.fori_loop(0, block_rows // rows, widen, 0)
    index_copy.wait()
    copies = []
    for number in range(owners):
        origin = number * capacity + first

        def some_rows(block, carry, origin=origin):
            base = pl.multiple_of(block * unroll, unroll)
            picks = [index[origin + base + i] for i in range(unroll)]
            found = [wide[pl.ds(pick, 1), :] for pick in picks]
            for i in range(unroll):
                picked[pl.ds(base + i, 1), :] = found[i]
            return carry

        lax.fori_loop(0, piece // unroll, some_rows, 0)
        packed[number] = picked[...].astype(jnp.bfloat16)
        copy = pltpu.make_async_copy(packed.at[number], out_ref.at[number], out_sems.at[number])
        copy.start()
        copies.append(copy)
    for copy in copies:
        copy.wait()


def pool_slots(first, place_ref, weight_ref, piece_refs, table, picked, put):
    width, slots, lanes = picked.shape
    start = 0
    for piece_ref in piece_refs:
        count = piece_ref.shape[0]
        rows = 256

        def widen(step, carry, piece_ref=piece_ref, start=start):
            base = pl.multiple_of(step * rows, rows)
            table[pl.ds(start + base, rows), :] = piece_ref[pl.ds(base, rows), :].astype(jnp.float32)
            return carry

        lax.fori_loop(0, count // rows, widen, 0)
        start += count

    def some_slots(step, carry):
        base = pl.multiple_of(step * 8, 8)
        for k in range(width):
            picks = [place_ref[k, first + base + i] for i in range(8)]
            rows = [table[pl.ds(pick, 1), :] for pick in picks]
            for i in range(8):
                picked[k, pl.ds(base + i, 1), :] = rows[i]
        return carry

    lax.fori_loop(0, slots // 8, some_slots, 0)
    weights = jnp.transpose(weight_ref[:, first : first + slots])
    for t, (lower, upper) in enumerate(bag_bounds):
        total = picked[lower] * weights[:, lower : lower + 1]
        for k in range(lower + 1, upper):
            total = total + picked[k] * weights[:, k : k + 1]
        put(slice(t * lanes, (t + 1) * lanes), total.astype(jnp.bfloat16))


def pool_kernel(place_ref, weight_ref, *refs):
    out_ref, table, picked = refs[-3:]

    def put(columns, total):
        out_ref[:, columns] = total

    pool_slots(0, place_ref, weight_ref, refs[:-3], table, picked, put)


def stage_kernel(
    pieces, sources, place_ref, me_ref, weight_ref, carried_ref, gain_ref, pooled_ref, *refs
):
    piece_refs = refs[:pieces]
    filter_refs = refs[pieces : pieces + sources]
    out_ref, table, picked, filters, first_buf, second_buf, result = refs[pieces + sources :][:7]
    filter_sems, out_sems = refs[pieces + sources :][7:]
    slots = result.shape[0]
    layers = filters.shape[0]
    filter_copies = []
    if sources == 1:
        filter_copies.append(pltpu.make_async_copy(filter_refs[0], filters, filter_sems.at[0]))
    else:
        held, half, depth, _ = filter_refs[0].shape
        for group, filter_ref in enumerate(filter_refs):
            bits, side = block_place(group, me_ref[1])
            for number in range(filter_ref.shape[0]):
                owner = me_ref[0] ^ (4 * number + bits)
                rows = pl.ds(pl.multiple_of(owner * depth, depth), depth)
                filter_copies.append(
                    pltpu.make_async_copy(
                        filter_ref.at[number],
                        filters.at[pl.ds(side * half, half), rows, :],
                        filter_sems.at[len(filter_copies)],
                    )
                )
    for copy in filter_copies:
        copy.start()
    front = 16
    early = pooled_ref.shape[0]
    first_buf[front : front + early, :] = pooled_ref[...].astype(jnp.float32)

    def put(columns, total):
        first_buf[front + early :, columns] = total.astype(jnp.float32)

    pool_slots(early, place_ref, weight_ref, piece_refs, table, picked, put)
    for copy in filter_copies:
        copy.wait()
    offset = 0
    out_copies = []
    for layer in range(layers):
        dilation = 2**layer
        span = 2 * dilation
        source, target = (first_buf, second_buf) if layer % 2 == 0 else (second_buf, first_buf)
        source[front - span : front, :] = carried_ref[offset : offset + span, :]
        offset += span
        for begin in range(0, slots, 256):
            rows = min(256, slots - begin)
            base = front + begin
            taps = [
                source[base - tap * dilation : base - tap * dilation + rows, :].astype(jnp.bfloat16)
                for tap in range(3)
            ]
            output = jnp.dot(
                jnp.concatenate(taps, axis=1), filters[layer], preferred_element_type=jnp.float32
            )
            mean = jnp.mean(output, axis=-1, keepdims=True)
            centred = output - mean
            spread = jnp.mean(centred * centred, axis=-1, keepdims=True)
            active = jnp.maximum(
                centred * lax.rsqrt(spread + epsilon) * gain_ref[layer : layer + 1, :], 0.0
            )
            if layer % 2 == 1:
                active = active + target[base : base + rows, :]
            active = active.astype(jnp.bfloat16)
            if layer == layers - 1:
                result[begin : begin + rows, :] = active
                copy = pltpu.make_async_copy(
                    result.at[pl.ds(begin, rows), :],
                    out_ref.at[pl.ds(begin, rows), :],
                    out_sems.at[len(out_copies)],
                )
                copy.start()
                out_copies.append(copy)
            else:
                target[base : base + rows, :] = active.astype(jnp.float32)
    for copy in out_copies:
        copy.wait()


def swapped(array, axis, distance):
    pairs = [(source, source ^ distance) for source in range(lax.axis_size(axis))]
    return lax.ppermute(array, axis, pairs)


def block_place(number, side):
    kind = number % 4
    bits = (2 if kind in (1, 3) else 0) + number // 4
    return bits, side if kind < 2 else 1 - side


def ordered_filters(blocks, me):
    count = blocks[0].shape[0]
    owners = 4 * count
    half = blocks[0].shape[1]
    layers = 2 * half
    whole = jnp.zeros((owners, layers) + blocks[0].shape[2:], blocks[0].dtype)
    for number, block in enumerate(blocks):
        bits, side = block_place(number, me[1])
        for shard in range(block.shape[0]):
            owner = me[0] ^ (4 * shard + bits)
            whole = lax.dynamic_update_slice(whole, block[shard][None], (owner, side * half, 0, 0))
    return whole.transpose(1, 0, 2, 3).reshape(layers, -1, whole.shape[-1])


def carried_rows(returning, home, entry, stores):
    copies = lax.axis_size("rep")
    me = lax.axis_index("rep")
    by_position = stores.transpose(1, 0, 2)
    positions, _, channels = by_position.shape
    carried = jnp.zeros((positions, channels), stores.dtype)
    for shift in range(copies):
        arrived = by_position
        if shift:
            pairs = [(source, (source + shift) % copies) for source in range(copies)]
            arrived = lax.ppermute(by_position, "rep", pairs)
        wanted = (returning[0] > 0) & (home[0] == (me + copies - shift) % copies)
        chosen = lax.dynamic_index_in_dim(arrived, entry[0], 1, keepdims=False)
        carried = jnp.where(wanted, chosen, carried)
    return carried.astype(jnp.float32)


def local(
    bag_rows, bag_owner, bag_weight, tables, returning, home, entry, stores, conv_weight, norm_gain
):
    owners = lax.axis_size("table")
    samples_here, slot_count, bag_width = bag_rows.shape
    token_count = samples_here * slot_count
    shard_rows = tables.shape[1]
    row_width = tables.shape[2]
    channels = conv_weight.shape[-1]
    capacity = min(token_count, (3 * token_count * bag_width + 2 * owners - 1) // (2 * owners))
    cuts = [0] + [round(capacity * end) // 16 * 16 for end in part_ends]
    early = cuts[-2]
    late = token_count - early
    smem = pl.BlockSpec(memory_space=pltpu.SMEM)
    vmem = pl.BlockSpec(memory_space=pltpu.VMEM)
    anywhere = pl.BlockSpec(memory_space=pl.ANY)

    me = jnp.stack([lax.axis_index("table"), lax.axis_index("rep") % 2]).astype(jnp.int32)
    half = conv_weight.shape[0] // 2
    shard = lax.dynamic_slice_in_dim(conv_weight, me[1] * half, half, 0)
    middle = owners // 8
    line = [shard] + [swapped(shard, "table", 4 * step) for step in range(1, middle + 1)]
    state = carried_rows(returning, home, entry, stores)
    rows_by_slot = bag_rows.reshape(token_count, bag_width).T
    owner_by_slot = bag_owner.reshape(token_count, bag_width).T
    requests, place = pl.pallas_call(
        functools.partial(prep_kernel, cuts, shard_rows),
        out_shape=(
            jax.ShapeDtypeStruct((owners, 1, capacity), jnp.int32),
            jax.ShapeDtypeStruct((bag_width, token_count), jnp.int32),
        ),
        in_specs=[vmem, vmem],
        out_specs=(vmem, vmem),
        compiler_params=pltpu.CompilerParams(vmem_limit_bytes=8 * megabyte),
        name="prep",
    )(rows_by_slot, owner_by_slot)
    received = lax.all_to_all(requests, "table", split_axis=0, concat_axis=0, tiled=True)
    received = received.reshape(owners * capacity)
    flat_table = tables.reshape(-1, row_width)
    returned = []
    sent = []
    for number in range(len(part_ends)):
        piece = cuts[number + 1] - cuts[number]
        if number == 1:
            middle_shard = tie(line[middle], received)
            forwarded = [swapped(middle_shard, "table", 4 * step) for step in range(1, middle)]
            line = line[:middle] + [middle_shard] + forwarded
        earlier = sent[-1:] if sent else line[1:]
        sent.append(
            pl.pallas_call(
                functools.partial(gather_kernel, capacity, cuts[number]),
                out_shape=jax.ShapeDtypeStruct((owners, piece, row_width), jnp.bfloat16),
                in_specs=[anywhere] * (2 + len(earlier)),
                out_specs=anywhere,
                scratch_shapes=[
                    pltpu.VMEM(flat_table.shape, jnp.bfloat16),
                    pltpu.VMEM(flat_table.shape, jnp.float32),
                    pltpu.VMEM((piece, row_width), jnp.float32),
                    pltpu.VMEM((owners, piece, row_width), jnp.bfloat16),
                    pltpu.SMEM((owners * capacity,), jnp.int32),
                    pltpu.SemaphoreType.DMA,
                    pltpu.SemaphoreType.DMA((8,)),
                    pltpu.SemaphoreType.DMA((owners,)),
                ],
                compiler_params=pltpu.CompilerParams(vmem_limit_bytes=58 * megabyte),
                cost_estimate=pl.CostEstimate(
                    flops=0, bytes_accessed=20 * megabyte, transcendentals=0
                ),
                name="owner_gather",
            )(received, flat_table, *earlier)
        )
    line = jnp.stack(line)
    by_table = swapped(line, "table", 2)
    by_rep = swapped(line, "rep", 1)
    by_table = tie(by_table, state)
    corner = swapped(by_table, "rep", 1)
    gates = [[], [sent[2]] + forwarded, [state, by_table, by_rep]]
    for rows, gate in zip(sent, gates):
        if returned:
            rows = tie(rows, returned[-1][: 16 if len(returned) > 1 else None], *gate)
        arrived = lax.all_to_all(rows, "table", split_axis=0, concat_axis=0, tiled=True)
        returned.append(arrived.reshape(-1, row_width))
    weight_by_slot = bag_weight.reshape(token_count, bag_width).T
    pooled = pl.pallas_call(
        pool_kernel,
        out_shape=jax.ShapeDtypeStruct((early, channels), jnp.bfloat16),
        in_specs=[smem] + [vmem] * len(returned),
        out_specs=vmem,
        scratch_shapes=[
            pltpu.VMEM((owners * early, row_width), jnp.float32),
            pltpu.VMEM((bag_width, early, row_width), jnp.float32),
        ],
        compiler_params=pltpu.CompilerParams(vmem_limit_bytes=32 * megabyte),
        cost_estimate=pl.CostEstimate(
            flops=0, bytes_accessed=24 * megabyte, transcendentals=0
        ),
        name="pool",
    )(place, weight_by_slot, *returned[:-1])
    corner = tie(corner, pooled)
    filters = [line, by_table, by_rep, corner]
    filters = filters + [swapped(block, "table", 1) for block in filters]
    if conv_weight.shape[1] % 16:
        filters = [ordered_filters(filters, me)]

    hidden = pl.pallas_call(
        functools.partial(stage_kernel, len(returned), len(filters)),
        out_shape=jax.ShapeDtypeStruct((token_count, channels), jnp.bfloat16),
        in_specs=[smem] * 2 + [vmem] * (4 + len(returned)) + [anywhere] * len(filters),
        out_specs=anywhere,
        scratch_shapes=[
            pltpu.VMEM((owners * cuts[-1], row_width), jnp.float32),
            pltpu.VMEM((bag_width, late, row_width), jnp.float32),
            pltpu.VMEM((conv_weight.shape[0], 3 * channels, channels), jnp.bfloat16),
            pltpu.VMEM((token_count + 16, channels), jnp.float32),
            pltpu.VMEM((token_count + 16, channels), jnp.float32),
            pltpu.VMEM((token_count, channels), jnp.bfloat16),
            pltpu.SemaphoreType.DMA((2 * owners,)),
            pltpu.SemaphoreType.DMA(((token_count + 255) // 256,)),
        ],
        compiler_params=pltpu.CompilerParams(vmem_limit_bytes=56 * megabyte),
        cost_estimate=pl.CostEstimate(
            flops=2 * token_count * 3 * channels * channels * conv_weight.shape[0],
            bytes_accessed=24 * megabyte,
            transcendentals=0,
        ),
        name="stage",
    )(place, me, weight_by_slot, state, norm_gain, pooled, *returned, *filters)
    return hidden.reshape(samples_here, slot_count, channels)


def solution(mesh):
    in_specs = (
        P(("table", "rep"), None, None),
        P(("table", "rep"), None, None),
        P(("table", "rep"), None, None),
        P(None, "table", None),
        P(("table", "rep")),
        P(("table", "rep")),
        P(("table", "rep")),
        P(("table", "rep"), None, None),
        P(None, "table", None),
        P(),
    )
    out_specs = P(("table", "rep"), None, None)
    return jax.shard_map(local, mesh=mesh, in_specs=in_specs, out_specs=out_specs, check_vma=False)
```

```python
import functools
import jax
import jax.numpy as jnp
from jax import lax
from jax.experimental import pallas as pl
from jax.experimental.pallas import tpu as pltpu
from jax.sharding import PartitionSpec as P

table_of_id = (0, 1, 2, 2, 3, 3, 3, 3)
bag_bounds = ((0, 1), (1, 2), (2, 4), (4, 8))
epsilon = 1e-05
part_ends = (0.25, 5 / 6, 1.0)
megabyte = 1024 * 1024


def prep_kernel(cuts, shard_rows, rows_ref, owner_ref, request_ref, place_ref):
    owner = owner_ref[...]
    rows = rows_ref[...]
    owners = request_ref.shape[0]
    width, slots = owner.shape
    value_bits = (len(bag_bounds) * shard_rows).bit_length()
    owner_ids = lax.broadcasted_iota(jnp.int32, (owners, slots), 0)
    lane = lax.broadcasted_iota(jnp.int32, (owners, slots), 1)
    value = jnp.zeros((owners, slots), jnp.int32)
    for k in range(width):
        named = owner[k : k + 1, :] == owner_ids
        value = jnp.where(named, rows[k : k + 1, :] + (table_of_id[k] * shard_rows + 1), value)
    present = jnp.where(value > 0, 1, 0)
    rank = present
    step = 1
    while step < slots:
        rank = rank + jnp.where(lane >= step, pltpu.roll(rank, step, 1), 0)
        step *= 2
    rank = rank - present
    place = jnp.zeros((width, slots), jnp.int32)
    for number in range(owners):
        place = jnp.where(owner == number, rank[number : number + 1, :], place)
    landing = jnp.zeros((width, slots), jnp.int32)
    for start, stop in zip(cuts[:-1], cuts[1:]):
        where = owners * start + owner * (stop - start) + place - start
        landing = jnp.where(place >= start, where, landing)
    place_ref[...] = landing
    packed = jnp.where(value > 0, ((lane - rank) << value_bits) + value, 0)
    step = 1
    level = value_bits
    while step < slots:
        moving = jnp.where(((packed >> level) & 1) == 1, packed, 0)
        packed = (packed - moving) + pltpu.roll(moving, slots - step, 1)
        step *= 2
        level += 1
    value = jnp.maximum((packed & ((1 << value_bits) - 1)) - 1, 0)
    for number in range(owners):
        request_ref[number] = value[number : number + 1, : request_ref.shape[2]]


def pass_kernel(*refs):
    pass


def tie(array, *others):
    anywhere = pl.BlockSpec(memory_space=pl.ANY)
    return pl.pallas_call(
        pass_kernel,
        out_shape=jax.ShapeDtypeStruct(array.shape, array.dtype),
        in_specs=[anywhere] * (1 + len(others)),
        out_specs=anywhere,
        input_output_aliases={0: 0},
        name="tie",
    )(array, *others)


def gather_kernel(capacity, first, index_ref, table_ref, *refs):
    out_ref, narrow, wide, picked, packed, index, index_sem, table_sems, out_sems = refs[-9:]
    owners, piece, _ = out_ref.shape
    unroll = 32 if piece % 32 == 0 else 16
    blocks = table_sems.shape[0]
    block_rows = table_ref.shape[0] // blocks
    table_copies = []
    for block in range(blocks):
        part = pl.ds(block * block_rows, block_rows)
        copy = pltpu.make_async_copy(table_ref.at[part, :], narrow.at[part, :], table_sems.at[block])
        copy.start()
        table_copies.append(copy)
    index_copy = pltpu.make_async_copy(index_ref, index, index_sem)
    index_copy.start()
    rows = 256

    for block in range(blocks):
        table_copies[block].wait()

        def widen(step, carry, block=block):
            base = pl.multiple_of(block * block_rows + step * rows, rows)
            wide[pl.ds(base, rows), :] = narrow[pl.ds(base, rows), :].astype(jnp.float32)
            return carry

        lax.fori_loop(0, block_rows // rows, widen, 0)
    index_copy.wait()
    copies = []
    for number in range(owners):
        origin = number * capacity + first

        def some_rows(block, carry, origin=origin):
            base = pl.multiple_of(block * unroll, unroll)
            picks = [index[origin + base + i] for i in range(unroll)]
            found = [wide[pl.ds(pick, 1), :] for pick in picks]
            for i in range(unroll):
                picked[pl.ds(base + i, 1), :] = found[i]
            return carry

        lax.fori_loop(0, piece // unroll, some_rows, 0)
        packed[number] = picked[...].astype(jnp.bfloat16)
        copy = pltpu.make_async_copy(packed.at[number], out_ref.at[number], out_sems.at[number])
        copy.start()
        copies.append(copy)
    for copy in copies:
        copy.wait()


def pool_slots(first, place_ref, weight_ref, piece_refs, table, picked, put):
    width, slots, lanes = picked.shape
    start = 0
    for piece_ref in piece_refs:
        count = piece_ref.shape[0]
        rows = 256

        def widen(step, carry, piece_ref=piece_ref, start=start):
            base = pl.multiple_of(step * rows, rows)
            table[pl.ds(start + base, rows), :] = piece_ref[pl.ds(base, rows), :].astype(jnp.float32)
            return carry

        lax.fori_loop(0, count // rows, widen, 0)
        start += count

    def some_slots(step, carry):
        base = pl.multiple_of(step * 8, 8)
        for k in range(width):
            picks = [place_ref[k, first + base + i] for i in range(8)]
            rows = [table[pl.ds(pick, 1), :] for pick in picks]
            for i in range(8):
                picked[k, pl.ds(base + i, 1), :] = rows[i]
        return carry

    lax.fori_loop(0, slots // 8, some_slots, 0)
    weights = jnp.transpose(weight_ref[:, first : first + slots])
    for t, (lower, upper) in enumerate(bag_bounds):
        total = picked[lower] * weights[:, lower : lower + 1]
        for k in range(lower + 1, upper):
            total = total + picked[k] * weights[:, k : k + 1]
        put(slice(t * lanes, (t + 1) * lanes), total.astype(jnp.bfloat16))


def pool_kernel(place_ref, weight_ref, *refs):
    out_ref, table, picked = refs[-3:]

    def put(columns, total):
        out_ref[:, columns] = total

    pool_slots(0, place_ref, weight_ref, refs[:-3], table, picked, put)


def stage_kernel(
    pieces, sources, place_ref, me_ref, weight_ref, carried_ref, gain_ref, pooled_ref, *refs
):
    piece_refs = refs[:pieces]
    filter_refs = refs[pieces : pieces + sources]
    out_ref, table, picked, filters, first_buf, second_buf, result = refs[pieces + sources :][:7]
    filter_sems, out_sems = refs[pieces + sources :][7:]
    slots = result.shape[0]
    layers = filters.shape[0]
    filter_copies = []
    if sources == 1:
        filter_copies.append(pltpu.make_async_copy(filter_refs[0], filters, filter_sems.at[0]))
    else:
        held, half, depth, _ = filter_refs[0].shape
        for group, filter_ref in enumerate(filter_refs):
            bits, side = block_place(group, me_ref[1])
            for number in range(filter_ref.shape[0]):
                owner = me_ref[0] ^ (4 * number + bits)
                rows = pl.ds(pl.multiple_of(owner * depth, depth), depth)
                filter_copies.append(
                    pltpu.make_async_copy(
                        filter_ref.at[number],
                        filters.at[pl.ds(side * half, half), rows, :],
                        filter_sems.at[len(filter_copies)],
                    )
                )
    for copy in filter_copies:
        copy.start()
    front = 16
    early = pooled_ref.shape[0]
    first_buf[front : front + early, :] = pooled_ref[...].astype(jnp.float32)

    def put(columns, total):
        first_buf[front + early :, columns] = total.astype(jnp.float32)

    pool_slots(early, place_ref, weight_ref, piece_refs, table, picked, put)
    for copy in filter_copies:
        copy.wait()
    offset = 0
    out_copies = []
    for layer in range(layers):
        dilation = 2**layer
        span = 2 * dilation
        source, target = (first_buf, second_buf) if layer % 2 == 0 else (second_buf, first_buf)
        source[front - span : front, :] = carried_ref[offset : offset + span, :]
        offset += span
        for begin in range(0, slots, 512):
            rows = min(512, slots - begin)
            base = front + begin
            taps = [
                source[base - tap * dilation : base - tap * dilation + rows, :].astype(jnp.bfloat16)
                for tap in range(3)
            ]
            output = jnp.dot(
                jnp.concatenate(taps, axis=1), filters[layer], preferred_element_type=jnp.float32
            )
            mean = jnp.mean(output, axis=-1, keepdims=True)
            centred = output - mean
            spread = jnp.mean(centred * centred, axis=-1, keepdims=True)
            active = jnp.maximum(
                centred * lax.rsqrt(spread + epsilon) * gain_ref[layer : layer + 1, :], 0.0
            )
            if layer % 2 == 1:
                active = active + target[base : base + rows, :]
            active = active.astype(jnp.bfloat16)
            if layer == layers - 1:
                result[begin : begin + rows, :] = active
                copy = pltpu.make_async_copy(
                    result.at[pl.ds(begin, rows), :],
                    out_ref.at[pl.ds(begin, rows), :],
                    out_sems.at[len(out_copies)],
                )
                copy.start()
                out_copies.append(copy)
            else:
                target[base : base + rows, :] = active.astype(jnp.float32)
    for copy in out_copies:
        copy.wait()


def swapped(array, axis, distance):
    pairs = [(source, source ^ distance) for source in range(lax.axis_size(axis))]
    return lax.ppermute(array, axis, pairs)


def block_place(number, side):
    kind = number % 4
    bits = (2 if kind in (1, 3) else 0) + number // 4
    return bits, side if kind < 2 else 1 - side


def ordered_filters(blocks, me):
    count = blocks[0].shape[0]
    owners = 4 * count
    half = blocks[0].shape[1]
    layers = 2 * half
    whole = jnp.zeros((owners, layers) + blocks[0].shape[2:], blocks[0].dtype)
    for number, block in enumerate(blocks):
        bits, side = block_place(number, me[1])
        for shard in range(block.shape[0]):
            owner = me[0] ^ (4 * shard + bits)
            whole = lax.dynamic_update_slice(whole, block[shard][None], (owner, side * half, 0, 0))
    return whole.transpose(1, 0, 2, 3).reshape(layers, -1, whole.shape[-1])


def carried_rows(returning, home, entry, stores):
    copies = lax.axis_size("rep")
    me = lax.axis_index("rep")
    by_position = stores.transpose(1, 0, 2)
    positions, _, channels = by_position.shape
    carried = jnp.zeros((positions, channels), stores.dtype)
    for shift in range(copies):
        arrived = by_position
        if shift:
            pairs = [(source, (source + shift) % copies) for source in range(copies)]
            arrived = lax.ppermute(by_position, "rep", pairs)
        wanted = (returning[0] > 0) & (home[0] == (me + copies - shift) % copies)
        chosen = lax.dynamic_index_in_dim(arrived, entry[0], 1, keepdims=False)
        carried = jnp.where(wanted, chosen, carried)
    return carried.astype(jnp.float32)


def local(
    bag_rows, bag_owner, bag_weight, tables, returning, home, entry, stores, conv_weight, norm_gain
):
    owners = lax.axis_size("table")
    samples_here, slot_count, bag_width = bag_rows.shape
    token_count = samples_here * slot_count
    shard_rows = tables.shape[1]
    row_width = tables.shape[2]
    channels = conv_weight.shape[-1]
    capacity = min(token_count, (3 * token_count * bag_width + 2 * owners - 1) // (2 * owners))
    cuts = [0] + [round(capacity * end) // 16 * 16 for end in part_ends]
    early = cuts[-2]
    late = token_count - early
    smem = pl.BlockSpec(memory_space=pltpu.SMEM)
    vmem = pl.BlockSpec(memory_space=pltpu.VMEM)
    anywhere = pl.BlockSpec(memory_space=pl.ANY)

    me = jnp.stack([lax.axis_index("table"), lax.axis_index("rep") % 2]).astype(jnp.int32)
    half = conv_weight.shape[0] // 2
    shard = lax.dynamic_slice_in_dim(conv_weight, me[1] * half, half, 0)
    middle = owners // 8
    line = [shard] + [swapped(shard, "table", 4 * step) for step in range(1, middle + 1)]
    state = carried_rows(returning, home, entry, stores)
    rows_by_slot = bag_rows.reshape(token_count, bag_width).T
    owner_by_slot = bag_owner.reshape(token_count, bag_width).T
    requests, place = pl.pallas_call(
        functools.partial(prep_kernel, cuts, shard_rows),
        out_shape=(
            jax.ShapeDtypeStruct((owners, 1, capacity), jnp.int32),
            jax.ShapeDtypeStruct((bag_width, token_count), jnp.int32),
        ),
        in_specs=[vmem, vmem],
        out_specs=(vmem, vmem),
        compiler_params=pltpu.CompilerParams(vmem_limit_bytes=8 * megabyte),
        name="prep",
    )(rows_by_slot, owner_by_slot)
    received = lax.all_to_all(requests, "table", split_axis=0, concat_axis=0, tiled=True)
    received = received.reshape(owners * capacity)
    flat_table = tables.reshape(-1, row_width)
    returned = []
    sent = []
    for number in range(len(part_ends)):
        piece = cuts[number + 1] - cuts[number]
        if number == 1:
            middle_shard = tie(line[middle], received)
            forwarded = [swapped(middle_shard, "table", 4 * step) for step in range(1, middle)]
            line = line[:middle] + [middle_shard] + forwarded
        earlier = sent[-1:] if sent else line[1:]
        sent.append(
            pl.pallas_call(
                functools.partial(gather_kernel, capacity, cuts[number]),
                out_shape=jax.ShapeDtypeStruct((owners, piece, row_width), jnp.bfloat16),
                in_specs=[anywhere] * (2 + len(earlier)),
                out_specs=anywhere,
                scratch_shapes=[
                    pltpu.VMEM(flat_table.shape, jnp.bfloat16),
                    pltpu.VMEM(flat_table.shape, jnp.float32),
                    pltpu.VMEM((piece, row_width), jnp.float32),
                    pltpu.VMEM((owners, piece, row_width), jnp.bfloat16),
                    pltpu.SMEM((owners * capacity,), jnp.int32),
                    pltpu.SemaphoreType.DMA,
                    pltpu.SemaphoreType.DMA((8,)),
                    pltpu.SemaphoreType.DMA((owners,)),
                ],
                compiler_params=pltpu.CompilerParams(vmem_limit_bytes=58 * megabyte),
                cost_estimate=pl.CostEstimate(
                    flops=0, bytes_accessed=20 * megabyte, transcendentals=0
                ),
                name="owner_gather",
            )(received, flat_table, *earlier)
        )
    line = jnp.stack(line)
    by_table = swapped(line, "table", 2)
    by_rep = swapped(line, "rep", 1)
    by_table = tie(by_table, state)
    corner = swapped(by_table, "rep", 1)
    gates = [[], [sent[2]] + forwarded, [state, by_table, by_rep]]
    for rows, gate in zip(sent, gates):
        if returned:
            rows = tie(rows, returned[-1][: 16 if len(returned) > 1 else None], *gate)
        arrived = lax.all_to_all(rows, "table", split_axis=0, concat_axis=0, tiled=True)
        returned.append(arrived.reshape(-1, row_width))
    weight_by_slot = bag_weight.reshape(token_count, bag_width).T
    pooled = pl.pallas_call(
        pool_kernel,
        out_shape=jax.ShapeDtypeStruct((early, channels), jnp.bfloat16),
        in_specs=[smem] + [vmem] * len(returned),
        out_specs=vmem,
        scratch_shapes=[
            pltpu.VMEM((owners * early, row_width), jnp.float32),
            pltpu.VMEM((bag_width, early, row_width), jnp.float32),
        ],
        compiler_params=pltpu.CompilerParams(vmem_limit_bytes=32 * megabyte),
        cost_estimate=pl.CostEstimate(
            flops=0, bytes_accessed=24 * megabyte, transcendentals=0
        ),
        name="pool",
    )(place, weight_by_slot, *returned[:-1])
    corner = tie(corner, pooled)
    filters = [line, by_table, by_rep, corner]
    filters = filters + [swapped(block, "table", 1) for block in filters]
    if conv_weight.shape[1] % 16:
        filters = [ordered_filters(filters, me)]

    hidden = pl.pallas_call(
        functools.partial(stage_kernel, len(returned), len(filters)),
        out_shape=jax.ShapeDtypeStruct((token_count, channels), jnp.bfloat16),
        in_specs=[smem] * 2 + [vmem] * (4 + len(returned)) + [anywhere] * len(filters),
        out_specs=anywhere,
        scratch_shapes=[
            pltpu.VMEM((owners * cuts[-1], row_width), jnp.float32),
            pltpu.VMEM((bag_width, late, row_width), jnp.float32),
            pltpu.VMEM((conv_weight.shape[0], 3 * channels, channels), jnp.bfloat16),
            pltpu.VMEM((token_count + 16, channels), jnp.float32),
            pltpu.VMEM((token_count + 16, channels), jnp.float32),
            pltpu.VMEM((token_count, channels), jnp.bfloat16),
            pltpu.SemaphoreType.DMA((2 * owners,)),
            pltpu.SemaphoreType.DMA(((token_count + 255) // 256,)),
        ],
        compiler_params=pltpu.CompilerParams(vmem_limit_bytes=56 * megabyte),
        cost_estimate=pl.CostEstimate(
            flops=2 * token_count * 3 * channels * channels * conv_weight.shape[0],
            bytes_accessed=24 * megabyte,
            transcendentals=0,
        ),
        name="stage",
    )(place, me, weight_by_slot, state, norm_gain, pooled, *returned, *filters)
    return hidden.reshape(samples_here, slot_count, channels)


def solution(mesh):
    in_specs = (
        P(("table", "rep"), None, None),
        P(("table", "rep"), None, None),
        P(("table", "rep"), None, None),
        P(None, "table", None),
        P(("table", "rep")),
        P(("table", "rep")),
        P(("table", "rep")),
        P(("table", "rep"), None, None),
        P(None, "table", None),
        P(),
    )
    out_specs = P(("table", "rep"), None, None)
    return jax.shard_map(local, mesh=mesh, in_specs=in_specs, out_specs=out_specs, check_vma=False)
```
